32 devices in a mesh: af: 4 (over z), row: 8 (over y, x, core).
Axes of the slice: x: 2, y: 2, z: 4, core: 2. Of those that a mesh axis runs over, the one named last changes fastest.
Arguments:
- image_in: bfloat16 [10, 2, 20, 256, 256], P(None, None, 'af', 'row'), may hold values from -6 to 6
- measured: float32 [10, 20, 256, 512], P(None, None, ('af', 'row')), may hold values from -6 to 6
- target: float32 [10, 20, 256, 512], P(None, None, ('af', 'row')), may hold values from -6 to 6
- line_mask: int32 [20, 256], P(None, ('af', 'row')), may hold values from 0 to 1, as said below
- window_half: int32 [20], replicated, may hold values from 0 to 2
- in_kernel: float32 [64, 54], replicated, may hold values from -0.875 to 0.875
- out_kernel: float32 [27, 2, 64], replicated, may hold values from -0.15625 to 0.15625
- biases: float32 [66], replicated, may hold values from -1 to 1
- in_moment: float32 [64, 54], replicated, may hold values from -0.00012207031 to 0.00012207031
- out_moment: float32 [27, 2, 64], replicated, may hold values from -0.00061035156 to 0.00061035156
- bias_moment: float32 [66], replicated, may hold values from -0.0004272461 to 0.0004272461
- in_square: float32 [64, 54], replicated, may hold values from 6.866455e-11 to 2.746582e-10
- out_square: float32 [27, 2, 64], replicated, may hold values from 1.7166137e-09 to 6.866455e-09
- bias_square: float32 [66], replicated, may hold values from 7.6293943e-10 to 3.0517577e-09
- in_smooth: float32 [64, 54], replicated, may hold values from -0.875 to 0.875
- out_smooth: float32 [27, 2, 64], replicated, may hold values from -0.15625 to 0.15625
- bias_smooth: float32 [66], replicated, may hold values from -1 to 1
Outputs:
- loss_total: float32 [], replicated
- unsampled_count: float32 [], replicated
- in_first: float32 [64, 54], replicated
- out_first: float32 [27, 2, 64], replicated
- bias_first: float32 [66], replicated
- in_second: float32 [64, 54], replicated
- out_second: float32 [27, 2, 64], replicated
- bias_second: float32 [66], replicated
- in_master: float32 [64, 54], replicated
- out_master: float32 [27, 2, 64], replicated
- bias_master: float32 [66], replicated
- in_average: float32 [64, 54], replicated
- out_average: float32 [27, 2, 64], replicated
- bias_average: float32 [66], replicated
- in_copy: bfloat16 [64, 54], replicated
- out_copy: bfloat16 [27, 2, 64], replicated
- bias_copy: bfloat16 [66], replicated
The draws below stay inside these ranges and needn't reach their ends.
Inputs may be any that keep to these rules, and one draw needn't show every extreme that they name: `line_mask`: 1 where line ky of frame t is sampled; line 256 - 1 is unsampled in every frame.
All inputs are finite; a program needn't handle non-finite values.
Results may differ from the reference program's by a relative error of at most 0.004.
The reference program's roundings to bfloat16 on the way count: a program that leaves them out, or rounds other values in their place, can miss the bound.
Values may be sent and summed in bfloat16 or wider, within the bound.
No kernel may reach another device: no remote copies, remote signals or barrier semaphores. Data moves between devices by JAX's collectives and lax.ppermute only.
A program may use at most 128 MiB of HBM per device.

```python
import math
import jax
import jax.numpy as jnp
from jax import lax

NX = 256
NY = 256
F = 20
CH = 64
STEP = 5
SLICES = 10
N_AF = 4


def draw_line_mask(key, part):
    key = jax.random.fold_in(key, 11)
    line = jnp.arange(NY, dtype=jnp.int32)
    block_size = NY // N_AF
    upper = line // block_size
    lower = line % block_size
    level = 150 + 350 * upper // max(N_AF - 1, 1) + 350 * lower // max(block_size - 1, 1)
    rolled = jax.random.randint(key, (F, NY), 0, 1000)
    sampled_mask = (rolled >= level[None, :]).astype(jnp.int32)
    return sampled_mask.at[:, NY - 1].set(0)


def plant(entries, own_key, smallest, largest):
    spot = [jax.random.randint(jax.random.fold_in(own_key, axis), (), 0, length) for axis, length in enumerate(entries.shape)]
    main_axis = entries.shape.index(max(entries.shape))
    neighbour = spot[:main_axis] + [(spot[main_axis] + 1) % entries.shape[main_axis]] + spot[main_axis + 1:]
    return entries.at[tuple(spot)].set(smallest).at[tuple(neighbour)].set(largest)


def shard_levels(stream_key, extent, cuts, smallest, largest):
    level = 1.0
    for dim, shards_of in cuts:
        draws = jax.random.uniform(jax.random.fold_in(jax.random.fold_in(stream_key, 6), dim), (shards_of,), jnp.float32, smallest / len(cuts), largest / len(cuts))
        level = level * jnp.repeat(jnp.exp(draws), extent[dim] // shards_of).reshape((-1,) + (1,) * (len(extent) - 1 - dim))
    return level


def noise(rng, extent, width, limit, split=(), kind=jnp.bfloat16):
    array = jax.random.normal(rng, extent, jnp.float32) * width
    if len(split) > 0:
        array = shard_levels(rng, extent, split, -0.22, 0.18) * array
    return jnp.clip(array, min=-limit, max=limit).astype(kind)


def setup_inputs(seed: int = 0) -> dict:
    key_list = jax.random.split(jax.random.key(seed), 18)
    return {
        "image_in": noise(key_list[0], (SLICES, 2, F, NX, NY), 1.0, 6.0, ((2, 4), (3, 8))),
        "measured": noise(key_list[1], (SLICES, F, NY, 2 * NX), 1.0, 6.0, ((2, 32),), jnp.float32),
        "target": noise(key_list[2], (SLICES, F, NY, 2 * NX), 1.0, 6.0, ((2, 32),), jnp.float32),
        "line_mask": draw_line_mask(jax.random.fold_in(key_list[17], 71), 0),
        "window_half": plant(jax.random.randint(key_list[4], (F,), 0, 3), jax.random.fold_in(key_list[4], 1), 0, 2).astype(jnp.int32),
        "in_kernel": noise(key_list[5], (CH, 54), 54 ** -0.5, 0.875, (), jnp.float32),
        "out_kernel": noise(key_list[6], (27, 2, CH), (27 * CH) ** -0.5, 0.15625, (), jnp.float32),
        "biases": noise(key_list[7], (CH + 2,), 0.2, 1.0, (), jnp.float32),
        "in_moment": noise(key_list[8], (CH, 54), (0.03 * (SLICES * F * NX * NY) ** -0.5), 0.00012207031, (), jnp.float32),
        "out_moment": noise(key_list[9], (27, 2, CH), (0.15 * (SLICES * F * NX * NY) ** -0.5), 0.00061035156, (), jnp.float32),
        "bias_moment": noise(key_list[10], (CH + 2,), (0.1 * (SLICES * F * NX * NY) ** -0.5), 0.0004272461, (), jnp.float32),
        "in_square": jnp.clip(jnp.exp(jax.random.uniform(key_list[11], (CH, 54), jnp.float32, math.log(6.866455320997389e-11), math.log(2.7465821283989555e-10))), 6.866455320997389e-11, 2.7465821283989555e-10),
        "out_square": jnp.clip(jnp.exp(jax.random.uniform(key_list[12], (27, 2, CH), jnp.float32, math.log(1.7166137400437265e-09), math.log(6.866454960174906e-09))), 1.7166137400437265e-09, 6.866454960174906e-09),
        "bias_square": jnp.clip(jnp.exp(jax.random.uniform(key_list[13], (CH + 2,), jnp.float32, math.log(7.629394338515283e-10), math.log(3.051757735406113e-09))), 7.629394338515283e-10, 3.051757735406113e-09),
        "in_smooth": noise(key_list[14], (CH, 54), 54 ** -0.5, 0.875, (), jnp.float32),
        "out_smooth": noise(key_list[15], (27, 2, CH), (27 * CH) ** -0.5, 0.15625, (), jnp.float32),
        "bias_smooth": noise(key_list[16], (CH + 2,), 0.2, 1.0, (), jnp.float32),
    }


beta_first = 0.5
beta_second = 0.5
rate_in = 0.2
rate_out = 0.04
rate_bias = 0.3
decay_weight = 0.01
average_keep = 0.9
epsilon = 1e-08

@jax.custom_vjp
def low(v):
    return lax.optimization_barrier(v.astype(jnp.bfloat16)).astype(jnp.float32)

@jax.custom_vjp
def low_back(v):
    return v

def low_keep(v):
    return (low(v), None)

def low_pass(kept, grad):
    return (grad,)

def back_keep(v):
    return (v, None)

def back_low(kept, grad):
    return (low(grad),)
low.defvjp(low_keep, low_pass)
low_back.defvjp(back_keep, back_low)

def dft_table(length):
    index = jnp.arange(length, dtype=jnp.int32)
    phase = (index[:, None] * index[None, :] % length).astype(jnp.float32) * (2.0 * math.pi / length)
    cosine = jnp.cos(phase) / math.sqrt(length)
    sine = jnp.sin(phase) / math.sqrt(length)
    upper = jnp.concatenate([cosine, -sine], axis=1)
    lower = jnp.concatenate([sine, cosine], axis=1)
    return jnp.concatenate([upper, lower], axis=0).astype(jnp.bfloat16)

def share_matrix(window_half, frames):
    index = jnp.arange(frames, dtype=jnp.int32)
    inside = (jnp.abs(index[None, :] - index[:, None]) <= window_half[:, None]).astype(jnp.float32)
    return inside / lax.optimization_barrier(jnp.sum(inside, axis=1, keepdims=True))

def convolve(volume, kernel):
    return lax.conv_general_dilated(volume, kernel, (1, 1, 1), ((1, 1), (1, 1), (1, 1)), dimension_numbers=('NCDHW', 'OIDHW', 'NCDHW'), precision=lax.Precision.HIGHEST)

def adam_step(master, grad, first, second, rate):
    first_new = beta_first * first + (1.0 - beta_first) * grad
    second_new = beta_second * second + (1.0 - beta_second) * grad * grad
    first_hat = first_new / (1.0 - beta_first ** STEP)
    second_hat = second_new / (1.0 - beta_second ** STEP)
    master_new = master - rate * (first_hat / (jnp.sqrt(second_hat) + epsilon) + decay_weight * master)
    return (first_new, second_new, master_new)

def reference(image_in, measured, target, line_mask, window_half, in_kernel, out_kernel, biases, in_moment, out_moment, bias_moment, in_square, out_square, bias_square, in_smooth, out_smooth, bias_smooth):
    highest = lax.Precision.HIGHEST
    table_y = dft_table(NY).astype(jnp.float32)
    table_x = dft_table(NX).astype(jnp.float32)
    share = share_matrix(window_half, F)
    sampled_mask = line_mask.astype(jnp.float32)[:, :, None]
    unsampled_mask = 1.0 - sampled_mask
    count = jnp.sum(unsampled_mask) * (2.0 * SLICES * NX)
    images = image_in.astype(jnp.float32)

    def slice_loss(weights, piece_list):
        kernel_in, kernel_out, bias_all = weights
        slice_input_image, slice_measured_kspace, slice_target_image = piece_list
        kernel_one = low(kernel_in).reshape(CH, 2, 3, 3, 3)
        kernel_two = low(kernel_out).reshape(3, 3, 3, 2, CH).transpose(3, 4, 0, 1, 2)
        preact = convolve(slice_input_image[None], kernel_one)[0] + bias_all[:CH, None, None, None]
        preact = low_back(preact)
        hidden = low(jax.nn.gelu(preact))
        branch = convolve(hidden[None], kernel_two)[0] + bias_all[CH:, None, None, None]
        image = slice_input_image + low_back(branch)
        rows_flat = low(image).transpose(1, 2, 0, 3).reshape(F, NX, 2 * NY)
        hybrid = low_back(low(jnp.dot(rows_flat, table_y, precision=highest)))
        spectrum = hybrid.reshape(F, NX, 2, NY).transpose(0, 3, 2, 1).reshape(F, NY, 2 * NX)
        kspace_data = jnp.dot(spectrum, table_x, precision=highest)
        filled_kspace = sampled_mask * slice_measured_kspace + unsampled_mask * kspace_data
        shared_kspace = jnp.einsum('ts,slk->tlk', share, filled_kspace, precision=highest)
        result_image = sampled_mask * slice_measured_kspace + unsampled_mask * shared_kspace
        differ = result_image - slice_target_image
        return jnp.sum(unsampled_mask * (jnp.sqrt(differ * differ + 1.0) - 1.0))
    checked = jax.checkpoint(slice_loss)

    def total_loss(weights):

        def accumulate(carry, piece_list):
            return (carry + checked(weights, piece_list), None)
        total = lax.scan(accumulate, jnp.zeros((), jnp.float32), (images, measured, target))[0]
        return (total / count, total)
    loss_value, backward, loss_total = jax.vjp(total_loss, (in_kernel, out_kernel, biases), has_aux=True)
    grad_in, grad_out, grad_bias = backward(jnp.ones((), jnp.float32))[0]
    in_first, in_second, in_master = adam_step(in_kernel, grad_in, in_moment, in_square, rate_in)
    out_first, out_second, out_master = adam_step(out_kernel, grad_out, out_moment, out_square, rate_out)
    bias_first, bias_second, bias_master = adam_step(biases, grad_bias, bias_moment, bias_square, rate_bias)
    in_average = average_keep * in_smooth + (1.0 - average_keep) * in_master
    out_average = average_keep * out_smooth + (1.0 - average_keep) * out_master
    bias_average = average_keep * bias_smooth + (1.0 - average_keep) * bias_master
    return (loss_total, count, in_first, out_first, bias_first, in_second, out_second, bias_second, in_master, out_master, bias_master, in_average, out_average, bias_average, in_master.astype(jnp.bfloat16), out_master.astype(jnp.bfloat16), bias_master.astype(jnp.bfloat16))
```

```python
import functools
import math

import jax
import jax.numpy as jnp
import numpy as np
from jax import lax
from jax.experimental import pallas as pl
from jax.experimental.pallas import tpu as pltpu
from jax.sharding import PartitionSpec as P

STEP = 5
AXES = ("af", "row")
BLOCK = 4
WIN = 8
SIDE = 16
DEPTH = 9 * SIDE
ONES_ROW = BLOCK + 2
VMEM = 60 * 2**20
GELU = math.sqrt(2.0 / math.pi)
CUBE = 0.044715

beta_first = 0.5
beta_second = 0.5
rate_in = 0.2
rate_out = 0.04
rate_bias = 0.3
decay_weight = 0.01
average_keep = 0.9
epsilon = 1e-08

NT = (((1,), (1,)), ((), ()))
TN = (((0,), (0,)), ((), ()))


def dft_table(length):
    index = np.arange(length)
    phase = (index[:, None] * index[None, :] % length) * (2.0 * math.pi / length)
    cosine = np.cos(phase) / math.sqrt(length)
    sine = np.sin(phase) / math.sqrt(length)
    upper = np.concatenate([cosine, -sine], axis=1)
    lower = np.concatenate([sine, cosine], axis=1)
    return np.concatenate([upper, lower], axis=0).astype(np.float32)


def share_matrix(window_half, frames):
    index = jnp.arange(frames, dtype=jnp.int32)
    inside = (jnp.abs(index[None, :] - index[:, None]) <= window_half[:, None]).astype(jnp.float32)
    return inside / jnp.sum(inside, axis=1, keepdims=True)


def adam_step(master, grad, first, second, rate):
    first_new = beta_first * first + (1.0 - beta_first) * grad
    second_new = beta_second * second + (1.0 - beta_second) * grad * grad
    first_hat = first_new / (1.0 - beta_first**STEP)
    second_hat = second_new / (1.0 - beta_second**STEP)
    master_new = master - rate * (
        first_hat / (jnp.sqrt(second_hat) + epsilon) + decay_weight * master
    )
    return (first_new, second_new, master_new)


def conv_in_weights(kernel, bias):
    width = kernel.shape[0]
    taps = kernel.astype(jnp.bfloat16).astype(jnp.float32).reshape(width, 2, 3, 3, 3)
    rows = []
    for j in range(BLOCK):
        row = jnp.pad(taps, ((0, 0), (0, 0), (0, 0), (j, WIN - 3 - j), (0, 0)))
        rows.append(row.transpose(0, 2, 4, 1, 3))
    spread = jnp.stack(rows)
    high = lax.reduce_precision(bias, 8, 7)
    rest = bias - high
    middle = lax.reduce_precision(rest, 8, 7)
    parts = jnp.stack([high, middle, rest - middle], axis=1)
    spread = spread.at[:, :, :, 0, 0, ONES_ROW].set(jnp.broadcast_to(parts, (BLOCK, width, 3)))
    return spread.reshape(BLOCK * width, DEPTH).astype(jnp.bfloat16)


def conv_out_weights(kernel):
    width = kernel.shape[2]
    taps = kernel.astype(jnp.bfloat16).reshape(3, 3, 3, 2, width)[:, ::-1]
    columns = []
    for j in range(BLOCK):
        column = jnp.pad(taps, ((0, 0), (j, WIN - 3 - j), (0, 0), (0, 0), (0, 0)))
        columns.append(column.transpose(0, 2, 3, 1, 4))
    return jnp.stack(columns, axis=4).reshape(DEPTH, BLOCK * width)


def conv_back_weights(kernel):
    width = kernel.shape[2]
    taps = kernel.astype(jnp.bfloat16).reshape(3, 3, 3, 2, width)[::-1, ::-1, ::-1]
    rows = []
    for j in range(BLOCK):
        row = jnp.pad(taps, ((0, 0), (j, WIN - 3 - j), (0, 0), (0, 0), (0, 0)))
        rows.append(row.transpose(4, 0, 2, 3, 1))
    return jnp.stack(rows).reshape(BLOCK * width, DEPTH)


def fold_in(total, width):
    spread = total.reshape(BLOCK, width, 3, 3, 2, WIN)
    taps = sum(spread[j][..., j : j + 3] for j in range(BLOCK))
    grad = taps.transpose(0, 3, 1, 4, 2).reshape(width, 54)
    return grad, jnp.sum(spread[:, :, 0, 0, 0, ONES_ROW], axis=0)


def fold_out(total, width):
    spread = total.reshape(BLOCK, width, 3, 3, 2, WIN)
    taps = sum(spread[j][..., j : j + 3] for j in range(BLOCK))
    return taps[:, ::-1, ::-1, :, ::-1].transpose(1, 4, 2, 3, 0).reshape(27, 2, width)


def load_volume(volume, own, edge_frames, edge_rows):
    _, channels, frames, rows, columns = own.shape
    lanes = (frames + 2) * columns
    for c in range(channels):
        volume[c, rows + 8 : rows + 16, :] = jnp.zeros((8, lanes), jnp.float32)
        for t in range(frames + 2):
            if t == 0:
                piece = edge_frames[0, 0, c]
            elif t == frames + 1:
                piece = edge_frames[0, 1, c]
            else:
                piece = own[0, c, t - 1]
            volume[c, 8 : 8 + rows, t * columns : (t + 1) * columns] = piece.astype(jnp.float32)
    outer = edge_rows[0].astype(jnp.float32)
    for c in range(channels):
        volume[c, 7:8, :] = outer[c : c + 1]
        volume[c, rows + 8 : rows + 9, :] = outer[2 + c : 3 + c]


def build_windows(volume, windows, columns, ones):
    blocks, _, lanes = windows.shape
    column = lax.broadcasted_iota(jnp.int32, (SIDE, columns), 1)
    row = lax.broadcasted_iota(jnp.int32, (SIDE, columns), 0)
    for block in range(blocks):
        for t in range(lanes // columns):
            here = slice(t * columns, (t + 1) * columns)
            start = 7 + BLOCK * block
            window = jnp.concatenate(
                [volume[c, start : start + WIN, here] for c in range(2)], axis=0
            )
            for e in range(3):
                shifted = window
                if e != 1:
                    shifted = pltpu.roll(window, (1 - e) % columns, axis=1)
                    shifted = jnp.where(column == (0 if e == 0 else columns - 1), 0.0, shifted)
                if ones and e == 0:
                    shifted = jnp.where(row == ONES_ROW, 1.0, shifted)
                windows[block, e * SIDE : (e + 1) * SIDE, here] = shifted.astype(jnp.bfloat16)


def forward_kernel(
    own, edge_frames, edge_rows, w_in, w_out, bias_out, main, part_frames, part_rows,
    volume, windows, total, hidden, mixed, spread,
):
    _, _, frames, rows, columns = own.shape
    blocks = windows.shape[0]
    load_volume(volume, own, edge_frames, edge_rows)
    build_windows(volume, windows, columns, True)
    column = lax.broadcasted_iota(jnp.int32, (SIDE, columns), 1)

    def step(block, carry):
        for f in range(frames):
            here = slice(f * columns, (f + 1) * columns)
            patch = jnp.concatenate(
                [windows[block, :, (f + a) * columns : (f + a + 1) * columns] for a in range(3)],
                axis=0,
            )
            x = jnp.dot(w_in[...], patch, preferred_element_type=jnp.float32)
            t = jnp.tanh(x * (GELU + (GELU * CUBE) * (x * x)))
            half = 0.5 * x
            hidden[:, here] = (half + half * t).astype(jnp.bfloat16)
            mixed[f] = jnp.dot(w_out[...], hidden[:, here], preferred_element_type=jnp.float32)
        for t in range(frames + 2):
            window = None
            for e in range(3):
                summed = None
                for a in range(3):
                    f = t - 2 + a
                    if 0 <= f < frames:
                        start = (a * 3 + e) * SIDE
                        piece = mixed[f, start : start + SIDE, :]
                        summed = piece if summed is None else summed + piece
                if e != 1:
                    summed = pltpu.roll(summed, (1 - e) % columns, axis=1)
                    summed = jnp.where(column == (0 if e == 0 else columns - 1), 0.0, summed)
                window = summed if window is None else window + summed
            spread[block, :, t * columns : (t + 1) * columns] = window
        return carry

    lax.fori_loop(0, blocks, step, 0)
    total[...] = jnp.zeros_like(total)
    for block in range(blocks):
        for o in range(2):
            start = 7 + BLOCK * block
            total[o, start : start + WIN, :] = (
                total[o, start : start + WIN, :] + spread[block, o * WIN : (o + 1) * WIN, :]
            )
    for o in range(2):
        for t in range(frames + 2):
            here = total[o, 8 : 8 + rows, t * columns : (t + 1) * columns]
            if t == 0:
                part_frames[0, 0, o] = here.astype(jnp.bfloat16)
            elif t == frames + 1:
                part_frames[0, 1, o] = here.astype(jnp.bfloat16)
            else:
                base = volume[o, 8 : 8 + rows, t * columns : (t + 1) * columns] + bias_out[o]
                main[0, t - 1, :, o * columns : (o + 1) * columns] = base + here
    part_rows[0] = jnp.concatenate(
        [total[o, at : at + 1, :] for at in (7, 8 + rows) for o in range(2)], axis=0
    ).astype(jnp.bfloat16)


def backward_kernel(
    own, edge_frames, edge_rows, grad, grad_frames, grad_rows, w_in, w_back, sum_in, sum_out,
    volume, windows, grad_windows, hidden, grads,
):
    _, _, frames, rows, columns = own.shape
    blocks = windows.shape[0]

    @pl.when(pl.program_id(0) == 0)
    def _():
        sum_in[...] = jnp.zeros_like(sum_in)
        sum_out[...] = jnp.zeros_like(sum_out)

    load_volume(volume, own, edge_frames, edge_rows)
    build_windows(volume, windows, columns, True)
    load_volume(volume, grad, grad_frames, grad_rows)
    build_windows(volume, grad_windows, columns, False)

    def step(block, carry):
        def patches(source):
            return jnp.concatenate(
                [source[block, :, a * columns : (a + frames) * columns] for a in range(3)], axis=0
            )

        patch = patches(windows)
        grad_patch = patches(grad_windows)
        for f in range(frames):
            here = slice(f * columns, (f + 1) * columns)
            x = jnp.dot(w_in[...], patch[:, here], preferred_element_type=jnp.float32)
            gh = jnp.dot(w_back[...], grad_patch[:, here], preferred_element_type=jnp.float32)
            u = x * x
            t = jnp.tanh(x * (GELU + (GELU * CUBE) * u))
            gate = 0.5 + 0.5 * t
            hidden[:, here] = (x * gate).astype(jnp.bfloat16)
            slope = x * (2.0 * GELU + (6.0 * GELU * CUBE) * u)
            grads[:, here] = (gate * (1.0 + slope * (1.0 - gate)) * gh).astype(jnp.bfloat16)
        sum_in[...] += lax.dot_general(grads[...], patch, NT, preferred_element_type=jnp.float32)
        sum_out[...] += lax.dot_general(
            hidden[...], grad_patch, NT, preferred_element_type=jnp.float32
        )
        return carry

    lax.fori_loop(0, blocks, step, 0)


def whole(shape):
    return pl.BlockSpec(tuple(shape), lambda s: (0,) * len(shape))


def a_slice(shape):
    return pl.BlockSpec((1,) + tuple(shape[1:]), lambda s: (s,) + (0,) * (len(shape) - 1))


def conv_scratch(frames, rows, columns):
    lanes = (frames + 2) * columns
    return (
        pltpu.VMEM((2, rows + 16, lanes), jnp.float32),
        pltpu.VMEM((rows // BLOCK, 3 * SIDE, lanes), jnp.bfloat16),
    )


def conv_forward(own, edge_frames, edge_rows, w_in, w_out, bias_out):
    slices, _, frames, rows, columns = own.shape
    lanes = (frames + 2) * columns
    span = w_in.shape[0]
    volume, windows = conv_scratch(frames, rows, columns)
    out_shape = [
        jax.ShapeDtypeStruct((slices, frames, rows, 2 * columns), jnp.float32),
        jax.ShapeDtypeStruct((slices, 2, 2, rows, columns), jnp.bfloat16),
        jax.ShapeDtypeStruct((slices, 4, lanes), jnp.bfloat16),
    ]
    return pl.pallas_call(
        forward_kernel,
        grid=(slices,),
        in_specs=[
            a_slice(own.shape),
            a_slice(edge_frames.shape),
            a_slice(edge_rows.shape),
            whole(w_in.shape),
            whole(w_out.shape),
            pl.BlockSpec(memory_space=pltpu.SMEM),
        ],
        out_specs=[a_slice(one.shape) for one in out_shape],
        out_shape=out_shape,
        scratch_shapes=[
            volume,
            windows,
            volume,
            pltpu.VMEM((span, frames * columns), jnp.bfloat16),
            pltpu.VMEM((frames, DEPTH, columns), jnp.float32),
            pltpu.VMEM((rows // BLOCK, SIDE, lanes), jnp.float32),
        ],
        compiler_params=pltpu.CompilerParams(vmem_limit_bytes=VMEM),
        name="conv_forward",
    )(own, edge_frames, edge_rows, w_in, w_out, bias_out)


def conv_backward(own, edge_frames, edge_rows, grad, grad_frames, grad_rows, w_in, w_back):
    slices, _, frames, rows, columns = own.shape
    span = w_in.shape[0]
    volume, windows = conv_scratch(frames, rows, columns)
    halves = pltpu.VMEM((span, frames * columns), jnp.bfloat16)
    total = jax.ShapeDtypeStruct((span, DEPTH), jnp.float32)
    arrays = (own, edge_frames, edge_rows, grad, grad_frames, grad_rows)
    return pl.pallas_call(
        backward_kernel,
        grid=(slices,),
        in_specs=[a_slice(one.shape) for one in arrays] + [whole(w_in.shape), whole(w_back.shape)],
        out_specs=[whole(total.shape)] * 2,
        out_shape=[total] * 2,
        scratch_shapes=[volume, windows, windows, halves, halves],
        compiler_params=pltpu.CompilerParams(vmem_limit_bytes=VMEM),
        name="conv_backward",
    )(*arrays, w_in, w_back)


def along(axis, step):
    count = lax.axis_size(axis)
    return [(i, i + step) for i in range(count) if 0 <= i + step < count]


def edges_of(volume):
    slices, _, frames, rows, columns = volume.shape
    below = lax.ppermute(volume[:, :, frames - 1], "af", along("af", 1))
    above = lax.ppermute(volume[:, :, 0], "af", along("af", -1))
    edge_frames = jnp.stack([below, above], axis=1)

    def flat(at):
        middle = volume[:, :, :, at].reshape(slices, 2, frames * columns)
        return jnp.concatenate([below[:, :, at], middle, above[:, :, at]], axis=2)

    left = lax.ppermute(flat(rows - 1), "row", along("row", 1))
    right = lax.ppermute(flat(0), "row", along("row", -1))
    return edge_frames, jnp.concatenate([left, right], axis=1)


def return_edges(part_frames, part_rows, columns):
    to_below = lax.ppermute(part_frames[:, 0], "af", along("af", -1))
    to_above = lax.ppermute(part_frames[:, 1], "af", along("af", 1))
    first = lax.ppermute(part_rows[:, :, :columns], "af", along("af", -1))
    last = lax.ppermute(part_rows[:, :, -columns:], "af", along("af", 1))
    frames = part_rows.shape[2] // columns - 2
    middle = part_rows[:, :, columns:-columns].astype(jnp.float32)
    wide = (frames - 1) * columns
    middle = middle + jnp.pad(first.astype(jnp.float32), ((0, 0), (0, 0), (wide, 0)))
    middle = middle + jnp.pad(last.astype(jnp.float32), ((0, 0), (0, 0), (0, wide)))
    middle = middle.astype(jnp.bfloat16)
    lower = lax.ppermute(middle[:, 0:2], "row", along("row", -1))
    upper = lax.ppermute(middle[:, 2:4], "row", along("row", 1))
    return jnp.stack([to_above, to_below], axis=1), jnp.concatenate([upper, lower], axis=1)


def image_kernel(main, add_frames, add_rows, table, out, image):
    slices, frames, rows, twice = main.shape
    columns = twice // 2
    row = lax.broadcasted_iota(jnp.int32, (rows, columns), 0)
    for s in range(slices):
        lines = add_rows[s].astype(jnp.float32)
        for f in range(frames):
            for o in range(2):
                here = slice(o * columns, (o + 1) * columns)
                value = main[s, f, :, here]
                if f == 0:
                    value = value + add_frames[s, 0, o].astype(jnp.float32)
                if f == frames - 1:
                    value = value + add_frames[s, 1, o].astype(jnp.float32)
                upper = lines[o : o + 1, f * columns : (f + 1) * columns]
                lower = lines[2 + o : 3 + o, f * columns : (f + 1) * columns]
                value = value + jnp.where(row == 0, upper, 0.0)
                value = value + jnp.where(row == rows - 1, lower, 0.0)
                start = (s * frames + f) * rows
                image[start : start + rows, here] = value.astype(jnp.bfloat16)
    size = slices * frames * rows
    for start in range(0, size, 512):
        stop = min(start + 512, size)
        out[:, start:stop] = lax.dot_general(
            table[...], image[start:stop, :], NT, preferred_element_type=jnp.float32
        ).astype(jnp.bfloat16)
    out[:, size:] = jnp.zeros((out.shape[0], out.shape[1] - size), jnp.bfloat16)


def image_to_hybrid(main, add_frames, add_rows, table):
    slices, frames, rows, twice = main.shape
    size = slices * frames * rows
    return pl.pallas_call(
        image_kernel,
        out_shape=jax.ShapeDtypeStruct((twice, -(-size // 128) * 128), jnp.bfloat16),
        scratch_shapes=[pltpu.VMEM((size, twice), jnp.bfloat16)],
        compiler_params=pltpu.CompilerParams(vmem_limit_bytes=VMEM),
        name="image_to_hybrid",
    )(main, add_frames, add_rows, table)


def grad_image_kernel(hybrid, table, out, sums):
    slices, _, frames, rows, columns = out.shape
    sums[...] = jnp.zeros_like(sums)
    for s in range(slices):
        size = frames * rows
        low = s * size // 128 * 128
        high = -(-(s + 1) * size // 128) * 128
        value = lax.dot_general(
            hybrid[:, low:high], table[...], TN, preferred_element_type=jnp.float32
        ).astype(jnp.bfloat16)
        for f in range(frames):
            start = s * size + f * rows - low
            for c in range(2):
                piece = value[start : start + rows, c * columns : (c + 1) * columns]
                out[s, c, f] = piece
                sums[c : c + 1, :] += jnp.sum(piece.astype(jnp.float32), axis=0, keepdims=True)


def hybrid_to_grad(hybrid, table, shape):
    return pl.pallas_call(
        grad_image_kernel,
        out_shape=[
            jax.ShapeDtypeStruct(shape, jnp.bfloat16),
            jax.ShapeDtypeStruct((2, shape[4]), jnp.float32),
        ],
        compiler_params=pltpu.CompilerParams(vmem_limit_bytes=VMEM),
        name="hybrid_to_grad",
    )(hybrid, table)


def chunk_transpose(pieces, low_half, even):
    a, c, b, d = pieces
    a, b = (
        jnp.where(low_half, a, pltpu.roll(b, 64, axis=1)),
        jnp.where(low_half, pltpu.roll(a, 64, axis=1), b),
    )
    c, d = (
        jnp.where(low_half, c, pltpu.roll(d, 64, axis=1)),
        jnp.where(low_half, pltpu.roll(c, 64, axis=1), d),
    )
    return (
        jnp.where(even, a, pltpu.roll(c, 32, axis=1)),
        jnp.where(even, pltpu.roll(a, 96, axis=1), c),
        jnp.where(even, b, pltpu.roll(d, 32, axis=1)),
        jnp.where(even, pltpu.roll(b, 96, axis=1), d),
    )


def kspace_kernel(
    frames_here, received, measured, target, sampled, share, scale, table, out, loss,
    spectrum, grads, loss_lanes,
):
    groups, _, lanes = received.shape
    pairs, n_af, _, twice = spectrum.shape
    rows = twice // 2
    n_row = groups // n_af
    frames = n_af * frames_here
    step = pl.program_id(0)
    lane = lax.broadcasted_iota(jnp.int32, (8, 128), 1)
    low_half = lane < 64
    even = lane % 64 < 32

    @pl.when(step == 0)
    def _():
        loss_lanes[...] = jnp.zeros_like(loss_lanes)

        def gather(af, carry):
            for tile in range(lanes // 128):
                for h in range(n_row // 4):
                    source = [
                        received[af * n_row + h * 4 + m, :, tile * 128 : (tile + 1) * 128].astype(
                            jnp.float32
                        )
                        for m in range(4)
                    ]
                    for c in range(2):
                        moved = chunk_transpose(
                            [one[c * 8 : (c + 1) * 8] for one in source], low_half, even
                        )
                        at = c * rows + h * 128
                        for k in range(4):
                            if tile * 4 + k < pairs:
                                spectrum[tile * 4 + k, af, :, at : at + 128] = moved[k]
            return carry

        lax.fori_loop(0, n_af, gather, 0)

    first = step * frames_here
    size = frames * 8
    here = spectrum[pl.ds(first, frames_here)].reshape(size, twice).astype(jnp.bfloat16)
    kspace = jnp.dot(here, table[...], preferred_element_type=jnp.float32)

    def place(t):
        return (t % frames_here) * n_af + t // frames_here

    filled = []
    for t in range(frames):
        mask = sampled[t]
        filled.append(mask * measured[0, t] + (1.0 - mask) * kspace[place(t) * 8 : place(t) * 8 + 8])
    slopes = []
    for t in range(frames):
        mask = sampled[t]
        near = range(max(t - 2, 0), min(t + 3, frames))
        shared = sum(share[t, s] * filled[s] for s in near)
        differ = mask * measured[0, t] + (1.0 - mask) * shared - target[0, t]
        square = differ * differ + 1.0
        inverse = lax.rsqrt(square)
        loss_lanes[...] += (1.0 - mask) * (square * inverse - 1.0)
        slopes.append((1.0 - mask) * differ * inverse * scale[0, 0])
    for s in range(frames):
        near = range(max(s - 2, 0), min(s + 3, frames))
        grad = sum(share[t, s] * slopes[t] for t in near)
        grads[place(s) * 8 : place(s) * 8 + 8, :] = (1.0 - sampled[s]) * grad
    grad = grads[...]
    high = grad.astype(jnp.bfloat16)
    low = (grad - high.astype(jnp.float32)).astype(jnp.bfloat16)
    back = lax.dot_general(high, table[...], NT, preferred_element_type=jnp.float32)
    back += lax.dot_general(low, table[...], NT, preferred_element_type=jnp.float32)
    spectrum[pl.ds(first, frames_here)] = back.reshape(frames_here, n_af, 8, twice)

    @pl.when(step == pl.num_programs(0) - 1)
    def _():
        loss[...] = loss_lanes[...]

        def scatter(af, carry):
            for tile in range(lanes // 128):
                for h in range(n_row // 4):
                    moved = []
                    for c in range(2):
                        at = c * rows + h * 128
                        moved.append(
                            chunk_transpose(
                                [
                                    spectrum[min(tile * 4 + k, pairs - 1), af, :, at : at + 128]
                                    for k in range(4)
                                ],
                                low_half,
                                even,
                            )
                        )
                    for m in range(4):
                        both = jnp.concatenate([moved[0][m], moved[1][m]], axis=0)
                        out[af * n_row + h * 4 + m, :, tile * 128 : (tile + 1) * 128] = both.astype(
                            jnp.bfloat16
                        )
            return carry

        lax.fori_loop(0, n_af, scatter, 0)


def kspace_step(received, measured, target, sampled, share, scale, table, frames_here):
    slices, frames, lines, twice = measured.shape
    n_af = frames // frames_here
    smem = pl.BlockSpec(memory_space=pltpu.SMEM)
    return pl.pallas_call(
        functools.partial(kspace_kernel, frames_here),
        grid=(slices,),
        in_specs=[
            whole(received.shape),
            a_slice(measured.shape),
            a_slice(target.shape),
            whole(sampled.shape),
            smem,
            smem,
            whole(table.shape),
        ],
        out_specs=[whole(received.shape), whole((lines, twice))],
        out_shape=[
            jax.ShapeDtypeStruct(received.shape, jnp.bfloat16),
            jax.ShapeDtypeStruct((lines, twice), jnp.float32),
        ],
        scratch_shapes=[
            pltpu.VMEM((slices * frames_here, n_af, lines, twice), jnp.float32),
            pltpu.VMEM((frames * lines, twice), jnp.float32),
            pltpu.VMEM((lines, twice), jnp.float32),
        ],
        compiler_params=pltpu.CompilerParams(vmem_limit_bytes=VMEM),
        name="kspace",
    )(received, measured, target, sampled, share, scale, table)


def middle_fast(
    main, add_frames, add_rows, measured, target, sampled, share, scale, table_y, table_x, volume
):
    groups = lax.axis_size("af") * lax.axis_size("row")
    slices, frames_here, rows, twice = main.shape
    lines = measured.shape[2]
    order = np.arange(twice).reshape(2, groups, lines).transpose(1, 0, 2).reshape(-1)
    permuted = jnp.asarray(np.ascontiguousarray(table_y[:, order].T), jnp.bfloat16)
    hybrid = image_to_hybrid(main, add_frames, add_rows, permuted)
    lanes = hybrid.shape[1]
    sent = hybrid.reshape(groups, 2 * lines, lanes)
    received = lax.all_to_all(sent, AXES, 0, 0, tiled=True)
    mask = jnp.broadcast_to(sampled[:, :, None], sampled.shape + (measured.shape[3],))
    back, loss = kspace_step(
        received,
        measured,
        target,
        mask,
        share,
        scale.reshape(1, 1),
        jnp.asarray(table_x, jnp.bfloat16),
        frames_here,
    )
    returned = lax.all_to_all(back, AXES, 0, 0, tiled=True).reshape(twice, lanes)
    grad, sums = hybrid_to_grad(returned, permuted, volume.shape)
    return jnp.sum(loss), grad, jnp.sum(sums, axis=1)


def middle_plain(
    main, add_frames, add_rows, measured, target, sampled, share, scale, table_y, table_x, volume
):
    highest = lax.Precision.HIGHEST
    slices, frames_here, rows_here, twice = main.shape
    columns = twice // 2
    frames, lines = measured.shape[1:3]
    rows = measured.shape[3] // 2
    table_y = jnp.asarray(table_y, jnp.bfloat16)
    table_x = jnp.asarray(table_x, jnp.bfloat16)
    image = main.reshape(slices, frames_here, rows_here, 2, columns)
    edge = jnp.transpose(add_frames.astype(jnp.float32), (1, 0, 3, 2, 4))
    image = image.at[:, 0].add(edge[0]).at[:, frames_here - 1].add(edge[1])
    line = add_rows.astype(jnp.float32).reshape(slices, 2, 2, frames_here, columns)
    line = jnp.transpose(line, (1, 0, 3, 2, 4))
    image = image.at[:, :, 0].add(line[0]).at[:, :, rows_here - 1].add(line[1])
    flat = image.reshape(slices, frames_here, rows_here, twice).astype(jnp.bfloat16)
    hybrid = jnp.dot(flat, table_y, preferred_element_type=jnp.float32).astype(jnp.bfloat16)
    hybrid = hybrid.reshape(slices, frames_here, rows_here, 2, columns)
    part = lax.all_to_all(hybrid, "af", split_axis=4, concat_axis=1, tiled=True)
    spread = lax.all_to_all(part, "row", split_axis=4, concat_axis=2, tiled=True)
    spectrum = jnp.transpose(spread, (0, 1, 4, 3, 2)).reshape(slices, frames, lines, 2 * rows)
    kspace = jnp.dot(spectrum, table_x, preferred_element_type=jnp.float32)
    mask = sampled[None, :, :, None]
    filled = mask * measured + (1.0 - mask) * kspace
    shared = jnp.einsum("ts,bslk->btlk", share, filled, precision=highest)
    differ = mask * measured + (1.0 - mask) * shared - target
    root = jnp.sqrt(differ * differ + 1.0)
    loss = jnp.sum((1.0 - mask) * (root - 1.0))
    slope = (1.0 - mask) * differ / root * scale
    grad = (1.0 - mask) * jnp.einsum("ts,btlk->bslk", share, slope, precision=highest)
    back = jnp.dot(grad, table_x.T.astype(jnp.float32), precision=highest).astype(jnp.bfloat16)
    back = jnp.transpose(back.reshape(slices, frames, lines, 2, rows), (0, 1, 4, 3, 2))
    part = lax.all_to_all(back, "row", split_axis=2, concat_axis=4, tiled=True)
    whole_rows = lax.all_to_all(part, "af", split_axis=1, concat_axis=4, tiled=True)
    grad = jnp.dot(
        whole_rows.reshape(slices, frames_here, rows_here, twice),
        table_y.T,
        preferred_element_type=jnp.float32,
    ).reshape(slices, frames_here, rows_here, 2, columns)
    grad = jnp.transpose(grad, (0, 3, 1, 2, 4)).astype(jnp.bfloat16)
    return loss, grad, jnp.sum(grad.astype(jnp.float32), axis=(0, 2, 3, 4))


def on_device(
    image_in, measured, target, line_mask, window_half, in_kernel, out_kernel, biases,
    in_moment, out_moment, bias_moment, in_square, out_square, bias_square,
    in_smooth, out_smooth, bias_smooth,
):
    slices, _, frames_here, rows_here, columns = image_in.shape
    frames, lines = measured.shape[1:3]
    width = in_kernel.shape[0]
    rows = rows_here * lax.axis_size("row")
    table_y = dft_table(columns)
    table_x = dft_table(rows)
    share = share_matrix(window_half, frames)
    sampled = line_mask.astype(jnp.float32)
    count = lax.psum(jnp.sum(1.0 - sampled) * (2.0 * slices * rows), AXES)
    w_in = conv_in_weights(in_kernel, biases[:width])
    w_out = conv_out_weights(out_kernel)
    w_back = conv_back_weights(out_kernel)

    edge_frames, edge_rows = edges_of(image_in)
    main, part_frames, part_rows = conv_forward(
        image_in, edge_frames, edge_rows, w_in, w_out, biases[width:]
    )
    add_frames, add_rows = return_edges(part_frames, part_rows, columns)
    fits = rows_here == 32 and lines == 8 and lax.axis_size("row") % 4 == 0
    middle = middle_fast if fits else middle_plain
    loss_part, grad_branch, sums = middle(
        main, add_frames, add_rows, measured, target, sampled, share, 1.0 / count,
        table_y, table_x, image_in,
    )
    grad_frames, grad_rows = edges_of(grad_branch)
    sum_in, sum_out = conv_backward(
        image_in, edge_frames, edge_rows, grad_branch, grad_frames, grad_rows, w_in, w_back
    )
    grad_in, bias_in = fold_in(sum_in, width)
    grad_out = fold_out(sum_out, width)
    grad_bias = jnp.concatenate([bias_in, sums])
    grad_in, grad_out, grad_bias, loss_total = lax.psum(
        (grad_in, grad_out, grad_bias, loss_part), AXES
    )
    in_first, in_second, in_master = adam_step(in_kernel, grad_in, in_moment, in_square, rate_in)
    out_first, out_second, out_master = adam_step(
        out_kernel, grad_out, out_moment, out_square, rate_out
    )
    bias_first, bias_second, bias_master = adam_step(
        biases, grad_bias, bias_moment, bias_square, rate_bias
    )
    in_average = average_keep * in_smooth + (1.0 - average_keep) * in_master
    out_average = average_keep * out_smooth + (1.0 - average_keep) * out_master
    bias_average = average_keep * bias_smooth + (1.0 - average_keep) * bias_master
    return (
        loss_total, count,
        in_first, out_first, bias_first,
        in_second, out_second, bias_second,
        in_master, out_master, bias_master,
        in_average, out_average, bias_average,
        in_master.astype(jnp.bfloat16), out_master.astype(jnp.bfloat16), bias_master.astype(jnp.bfloat16),
    )


def solution(mesh):
    in_specs = (
        P(None, None, "af", "row", None),
        P(None, None, ("af", "row"), None),
        P(None, None, ("af", "row"), None),
        P(None, ("af", "row")),
    ) + (P(),) * 13
    return jax.shard_map(
        on_device, mesh=mesh, in_specs=in_specs, out_specs=(P(),) * 17, check_vma=False
    )
```

```python
import functools
import math

import jax
import jax.numpy as jnp
import numpy as np
from jax import lax
from jax.experimental import pallas as pl
from jax.experimental.pallas import tpu as pltpu
from jax.sharding import PartitionSpec as P

STEP = 5
AXES = ("af", "row")
BLOCK = 4
WIN = 8
SIDE = 16
DEPTH = 9 * SIDE
ONES_ROW = BLOCK + 2
PACKED = 128
BIAS_LANE = WIN - 1
VMEM = 60 * 2**20
GELU = math.sqrt(2.0 / math.pi)
CUBE = 0.044715

beta_first = 0.5
beta_second = 0.5
rate_in = 0.2
rate_out = 0.04
rate_bias = 0.3
decay_weight = 0.01
average_keep = 0.9
epsilon = 1e-08

NT = (((1,), (1,)), ((), ()))
TN = (((0,), (0,)), ((), ()))


def dft_table(length):
    index = np.arange(length)
    phase = (index[:, None] * index[None, :] % length) * (2.0 * math.pi / length)
    cosine = np.cos(phase) / math.sqrt(length)
    sine = np.sin(phase) / math.sqrt(length)
    upper = np.concatenate([cosine, -sine], axis=1)
    lower = np.concatenate([sine, cosine], axis=1)
    return np.concatenate([upper, lower], axis=0).astype(np.float32)


def share_matrix(window_half, frames):
    index = jnp.arange(frames, dtype=jnp.int32)
    inside = (jnp.abs(index[None, :] - index[:, None]) <= window_half[:, None]).astype(jnp.float32)
    return inside / jnp.sum(inside, axis=1, keepdims=True)


def adam_step(master, grad, first, second, rate):
    first_new = beta_first * first + (1.0 - beta_first) * grad
    second_new = beta_second * second + (1.0 - beta_second) * grad * grad
    first_hat = first_new / (1.0 - beta_first**STEP)
    second_hat = second_new / (1.0 - beta_second**STEP)
    master_new = master - rate * (
        first_hat / (jnp.sqrt(second_hat) + epsilon) + decay_weight * master
    )
    return (first_new, second_new, master_new)


def conv_in_weights(kernel, bias):
    width = kernel.shape[0]
    taps = kernel.astype(jnp.bfloat16).astype(jnp.float32).reshape(width, 2, 3, 3, 3)
    rows = []
    for j in range(BLOCK):
        row = jnp.pad(taps, ((0, 0), (0, 0), (0, 0), (j, WIN - 3 - j), (0, 0)))
        rows.append(row.transpose(0, 2, 4, 1, 3))
    spread = jnp.stack(rows)
    high = lax.reduce_precision(bias, 8, 7)
    rest = bias - high
    middle = lax.reduce_precision(rest, 8, 7)
    parts = jnp.stack([high, middle, rest - middle], axis=1)
    spread = spread.at[:, :, :, 0, 0, ONES_ROW].set(jnp.broadcast_to(parts, (BLOCK, width, 3)))
    return spread.reshape(BLOCK * width, DEPTH).astype(jnp.bfloat16)


def conv_out_weights(kernel):
    width = kernel.shape[2]
    taps = kernel.astype(jnp.bfloat16).reshape(3, 3, 3, 2, width)[:, ::-1]
    columns = []
    for j in range(BLOCK):
        column = jnp.pad(taps, ((0, 0), (j, WIN - 3 - j), (0, 0), (0, 0), (0, 0)))
        columns.append(column.transpose(0, 2, 3, 1, 4))
    return jnp.stack(columns, axis=4).reshape(DEPTH, BLOCK * width)


def conv_back_weights(kernel):
    width = kernel.shape[2]
    taps = kernel.astype(jnp.bfloat16).reshape(3, 3, 3, 2, width)[::-1, ::-1, ::-1]
    rows = []
    for j in range(BLOCK):
        row = jnp.pad(taps, ((0, 0), (j, WIN - 3 - j), (0, 0), (0, 0), (0, 0)))
        rows.append(row.transpose(4, 0, 2, 3, 1))
    return jnp.stack(rows).reshape(BLOCK * width, DEPTH)


def pick_table():
    table = np.zeros((2, 256, PACKED), np.float32)
    for a, b, e, c in np.ndindex(3, 3, 3, 2):
        lane = ((a * 3 + e) * 2 + c) * WIN + b
        table[0, lane, 27 * c + 9 * a + 3 * b + e] = 1.0
        tap = 9 * (2 - a) + 3 * (2 - b) + 2 - e
        table[1, lane, PACKED // 2 + 2 * tap + c] = 1.0
    table[0, BIAS_LANE, 54] = 1.0
    return jnp.asarray(table, jnp.bfloat16)


def load_volume(volume, own, below, above, left, right):
    _, channels, frames, rows, columns = own.shape
    lanes = (frames + 2) * columns
    for c in range(channels):
        volume[c, rows + 8 : rows + 16, :] = jnp.zeros((8, lanes), jnp.float32)
        for t in range(frames + 2):
            if t == 0:
                piece = below[0, c]
            elif t == frames + 1:
                piece = above[0, c]
            else:
                piece = own[0, c, t - 1]
            volume[c, 8 : 8 + rows, t * columns : (t + 1) * columns] = piece.astype(jnp.float32)
    first = left[0].astype(jnp.float32)
    last = right[0].astype(jnp.float32)
    for c in range(channels):
        volume[c, 7:8, :] = first[c : c + 1]
        volume[c, rows + 8 : rows + 9, :] = last[c : c + 1]


def build_windows(volume, windows, columns, ones):
    blocks, _, lanes = windows.shape
    column = lax.broadcasted_iota(jnp.int32, (SIDE, columns), 1)
    row = lax.broadcasted_iota(jnp.int32, (SIDE, columns), 0)
    for block in range(blocks):
        for t in range(lanes // columns):
            here = slice(t * columns, (t + 1) * columns)
            start = 7 + BLOCK * block
            window = jnp.concatenate(
                [volume[c, start : start + WIN, here] for c in range(2)], axis=0
            )
            for e in range(3):
                shifted = window
                if e != 1:
                    shifted = pltpu.roll(window, (1 - e) % columns, axis=1)
                    shifted = jnp.where(column == (0 if e == 0 else columns - 1), 0.0, shifted)
                if ones and e == 0:
                    shifted = jnp.where(row == ONES_ROW, 1.0, shifted)
                windows[block, e * SIDE : (e + 1) * SIDE, here] = shifted.astype(jnp.bfloat16)


def forward_kernel(
    own, below, above, left, right, w_in, w_out, bias_out,
    main, part_below, part_above, part_left, part_right,
    volume, windows, total, hidden, mixed, spread,
):
    _, _, frames, rows, columns = own.shape
    blocks = windows.shape[0]
    load_volume(volume, own, below, above, left, right)
    build_windows(volume, windows, columns, True)
    column = lax.broadcasted_iota(jnp.int32, (SIDE, columns), 1)

    def step(block, carry):
        for f in range(frames):
            here = slice(f * columns, (f + 1) * columns)
            patch = jnp.concatenate(
                [windows[block, :, (f + a) * columns : (f + a + 1) * columns] for a in range(3)],
                axis=0,
            )
            x = jnp.dot(w_in[...], patch, preferred_element_type=jnp.float32)
            t = jnp.tanh(x * (GELU + (GELU * CUBE) * (x * x)))
            half = 0.5 * x
            hidden[:, here] = (half + half * t).astype(jnp.bfloat16)
            mixed[f] = jnp.dot(w_out[...], hidden[:, here], preferred_element_type=jnp.float32)
        for t in range(frames + 2):
            window = None
            for e in range(3):
                summed = None
                for a in range(3):
                    f = t - 2 + a
                    if 0 <= f < frames:
                        start = (a * 3 + e) * SIDE
                        piece = mixed[f, start : start + SIDE, :]
                        summed = piece if summed is None else summed + piece
                if e != 1:
                    summed = pltpu.roll(summed, (1 - e) % columns, axis=1)
                    summed = jnp.where(column == (0 if e == 0 else columns - 1), 0.0, summed)
                window = summed if window is None else window + summed
            spread[block, :, t * columns : (t + 1) * columns] = window
        return carry

    lax.fori_loop(0, blocks, step, 0, unroll=True)
    total[...] = jnp.zeros_like(total)
    for block in range(blocks):
        for o in range(2):
            start = 7 + BLOCK * block
            total[o, start : start + WIN, :] = (
                total[o, start : start + WIN, :] + spread[block, o * WIN : (o + 1) * WIN, :]
            )
    for o in range(2):
        for t in range(frames + 2):
            here = total[o, 8 : 8 + rows, t * columns : (t + 1) * columns]
            if t == 0:
                part_below[0, o] = here.astype(jnp.bfloat16)
            elif t == frames + 1:
                part_above[0, o] = here.astype(jnp.bfloat16)
            else:
                base = volume[o, 8 : 8 + rows, t * columns : (t + 1) * columns] + bias_out[o]
                main[0, t - 1, :, o * columns : (o + 1) * columns] = base + here
    for at, out in ((7, part_left), (8 + rows, part_right)):
        both = [total[o, at : at + 1, :] for o in range(2)]
        out[0] = jnp.concatenate(both, axis=0).astype(jnp.bfloat16)


def patches(source, block, frames, columns):
    return jnp.concatenate(
        [source[block, :, a * columns : (a + frames) * columns] for a in range(3)], axis=0
    )


def hidden_kernel(
    own, below, above, left, right, w_in, hidden, slopes, volume, windows
):
    _, _, frames, rows, columns = own.shape
    load_volume(volume, own, below, above, left, right)
    build_windows(volume, windows, columns, True)

    def step(block, carry):
        patch = patches(windows, block, frames, columns)
        for f in range(frames):
            here = slice(f * columns, (f + 1) * columns)
            x = jnp.dot(w_in[...], patch[:, here], preferred_element_type=jnp.float32)
            u = x * x
            t = jnp.tanh(x * (GELU + (GELU * CUBE) * u))
            gate = 0.5 + 0.5 * t
            hidden[0, block, :, here] = (x * gate).astype(jnp.bfloat16)
            slope = x * (2.0 * GELU + (6.0 * GELU * CUBE) * u)
            slopes[0, block, :, here] = (gate + gate * slope * (1.0 - gate)).astype(jnp.bfloat16)
        return carry

    lax.fori_loop(0, windows.shape[0], step, 0, unroll=True)


def backward_kernel(
    own, below, above, left, right, grad, grad_below, grad_above, grad_left, grad_right,
    hidden, slopes, w_back, pick, extras, out,
    volume, windows, grad_windows, grads, sum_in, sum_out,
):
    _, _, frames, rows, columns = own.shape

    @pl.when(pl.program_id(0) == 0)
    def _():
        sum_in[...] = jnp.zeros_like(sum_in)
        sum_out[...] = jnp.zeros_like(sum_out)

    load_volume(volume, own, below, above, left, right)
    build_windows(volume, windows, columns, True)
    load_volume(volume, grad, grad_below, grad_above, grad_left, grad_right)
    build_windows(volume, grad_windows, columns, False)

    def step(block, carry):
        patch = patches(windows, block, frames, columns)
        grad_patch = patches(grad_windows, block, frames, columns)
        for f in range(frames):
            here = slice(f * columns, (f + 1) * columns)
            gh = jnp.dot(w_back[...], grad_patch[:, here], preferred_element_type=jnp.float32)
            grads[:, here] = (slopes[0, block, :, here].astype(jnp.float32) * gh).astype(
                jnp.bfloat16
            )
        sum_in[:, :DEPTH] += lax.dot_general(
            grads[...], patch, NT, preferred_element_type=jnp.float32
        )
        sum_out[:, :DEPTH] += lax.dot_general(
            hidden[0, block], grad_patch, NT, preferred_element_type=jnp.float32
        )
        return carry

    lax.fori_loop(0, windows.shape[0], step, 0, unroll=True)

    @pl.when(pl.program_id(0) == pl.num_programs(0) - 1)
    def _():
        width = sum_in.shape[0] // BLOCK
        lanes = sum_in.shape[1]
        lane = lax.broadcasted_iota(jnp.int32, (width, lanes), 1)
        picked = jnp.zeros((width, pick.shape[2]), jnp.float32)
        for index, source in enumerate((sum_in, sum_out)):
            folded = source[0:width, :]
            bias = folded
            for j in range(1, BLOCK):
                part = source[j * width : (j + 1) * width, :]
                folded = folded + pltpu.roll(part, lanes - j, axis=1)
                bias = bias + part
            if index == 0:
                moved = pltpu.roll(bias, BIAS_LANE - ONES_ROW, axis=1)
                folded = jnp.where(lane == BIAS_LANE, moved, folded)
            for _ in range(3):
                part = folded.astype(jnp.bfloat16)
                folded = folded - part.astype(jnp.float32)
                picked = picked + jnp.dot(part, pick[index], preferred_element_type=jnp.float32)
        out[0:width, :] = picked + extras[0:width, :]
        out[width:, :] = extras[width:, :]


def whole(shape):
    return pl.BlockSpec(tuple(shape), lambda s: (0,) * len(shape))


def a_slice(shape, first=0):
    rest = (0,) * (len(shape) - 1)
    return pl.BlockSpec((1,) + tuple(shape[1:]), lambda s: (s + first,) + rest)


def expected(microseconds):
    return pl.CostEstimate(
        flops=int(microseconds * 1.15e9), bytes_accessed=0, transcendentals=0
    )


def conv_scratch(frames, rows, columns):
    lanes = (frames + 2) * columns
    return (
        pltpu.VMEM((2, rows + 16, lanes), jnp.float32),
        pltpu.VMEM((rows // BLOCK, 3 * SIDE, lanes), jnp.bfloat16),
    )


def conv_forward(own, edges, group, w_in, w_out, bias_out):
    _, _, frames, rows, columns = own.shape
    first, slices = group
    lanes = (frames + 2) * columns
    span = w_in.shape[0]
    volume, windows = conv_scratch(frames, rows, columns)
    out_shape = [
        jax.ShapeDtypeStruct((slices, frames, rows, 2 * columns), jnp.float32),
        jax.ShapeDtypeStruct((slices, 2, rows, columns), jnp.bfloat16),
        jax.ShapeDtypeStruct((slices, 2, rows, columns), jnp.bfloat16),
        jax.ShapeDtypeStruct((slices, 2, lanes), jnp.bfloat16),
        jax.ShapeDtypeStruct((slices, 2, lanes), jnp.bfloat16),
    ]
    return pl.pallas_call(
        forward_kernel,
        grid=(slices,),
        in_specs=[a_slice(own.shape, first)]
        + [a_slice(one.shape) for one in edges]
        + [whole(w_in.shape), whole(w_out.shape), pl.BlockSpec(memory_space=pltpu.SMEM)],
        out_specs=[a_slice(one.shape) for one in out_shape],
        out_shape=out_shape,
        scratch_shapes=[
            volume,
            windows,
            volume,
            pltpu.VMEM((span, frames * columns), jnp.bfloat16),
            pltpu.VMEM((frames, DEPTH, columns), jnp.float32),
            pltpu.VMEM((rows // BLOCK, SIDE, lanes), jnp.float32),
        ],
        compiler_params=pltpu.CompilerParams(vmem_limit_bytes=VMEM),
        cost_estimate=expected(6 * slices),
        name="conv_forward",
    )(own, *edges, w_in, w_out, bias_out)


def hidden_again(own, edges, group, w_in):
    _, _, frames, rows, columns = own.shape
    first, slices = group
    volume, windows = conv_scratch(frames, rows, columns)
    shape = (slices, rows // BLOCK, w_in.shape[0], frames * columns)
    return pl.pallas_call(
        hidden_kernel,
        grid=(slices,),
        in_specs=[a_slice(own.shape, first)]
        + [a_slice(one.shape, first) for one in edges]
        + [whole(w_in.shape)],
        out_specs=[a_slice(shape)] * 2,
        out_shape=[jax.ShapeDtypeStruct(shape, jnp.bfloat16)] * 2,
        scratch_shapes=[volume, windows],
        compiler_params=pltpu.CompilerParams(vmem_limit_bytes=VMEM),
        cost_estimate=expected(5 * slices),
        name="hidden_again",
    )(own, *edges, w_in)


def conv_backward(own, edges, group, grad, grad_edges, hidden, slopes, w_back, extras):
    _, _, frames, rows, columns = own.shape
    first, slices = group
    span = w_back.shape[0]
    volume, windows = conv_scratch(frames, rows, columns)
    total = pltpu.VMEM((span, 2 * 128), jnp.float32)
    fixed = (w_back, pick_table(), extras)
    here = (own, *edges, grad, *grad_edges)
    kept = (hidden, slopes)
    return pl.pallas_call(
        backward_kernel,
        grid=(slices,),
        in_specs=[a_slice(one.shape, first) for one in here]
        + [a_slice(one.shape) for one in kept]
        + [whole(one.shape) for one in fixed],
        out_specs=whole(extras.shape),
        out_shape=jax.ShapeDtypeStruct(extras.shape, jnp.float32),
        scratch_shapes=[
            volume,
            windows,
            windows,
            pltpu.VMEM((span, frames * columns), jnp.bfloat16),
            total,
            total,
        ],
        compiler_params=pltpu.CompilerParams(vmem_limit_bytes=VMEM),
        cost_estimate=expected(6 * slices),
        name="conv_backward",
    )(*here, *kept, *fixed)


def along(axis, step):
    count = lax.axis_size(axis)
    return [(i, i + step) for i in range(count) if 0 <= i + step < count]


def sum_over(array, axis):
    size = lax.axis_size(axis)
    if size & (size - 1):
        return lax.psum(array, axis)

    def other(values, bits):
        return lax.ppermute(values, axis, [(i, i ^ bits) for i in range(size)])

    bit = 1
    if size.bit_length() % 2 == 0:
        array = array + other(array, bit)
        bit = 2
    while bit < size:
        one, two, three = (other(array, bit * k) for k in (1, 2, 3))
        array = (array + one) + (two + three)
        bit *= 4
    return array


def share_edges(low, high, first, last):
    below = lax.ppermute(high, "af", along("af", 1))
    above = lax.ppermute(low, "af", along("af", -1))

    def around(middle, at):
        return jnp.concatenate([below[:, :, at], middle, above[:, :, at]], axis=2)

    left = lax.ppermute(around(last, low.shape[2] - 1), "row", along("row", 1))
    right = lax.ppermute(around(first, 0), "row", along("row", -1))
    return below, above, left, right


def image_edges(image, group):
    start, slices = group
    part = image[start : start + slices]
    _, _, frames, rows, columns = part.shape
    flat = (slices, 2, frames * columns)
    return share_edges(
        part[:, :, 0], part[:, :, frames - 1],
        part[:, :, :, 0].reshape(flat), part[:, :, :, rows - 1].reshape(flat),
    )


def return_edges(part_below, part_above, part_left, part_right, columns):
    lower = lax.ppermute(part_left, "row", along("row", -1))
    upper = lax.ppermute(part_right, "row", along("row", 1))
    rows = part_below.shape[2]
    row = lax.broadcasted_iota(jnp.int32, (1, 1, rows, 1), 2)

    def with_rows(frame, at):
        top = upper[:, :, None, at].astype(jnp.float32)
        end = lower[:, :, None, at].astype(jnp.float32)
        added = jnp.where(row == 0, top, 0.0) + jnp.where(row == rows - 1, end, 0.0)
        return (frame.astype(jnp.float32) + added).astype(jnp.bfloat16)

    lanes = part_left.shape[2]
    from_above = lax.ppermute(
        with_rows(part_below, slice(0, columns)), "af", along("af", -1)
    )
    from_below = lax.ppermute(
        with_rows(part_above, slice(lanes - columns, lanes)), "af", along("af", 1)
    )
    return from_below, from_above, upper, lower


def image_kernel(main, from_below, from_above, upper, lower, table, note, out, image):
    slices, frames, rows, twice = main.shape
    columns = twice // 2
    row = lax.broadcasted_iota(jnp.int32, (rows, columns), 0)
    for s in range(slices):
        tops = upper[s].astype(jnp.float32)
        ends = lower[s].astype(jnp.float32)
        for f in range(frames):
            at = slice((f + 1) * columns, (f + 2) * columns)
            for o in range(2):
                here = slice(o * columns, (o + 1) * columns)
                value = main[s, f, :, here]
                if f == 0:
                    value = value + from_below[s, o].astype(jnp.float32)
                if f == frames - 1:
                    value = value + from_above[s, o].astype(jnp.float32)
                value = value + jnp.where(row == 0, tops[o : o + 1, at], 0.0)
                value = value + jnp.where(row == rows - 1, ends[o : o + 1, at], 0.0)
                start = (s * frames + f) * rows
                image[start : start + rows, here] = value.astype(jnp.bfloat16)
    size = slices * frames * rows
    for start in range(0, size, 512):
        stop = min(start + 512, size)
        out[:, start:stop] = lax.dot_general(
            table[...], image[start:stop, :], NT, preferred_element_type=jnp.float32
        ).astype(jnp.bfloat16)
    rest = out.shape[1] - size
    if rest:
        lane = lax.broadcasted_iota(jnp.int32, (out.shape[0], rest), 1)
        out[:, size:] = jnp.where(lane == 0, note[0, 0], 0.0).astype(jnp.bfloat16)


def image_to_hybrid(main, added, table, note, lanes):
    slices, frames, rows, twice = main.shape
    return pl.pallas_call(
        image_kernel,
        in_specs=[pl.BlockSpec(memory_space=pltpu.VMEM)] * 6
        + [pl.BlockSpec(memory_space=pltpu.SMEM)],
        out_shape=jax.ShapeDtypeStruct((twice, lanes), jnp.bfloat16),
        scratch_shapes=[pltpu.VMEM((slices * frames * rows, twice), jnp.bfloat16)],
        compiler_params=pltpu.CompilerParams(vmem_limit_bytes=VMEM),
        cost_estimate=expected(slices / 2),
        name="image_to_hybrid",
    )(main, *added, table, note)


def grad_image_kernel(hybrid, table, out, low, high, first, last, sums):
    slices, _, frames, rows, columns = out.shape
    sums[...] = jnp.zeros_like(sums)
    for s in range(slices):
        size = frames * rows
        start = s * size // 128 * 128
        stop = -(-(s + 1) * size // 128) * 128
        value = lax.dot_general(
            hybrid[:, start:stop], table[...], TN, preferred_element_type=jnp.float32
        ).astype(jnp.bfloat16)
        for c in range(2):
            tops, ends = [], []
            for f in range(frames):
                at = s * size + f * rows - start
                piece = value[at : at + rows, c * columns : (c + 1) * columns]
                out[s, c, f] = piece
                if f == 0:
                    low[s, c] = piece
                if f == frames - 1:
                    high[s, c] = piece
                wide = piece.astype(jnp.float32)
                sums[c : c + 1, :] += jnp.sum(wide, axis=0, keepdims=True)
                tops.append(wide[0:1])
                ends.append(wide[rows - 1 :])
            first[s, c : c + 1, :] = jnp.concatenate(tops, axis=1)
            last[s, c : c + 1, :] = jnp.concatenate(ends, axis=1)


def hybrid_to_grad(hybrid, table, shape):
    slices, channels, frames, rows, columns = shape
    edge_frame = jax.ShapeDtypeStruct((slices, channels, rows, columns), jnp.bfloat16)
    edge_row = jax.ShapeDtypeStruct((slices, channels, frames * columns), jnp.float32)
    return pl.pallas_call(
        grad_image_kernel,
        out_shape=[
            jax.ShapeDtypeStruct(shape, jnp.bfloat16),
            edge_frame,
            edge_frame,
            edge_row,
            edge_row,
            jax.ShapeDtypeStruct((2, columns), jnp.float32),
        ],
        compiler_params=pltpu.CompilerParams(vmem_limit_bytes=VMEM),
        cost_estimate=expected(slices / 2),
        name="hybrid_to_grad",
    )(hybrid, table)


def chunk_transpose(pieces, low_half, even):
    a, c, b, d = pieces
    a, b = (
        jnp.where(low_half, a, pltpu.roll(b, 64, axis=1)),
        jnp.where(low_half, pltpu.roll(a, 64, axis=1), b),
    )
    c, d = (
        jnp.where(low_half, c, pltpu.roll(d, 64, axis=1)),
        jnp.where(low_half, pltpu.roll(c, 64, axis=1), d),
    )
    return (
        jnp.where(even, a, pltpu.roll(c, 32, axis=1)),
        jnp.where(even, pltpu.roll(a, 96, axis=1), c),
        jnp.where(even, b, pltpu.roll(d, 32, axis=1)),
        jnp.where(even, pltpu.roll(b, 96, axis=1), d),
    )


def kspace_kernel(
    frames_here, received, measured, target, sampled, share, scale, table, out, loss,
    spectrum, grads, loss_lanes,
):
    groups, _, lanes = received.shape
    pairs, n_af, _, twice = spectrum.shape
    rows = twice // 2
    n_row = groups // n_af
    frames = n_af * frames_here
    step = pl.program_id(0)
    lane = lax.broadcasted_iota(jnp.int32, (SIDE, 128), 1)
    low_half = lane < 64
    even = lane % 64 < 32

    @pl.when(step == 0)
    def _():
        loss_lanes[...] = jnp.zeros_like(loss_lanes)
        def gather(af, carry):
            for tile in range(lanes // 128):
                for h in range(n_row // 4):
                    source = [
                        received[af * n_row + h * 4 + m, :, tile * 128 : (tile + 1) * 128]
                        for m in range(4)
                    ]
                    moved = chunk_transpose(source, low_half, even)
                    for k in range(4):
                        if tile * 4 + k < pairs:
                            wide = moved[k].astype(jnp.float32)
                            for c in range(2):
                                at = c * rows + h * 128
                                spectrum[tile * 4 + k, af, :, at : at + 128] = wide[
                                    c * 8 : (c + 1) * 8
                                ]
            return carry

        lax.fori_loop(0, n_af, gather, 0)

    first = step * frames_here
    size = frames * 8
    here = spectrum[pl.ds(first, frames_here)].reshape(size, twice).astype(jnp.bfloat16)
    kspace = jnp.dot(here, table[...], preferred_element_type=jnp.float32)

    def place(t):
        return (t % frames_here) * n_af + t // frames_here

    filled = []
    for t in range(frames):
        mask = sampled[t]
        filled.append(mask * measured[0, t] + (1.0 - mask) * kspace[place(t) * 8 : place(t) * 8 + 8])
    slopes = []
    for t in range(frames):
        mask = sampled[t]
        near = range(max(t - 2, 0), min(t + 3, frames))
        shared = sum(share[t, s] * filled[s] for s in near)
        differ = mask * measured[0, t] + (1.0 - mask) * shared - target[0, t]
        square = differ * differ + 1.0
        inverse = lax.rsqrt(square)
        loss_lanes[...] += (1.0 - mask) * (square * inverse - 1.0)
        slopes.append((1.0 - mask) * differ * inverse * scale[0, 0])
    for s in range(frames):
        near = range(max(s - 2, 0), min(s + 3, frames))
        grad = sum(share[t, s] * slopes[t] for t in near)
        grads[place(s) * 8 : place(s) * 8 + 8, :] = (1.0 - sampled[s]) * grad
    grad = grads[...]
    high = grad.astype(jnp.bfloat16)
    low = (grad - high.astype(jnp.float32)).astype(jnp.bfloat16)
    back = lax.dot_general(high, table[...], NT, preferred_element_type=jnp.float32)
    back += lax.dot_general(low, table[...], NT, preferred_element_type=jnp.float32)
    spectrum[pl.ds(first, frames_here)] = back.reshape(frames_here, n_af, 8, twice)

    @pl.when(step == pl.num_programs(0) - 1)
    def _():
        loss[...] = loss_lanes[...]

        def scatter(af, carry):
            for tile in range(lanes // 128):
                for h in range(n_row // 4):
                    source = []
                    for k in range(4):
                        pair = min(tile * 4 + k, pairs - 1)
                        both = [
                            spectrum[pair, af, :, c * rows + h * 128 : c * rows + h * 128 + 128]
                            for c in range(2)
                        ]
                        source.append(jnp.concatenate(both, axis=0).astype(jnp.bfloat16))
                    moved = chunk_transpose(source, low_half, even)
                    for m in range(4):
                        out[af * n_row + h * 4 + m, :, tile * 128 : (tile + 1) * 128] = moved[m]
            return carry

        lax.fori_loop(0, n_af, scatter, 0)


def kspace_step(received, measured, target, sampled, share, scale, table, frames_here, group):
    _, frames, lines, twice = measured.shape
    first, slices = group
    n_af = frames // frames_here
    smem = pl.BlockSpec(memory_space=pltpu.SMEM)
    return pl.pallas_call(
        functools.partial(kspace_kernel, frames_here),
        grid=(slices,),
        in_specs=[
            whole(received.shape),
            a_slice(measured.shape, first),
            a_slice(target.shape, first),
            whole(sampled.shape),
            smem,
            smem,
            whole(table.shape),
        ],
        out_specs=[whole(received.shape), whole((lines, twice))],
        out_shape=[
            jax.ShapeDtypeStruct(received.shape, jnp.bfloat16),
            jax.ShapeDtypeStruct((lines, twice), jnp.float32),
        ],
        scratch_shapes=[
            pltpu.VMEM((slices * frames_here, n_af, lines, twice), jnp.float32),
            pltpu.VMEM((frames * lines, twice), jnp.float32),
            pltpu.VMEM((lines, twice), jnp.float32),
        ],
        compiler_params=pltpu.CompilerParams(vmem_limit_bytes=VMEM),
        cost_estimate=expected(3 * slices),
        name="kspace",
    )(received, measured, target, sampled, share, scale, table)


def middle_plain(main, added, measured, target, sampled, share, table_y, table_x):
    highest = lax.Precision.HIGHEST
    slices, frames_here, rows_here, twice = main.shape
    count = lax.psum(jnp.sum(1.0 - sampled) * (2.0 * slices * measured.shape[3] / 2), AXES)
    columns = twice // 2
    frames, lines = measured.shape[1:3]
    rows = measured.shape[3] // 2
    table_y = jnp.asarray(table_y, jnp.bfloat16)
    table_x = jnp.asarray(table_x, jnp.bfloat16)
    image = main.reshape(slices, frames_here, rows_here, 2, columns)
    below, above, upper, lower = (one.astype(jnp.float32) for one in added)
    image = image.at[:, 0].add(below.transpose(0, 2, 1, 3))
    image = image.at[:, frames_here - 1].add(above.transpose(0, 2, 1, 3))
    for at, line in ((0, upper), (rows_here - 1, lower)):
        line = line[:, :, columns:-columns].reshape(slices, 2, frames_here, columns)
        image = image.at[:, :, at].add(line.transpose(0, 2, 1, 3))
    flat = image.reshape(slices, frames_here, rows_here, twice).astype(jnp.bfloat16)
    hybrid = jnp.dot(flat, table_y, preferred_element_type=jnp.float32).astype(jnp.bfloat16)
    hybrid = hybrid.reshape(slices, frames_here, rows_here, 2, columns)
    part = lax.all_to_all(hybrid, "af", split_axis=4, concat_axis=1, tiled=True)
    spread = lax.all_to_all(part, "row", split_axis=4, concat_axis=2, tiled=True)
    spectrum = jnp.transpose(spread, (0, 1, 4, 3, 2)).reshape(slices, frames, lines, 2 * rows)
    kspace = jnp.dot(spectrum, table_x, preferred_element_type=jnp.float32)
    mask = sampled[None, :, :, None]
    filled = mask * measured + (1.0 - mask) * kspace
    shared = jnp.einsum("ts,bslk->btlk", share, filled, precision=highest)
    differ = mask * measured + (1.0 - mask) * shared - target
    root = jnp.sqrt(differ * differ + 1.0)
    loss = jnp.sum((1.0 - mask) * (root - 1.0))
    slope = (1.0 - mask) * differ / root / count
    grad = (1.0 - mask) * jnp.einsum("ts,btlk->bslk", share, slope, precision=highest)
    back = jnp.dot(grad, table_x.T.astype(jnp.float32), precision=highest).astype(jnp.bfloat16)
    back = jnp.transpose(back.reshape(slices, frames, lines, 2, rows), (0, 1, 4, 3, 2))
    part = lax.all_to_all(back, "row", split_axis=2, concat_axis=4, tiled=True)
    whole_rows = lax.all_to_all(part, "af", split_axis=1, concat_axis=4, tiled=True)
    grad = jnp.dot(
        whole_rows.reshape(slices, frames_here, rows_here, twice),
        table_y.T,
        preferred_element_type=jnp.float32,
    ).reshape(slices, frames_here, rows_here, 2, columns)
    grad = jnp.transpose(grad, (0, 3, 1, 2, 4)).astype(jnp.bfloat16)
    return loss, count, grad, jnp.sum(grad.astype(jnp.float32), axis=(0, 2, 3, 4))


def packed_extras(width, loss, sums):
    row = jnp.concatenate([loss.reshape(1), sums])
    return jnp.pad(row.reshape(1, 3), ((width, 7), (0, PACKED - 3)))


def middle_fast(
    main, added, measured, target, sampled, share, table_y, table_x, between, after
):
    devices = lax.axis_size("af") * lax.axis_size("row")
    slices, frames_here, rows, twice = main.shape
    lines, readout = measured.shape[2:]
    size = slices * frames_here * rows
    order = np.arange(twice).reshape(2, devices, lines).transpose(1, 0, 2).reshape(-1)
    permuted = jnp.asarray(np.ascontiguousarray(table_y[:, order].T), jnp.bfloat16)
    mask = jnp.broadcast_to(sampled[:, :, None], sampled.shape + (readout,))
    note = jnp.sum(1.0 - sampled).reshape(1, 1)
    lanes = (size // 128 + 1) * 128
    hybrid = image_to_hybrid(main, added, permuted, note, lanes)
    received = lax.all_to_all(
        hybrid.reshape(devices, 2 * lines, lanes), AXES, 0, 0, tiled=True
    )
    first = between(hybrid)
    received, first = lax.optimization_barrier((received, first))
    notes = received[:, 0, size].astype(jnp.float32)
    count = jnp.sum(notes) * (1.0 * slices * readout)
    back, loss = kspace_step(
        received, measured, target, mask, share, (1.0 / count).reshape(1, 1),
        jnp.asarray(table_x, jnp.bfloat16), frames_here, (0, slices),
    )
    returned = lax.all_to_all(back, AXES, 0, 0, tiled=True)
    second = after(back)
    returned, second = lax.optimization_barrier((returned, second))
    shape = (slices, 2, frames_here, rows, twice // 2)
    grad, *grad_edge, sums = hybrid_to_grad(returned.reshape(twice, lanes), permuted, shape)
    return jnp.sum(loss), count, grad, grad_edge, jnp.sum(sums, axis=1), first, second


def train_step(
    image_in, measured, target, sampled, share, table_y, table_x, w_in, w_out, w_back, bias_out
):
    slices, _, frames_here, rows, columns = image_in.shape
    frames, lines = measured.shape[1:3]
    cut = (slices + 1) // 2
    groups = [(0, cut), (cut, slices - cut)]
    edges = image_edges(image_in, (0, slices))
    main, *part = conv_forward(image_in, edges, (0, slices), w_in, w_out, bias_out)
    added = return_edges(*part, columns)

    def again(group):
        def compute(after):
            held, _ = lax.optimization_barrier((w_in, after))
            return hidden_again(image_in, edges, group, held)

        return compute

    fits = rows == 32 and lines == 8 and lax.axis_size("row") % 4 == 0
    fits = fits and frames * lines <= 256
    if fits:
        loss, count, grad, grad_edge, sums, *kept = middle_fast(
            main, added, measured, target, sampled, share, table_y, table_x,
            again(groups[0]), again(groups[1]),
        )
    else:
        loss, count, grad, sums = middle_plain(
            main, added, measured, target, sampled, share, table_y, table_x
        )
        flat = (slices, 2, frames_here * columns)
        grad_edge = (
            grad[:, :, 0], grad[:, :, frames_here - 1],
            grad[:, :, :, 0].reshape(flat), grad[:, :, :, rows - 1].reshape(flat),
        )
        kept = []
    around = share_edges(*grad_edge)
    total = packed_extras(w_in.shape[0] // BLOCK, loss, sums)
    for index, group in enumerate(groups):
        hidden, slopes = kept[index] if kept else again(group)(total)
        total = conv_backward(
            image_in, edges, group, grad, around, hidden, slopes, w_back, total
        )
    return count, total


def on_device(
    image_in, measured, target, line_mask, window_half, in_kernel, out_kernel, biases,
    in_moment, out_moment, bias_moment, in_square, out_square, bias_square,
    in_smooth, out_smooth, bias_smooth,
):
    slices, _, frames_here, rows_here, columns = image_in.shape
    frames = measured.shape[1]
    width = in_kernel.shape[0]
    rows = rows_here * lax.axis_size("row")
    table_y = dft_table(columns)
    table_x = dft_table(rows)
    share = share_matrix(window_half, frames)
    sampled = line_mask.astype(jnp.float32)
    w_in = conv_in_weights(in_kernel, biases[:width])
    w_out = conv_out_weights(out_kernel)
    w_back = conv_back_weights(out_kernel)

    count, total = train_step(
        image_in, measured, target, sampled, share, table_y, table_x,
        w_in, w_out, w_back, biases[width:],
    )
    total = sum_over(sum_over(total, "row"), "af")
    loss_total = total[width, 0]
    grad_in = total[:width, :54]
    grad_out = total[:width, PACKED // 2 : PACKED // 2 + 54].T.reshape(out_kernel.shape)
    grad_bias = jnp.concatenate([total[:width, 54], total[width, 1:3]])
    in_first, in_second, in_master = adam_step(in_kernel, grad_in, in_moment, in_square, rate_in)
    out_first, out_second, out_master = adam_step(
        out_kernel, grad_out, out_moment, out_square, rate_out
    )
    bias_first, bias_second, bias_master = adam_step(
        biases, grad_bias, bias_moment, bias_square, rate_bias
    )
    in_average = average_keep * in_smooth + (1.0 - average_keep) * in_master
    out_average = average_keep * out_smooth + (1.0 - average_keep) * out_master
    bias_average = average_keep * bias_smooth + (1.0 - average_keep) * bias_master
    return (
        loss_total, count,
        in_first, out_first, bias_first,
        in_second, out_second, bias_second,
        in_master, out_master, bias_master,
        in_average, out_average, bias_average,
        in_master.astype(jnp.bfloat16), out_master.astype(jnp.bfloat16), bias_master.astype(jnp.bfloat16),
    )


def solution(mesh):
    in_specs = (
        P(None, None, "af", "row", None),
        P(None, None, ("af", "row"), None),
        P(None, None, ("af", "row"), None),
        P(None, ("af", "row")),
    ) + (P(),) * 13
    return jax.shard_map(
        on_device, mesh=mesh, in_specs=in_specs, out_specs=(P(),) * 17, check_vma=False
    )
```

```python
import functools
import math

import jax
import jax.numpy as jnp
import numpy as np
from jax import lax
from jax.experimental import pallas as pl
from jax.experimental.pallas import tpu as pltpu
from jax.sharding import PartitionSpec as P

STEP = 5
AXES = ("af", "row")
BLOCK = 4
WIN = 8
SIDE = 16
DEPTH = 9 * SIDE
ONES_ROW = BLOCK + 2
PACKED = 128
EDGES = 6
BIAS_LANE = WIN - 1
VMEM = 60 * 2**20
GELU = math.sqrt(2.0 / math.pi)
CUBE = 0.044715

beta_first = 0.5
beta_second = 0.5
rate_in = 0.2
rate_out = 0.04
rate_bias = 0.3
decay_weight = 0.01
average_keep = 0.9
epsilon = 1e-08

NT = (((1,), (1,)), ((), ()))
TN = (((0,), (0,)), ((), ()))


def dft_table(length):
    index = np.arange(length)
    phase = (index[:, None] * index[None, :] % length) * (2.0 * math.pi / length)
    cosine = np.cos(phase) / math.sqrt(length)
    sine = np.sin(phase) / math.sqrt(length)
    upper = np.concatenate([cosine, -sine], axis=1)
    lower = np.concatenate([sine, cosine], axis=1)
    return np.concatenate([upper, lower], axis=0).astype(np.float32)


def share_matrix(window_half, frames):
    index = jnp.arange(frames, dtype=jnp.int32)
    inside = (jnp.abs(index[None, :] - index[:, None]) <= window_half[:, None]).astype(jnp.float32)
    return inside / jnp.sum(inside, axis=1, keepdims=True)


def adam_step(master, grad, first, second, rate):
    first_new = beta_first * first + (1.0 - beta_first) * grad
    second_new = beta_second * second + (1.0 - beta_second) * grad * grad
    first_hat = first_new / (1.0 - beta_first**STEP)
    second_hat = second_new / (1.0 - beta_second**STEP)
    master_new = master - rate * (
        first_hat / (jnp.sqrt(second_hat) + epsilon) + decay_weight * master
    )
    return (first_new, second_new, master_new)


def conv_in_weights(kernel, bias):
    width = kernel.shape[0]
    taps = kernel.astype(jnp.bfloat16).astype(jnp.float32).reshape(width, 2, 3, 3, 3)
    rows = []
    for j in range(BLOCK):
        row = jnp.pad(taps, ((0, 0), (0, 0), (0, 0), (j, WIN - 3 - j), (0, 0)))
        rows.append(row.transpose(0, 2, 4, 1, 3))
    spread = jnp.stack(rows)
    high = lax.reduce_precision(bias, 8, 7)
    rest = bias - high
    middle = lax.reduce_precision(rest, 8, 7)
    parts = jnp.stack([high, middle, rest - middle], axis=1)
    spread = spread.at[:, :, :, 0, 0, ONES_ROW].set(jnp.broadcast_to(parts, (BLOCK, width, 3)))
    return 0.5 * spread.reshape(BLOCK * width, DEPTH)


def conv_out_weights(kernel):
    width = kernel.shape[2]
    taps = kernel.astype(jnp.bfloat16).reshape(3, 3, 3, 2, width)[:, ::-1]
    columns = []
    for j in range(BLOCK):
        column = jnp.pad(taps, ((0, 0), (j, WIN - 3 - j), (0, 0), (0, 0), (0, 0)))
        columns.append(column.transpose(0, 2, 3, 1, 4))
    return jnp.stack(columns, axis=4).reshape(DEPTH, BLOCK * width)


def conv_back_weights(kernel):
    width = kernel.shape[2]
    taps = kernel.astype(jnp.bfloat16).reshape(3, 3, 3, 2, width)[::-1, ::-1, ::-1]
    rows = []
    for j in range(BLOCK):
        row = jnp.pad(taps, ((0, 0), (j, WIN - 3 - j), (0, 0), (0, 0), (0, 0)))
        rows.append(row.transpose(0, 2, 3, 1, 4))
    return 0.5 * jnp.stack(rows, axis=4).reshape(DEPTH, BLOCK * width)


def pick_table():
    table = np.zeros((2, 256, PACKED), np.float32)
    for a, b, e, c in np.ndindex(3, 3, 3, 2):
        lane = ((a * 3 + e) * 2 + c) * WIN + b
        table[0, lane, 27 * c + 9 * a + 3 * b + e] = 1.0
        tap = 9 * (2 - a) + 3 * (2 - b) + 2 - e
        table[1, lane, PACKED // 2 + 2 * tap + c] = 1.0
    table[0, BIAS_LANE, 54] = 1.0
    return jnp.asarray(table, jnp.bfloat16)


def load_volume(volume, own, below, above, left, right, corner_below, corner_above):
    _, channels, frames, rows, columns = own.shape
    lanes = (frames + 2) * columns
    for c in range(channels):
        volume[c, rows + 8 : rows + 16, :] = jnp.zeros((8, lanes), jnp.float32)
        for t in range(frames + 2):
            if t == 0:
                piece = below[0, c]
            elif t == frames + 1:
                piece = above[0, c]
            else:
                piece = own[0, c, t - 1]
            volume[c, 8 : 8 + rows, t * columns : (t + 1) * columns] = piece.astype(jnp.float32)
    low = corner_below[0].astype(jnp.float32)
    high = corner_above[0].astype(jnp.float32)
    for side, at, line in ((0, 7, left), (1, rows + 8, right)):
        middle = line[0].astype(jnp.float32)
        for c in range(channels):
            k = 2 * side + c
            volume[c, at : at + 1, 0:columns] = low[k : k + 1]
            volume[c, at : at + 1, columns : lanes - columns] = middle[c : c + 1]
            volume[c, at : at + 1, lanes - columns :] = high[k : k + 1]


def build_windows(volume, windows, columns, ones):
    blocks, _, lanes = windows.shape
    column = lax.broadcasted_iota(jnp.int32, (SIDE, columns), 1)
    row = lax.broadcasted_iota(jnp.int32, (SIDE, columns), 0)
    zero = jnp.zeros((SIDE, columns), jnp.bfloat16)
    for block in range(blocks):
        for t in range(lanes // columns):
            here = slice(t * columns, (t + 1) * columns)
            start = 7 + BLOCK * block
            window = jnp.concatenate(
                [volume[c, start : start + WIN, here] for c in range(2)], axis=0
            ).astype(jnp.bfloat16)
            for e in range(3):
                shifted = window
                if e != 1:
                    shifted = pltpu.roll(window, (1 - e) % columns, axis=1)
                    shifted = jnp.where(column == (0 if e == 0 else columns - 1), zero, shifted)
                if ones and e == 0:
                    shifted = jnp.where(row == ONES_ROW, zero + 1.0, shifted)
                windows[block, e * SIDE : (e + 1) * SIDE, here] = shifted


def forward_kernel(
    own, *refs,
):
    edges, refs = refs[:EDGES], refs[EDGES:]
    (
    w_in, w_out, bias_out,
    main, part_below, part_above, part_left, part_right,
    volume, windows, total, hidden, mixed, spread,
    ) = refs
    _, _, frames, rows, columns = own.shape
    blocks = windows.shape[0]
    load_volume(volume, own, *edges)
    build_windows(volume, windows, columns, True)
    column = lax.broadcasted_iota(jnp.int32, (SIDE, columns), 1)

    def step(block, carry):
        for f in range(frames):
            here = slice(f * columns, (f + 1) * columns)
            patch = jnp.concatenate(
                [windows[block, :, (f + a) * columns : (f + a + 1) * columns] for a in range(3)],
                axis=0,
            )
            half = jnp.dot(w_in[...], patch, preferred_element_type=jnp.float32)
            t = jnp.tanh(half * (2.0 * GELU + (8.0 * GELU * CUBE) * (half * half)))
            hidden[:, here] = (half + half * t).astype(jnp.bfloat16)
        for f in range(frames):
            here = slice(f * columns, (f + 1) * columns)
            mixed[f] = jnp.dot(w_out[...], hidden[:, here], preferred_element_type=jnp.float32)
        for t in range(frames + 2):
            window = None
            for e in range(3):
                summed = None
                for a in range(3):
                    f = t - 2 + a
                    if 0 <= f < frames:
                        start = (a * 3 + e) * SIDE
                        piece = mixed[f, start : start + SIDE, :]
                        summed = piece if summed is None else summed + piece
                if e != 1:
                    summed = pltpu.roll(summed, (1 - e) % columns, axis=1)
                    summed = jnp.where(column == (0 if e == 0 else columns - 1), 0.0, summed)
                window = summed if window is None else window + summed
            spread[block, :, t * columns : (t + 1) * columns] = window
        return carry

    lax.fori_loop(0, blocks, step, 0, unroll=True)
    total[...] = jnp.zeros_like(total)
    for block in range(blocks):
        for o in range(2):
            start = 7 + BLOCK * block
            total[o, start : start + WIN, :] = (
                total[o, start : start + WIN, :] + spread[block, o * WIN : (o + 1) * WIN, :]
            )
    for o in range(2):
        for t in range(frames + 2):
            here = total[o, 8 : 8 + rows, t * columns : (t + 1) * columns]
            if t == 0:
                part_below[0, o] = here.astype(jnp.bfloat16)
            elif t == frames + 1:
                part_above[0, o] = here.astype(jnp.bfloat16)
            else:
                base = volume[o, 8 : 8 + rows, t * columns : (t + 1) * columns] + bias_out[o]
                main[0, t - 1, :, o * columns : (o + 1) * columns] = base + here
    for at, out in ((7, part_left), (8 + rows, part_right)):
        both = [total[o, at : at + 1, :] for o in range(2)]
        out[0] = jnp.concatenate(both, axis=0).astype(jnp.bfloat16)


def patches(source, block, frames, columns):
    return jnp.concatenate(
        [source[block, :, a * columns : (a + frames) * columns] for a in range(3)], axis=0
    )


def hidden_kernel(own, *refs):
    edges, (w_in, *_, hidden, slopes, volume, windows) = refs[:EDGES], refs[EDGES:]
    _, _, frames, rows, columns = own.shape
    load_volume(volume, own, *edges)
    build_windows(volume, windows, columns, True)

    def step(block, carry):
        patch = patches(windows, block, frames, columns)
        for f in range(frames):
            here = slice(f * columns, (f + 1) * columns)
            half = lax.dot_general(
                patch[:, here], w_in[...], TN, preferred_element_type=jnp.float32
            )
            u = half * half
            t = jnp.tanh(half * (2.0 * GELU + (8.0 * GELU * CUBE) * u))
            up = 1.0 + t
            hidden[0, block, here, :] = (half * up).astype(jnp.bfloat16)
            slope = half * (2.0 * GELU + (24.0 * GELU * CUBE) * u)
            slopes[0, block, here, :] = (up + (up * (1.0 - t)) * slope).astype(jnp.bfloat16)
        return carry

    lax.fori_loop(0, windows.shape[0], step, 0, unroll=True)


def backward_kernel(
    own, *refs,
):
    edges, grad, grad_edges = refs[:EDGES], refs[EDGES], refs[EDGES + 1 : 2 * EDGES + 1]
    (
        hidden, slopes, w_back, pick, extras, out,
        volume, windows, grad_windows, grads, sum_in, sum_out,
    ) = refs[2 * EDGES + 1 :]
    _, _, frames, rows, columns = own.shape

    part = pl.program_id(1)

    @pl.when((pl.program_id(0) == 0) & (part == 0))
    def _():
        sum_in[...] = jnp.zeros_like(sum_in)
        sum_out[...] = jnp.zeros_like(sum_out)

    @pl.when(part == 0)
    def _():
        load_volume(volume, own, *edges)
        build_windows(volume, windows, columns, True)
        load_volume(volume, grad, *grad_edges)
        build_windows(volume, grad_windows, columns, False)

    blocks = hidden.shape[1]

    def step(at):
        block = part * blocks + at
        patch = patches(windows, block, frames, columns)
        grad_patch = patches(grad_windows, block, frames, columns)
        for f in range(frames):
            here = slice(f * columns, (f + 1) * columns)
            gh = lax.dot_general(
                grad_patch[:, here], w_back[...], TN, preferred_element_type=jnp.float32
            )
            grads[here, :] = (slopes[0, at, here, :].astype(jnp.float32) * gh).astype(
                jnp.bfloat16
            )
        sum_in[:DEPTH, :] += jnp.dot(patch, grads[...], preferred_element_type=jnp.float32)
        sum_out[:DEPTH, :] += jnp.dot(
            grad_patch, hidden[0, at], preferred_element_type=jnp.float32
        )

    for at in range(blocks):
        step(at)

    @pl.when((pl.program_id(0) == pl.num_programs(0) - 1) & (part == pl.num_programs(1) - 1))
    def _():
        width = sum_in.shape[1] // BLOCK
        lanes = sum_in.shape[0]
        lane = lax.broadcasted_iota(jnp.int32, (width, lanes), 1)
        picked = jnp.zeros((width, pick.shape[2]), jnp.float32)
        for index, source in enumerate((sum_in[...].T, sum_out[...].T)):
            folded = source[0:width, :]
            bias = folded
            for j in range(1, BLOCK):
                piece = source[j * width : (j + 1) * width, :]
                folded = folded + pltpu.roll(piece, lanes - j, axis=1)
                bias = bias + piece
            if index == 0:
                moved = pltpu.roll(bias, BIAS_LANE - ONES_ROW, axis=1)
                folded = jnp.where(lane == BIAS_LANE, moved, folded)
            for _ in range(3):
                piece = folded.astype(jnp.bfloat16)
                folded = folded - piece.astype(jnp.float32)
                picked = picked + jnp.dot(piece, pick[index], preferred_element_type=jnp.float32)
        out[0:width, :] = picked + extras[0:width, :]
        out[width:, :] = extras[width:, :]


def whole(shape):
    return pl.BlockSpec(tuple(shape), lambda s: (0,) * len(shape))


def a_slice(shape, first=0):
    rest = (0,) * (len(shape) - 1)
    return pl.BlockSpec((1,) + tuple(shape[1:]), lambda s: (s + first,) + rest)


def expected(microseconds):
    return pl.CostEstimate(
        flops=int(microseconds * 1.15e9), bytes_accessed=0, transcendentals=0
    )


def conv_scratch(frames, rows, columns):
    lanes = (frames + 2) * columns
    return (
        pltpu.VMEM((2, rows + 16, lanes), jnp.float32),
        pltpu.VMEM((rows // BLOCK, 3 * SIDE, lanes), jnp.bfloat16),
    )


def conv_forward(own, edges, group, w_in, w_out, bias_out):
    _, _, frames, rows, columns = own.shape
    first, slices = group
    lanes = (frames + 2) * columns
    span = w_in.shape[0]
    volume, windows = conv_scratch(frames, rows, columns)
    out_shape = [
        jax.ShapeDtypeStruct((slices, frames, rows, 2 * columns), jnp.float32),
        jax.ShapeDtypeStruct((slices, 2, rows, columns), jnp.bfloat16),
        jax.ShapeDtypeStruct((slices, 2, rows, columns), jnp.bfloat16),
        jax.ShapeDtypeStruct((slices, 2, lanes), jnp.bfloat16),
        jax.ShapeDtypeStruct((slices, 2, lanes), jnp.bfloat16),
    ]
    return pl.pallas_call(
        forward_kernel,
        grid=(slices,),
        in_specs=[a_slice(own.shape, first)]
        + [a_slice(one.shape) for one in edges]
        + [whole(w_in.shape), whole(w_out.shape), pl.BlockSpec(memory_space=pltpu.SMEM)],
        out_specs=[a_slice(one.shape) for one in out_shape],
        out_shape=out_shape,
        scratch_shapes=[
            volume,
            windows,
            volume,
            pltpu.VMEM((span, frames * columns), jnp.bfloat16),
            pltpu.VMEM((frames, DEPTH, columns), jnp.float32),
            pltpu.VMEM((rows // BLOCK, SIDE, lanes), jnp.float32),
        ],
        compiler_params=pltpu.CompilerParams(vmem_limit_bytes=VMEM),
        cost_estimate=expected(6 * slices),
        name="conv_forward",
    )(own, *edges, w_in, w_out, bias_out)


def hidden_again(own, edges, group, w_in, kept=()):
    _, _, frames, rows, columns = own.shape
    first, slices = group
    volume, windows = conv_scratch(frames, rows, columns)
    shape = (own.shape[0], rows // BLOCK, frames * columns, w_in.shape[1])
    return pl.pallas_call(
        hidden_kernel,
        grid=(slices,),
        in_specs=[a_slice(own.shape, first)]
        + [a_slice(one.shape, first) for one in edges]
        + [whole(w_in.shape)]
        + [pl.BlockSpec(memory_space=pl.ANY)] * len(kept),
        out_specs=[a_slice(shape, first)] * 2,
        out_shape=[jax.ShapeDtypeStruct(shape, jnp.bfloat16)] * 2,
        input_output_aliases={2 + EDGES + k: k for k in range(len(kept))},
        scratch_shapes=[volume, windows],
        compiler_params=pltpu.CompilerParams(vmem_limit_bytes=VMEM),
        cost_estimate=expected(5 * slices),
        name="hidden_again",
    )(own, *edges, w_in, *kept)


def conv_backward(own, edges, grad, grad_edges, hidden, slopes, w_back, extras):
    slices, _, frames, rows, columns = own.shape
    span = w_back.shape[1]
    volume, windows = conv_scratch(frames, rows, columns)
    total = pltpu.VMEM((2 * 128, span), jnp.float32)
    fixed = (w_back, pick_table(), extras)
    here = (own, *edges, grad, *grad_edges)
    blocks = rows // BLOCK
    parts = 1

    def of_slice(shape):
        rest = (0,) * (len(shape) - 1)
        return pl.BlockSpec((1,) + tuple(shape[1:]), lambda s, part: (s,) + rest)

    def part_of_slice(shape):
        size = (1, blocks // parts) + tuple(shape[2:])
        return pl.BlockSpec(size, lambda s, part: (s, part, 0, 0))

    def all_of(shape):
        return pl.BlockSpec(tuple(shape), lambda s, part: (0,) * len(shape))

    return pl.pallas_call(
        backward_kernel,
        grid=(slices, parts),
        in_specs=[of_slice(one.shape) for one in here]
        + [part_of_slice(one.shape) for one in (hidden, slopes)]
        + [all_of(one.shape) for one in fixed],
        out_specs=all_of(extras.shape),
        out_shape=jax.ShapeDtypeStruct(extras.shape, jnp.float32),
        scratch_shapes=[
            volume,
            windows,
            windows,
            pltpu.VMEM((frames * columns, span), jnp.bfloat16),
            total,
            total,
        ],
        compiler_params=pltpu.CompilerParams(vmem_limit_bytes=VMEM),
        cost_estimate=expected(5 * slices),
        name="conv_backward",
    )(*here, hidden, slopes, *fixed)


def along(axis, step):
    count = lax.axis_size(axis)
    return [(i, i + step) for i in range(count) if 0 <= i + step < count]


def sum_over(array, axis):
    size = lax.axis_size(axis)
    if size & (size - 1):
        return lax.psum(array, axis)

    def other(values, bits):
        return lax.ppermute(values, axis, [(i, i ^ bits) for i in range(size)])

    bit = 1
    if size.bit_length() % 2 == 0:
        array = array + other(array, bit)
        bit = 2
    while bit < size:
        one, two, three = (other(array, bit * k) for k in (1, 2, 3))
        array = (array + one) + (two + three)
        bit *= 4
    return array


def corners_along(left, right, columns):
    both = jnp.concatenate([left, right], axis=1)
    lanes = both.shape[2]
    below = lax.ppermute(both[:, :, lanes - columns :], "af", along("af", 1))
    above = lax.ppermute(both[:, :, :columns], "af", along("af", -1))
    return below, above


def share_edges(low, high, first, last):
    left = lax.ppermute(last, "row", along("row", 1))
    right = lax.ppermute(first, "row", along("row", -1))
    below = lax.ppermute(high, "af", along("af", 1))
    above = lax.ppermute(low, "af", along("af", -1))
    return below, above, left, right, *corners_along(left, right, low.shape[3])


def image_edges(image, group):
    start, slices = group
    part = image[start : start + slices]
    _, _, frames, rows, columns = part.shape
    flat = (slices, 2, frames * columns)
    return share_edges(
        part[:, :, 0], part[:, :, frames - 1],
        part[:, :, :, 0].reshape(flat), part[:, :, :, rows - 1].reshape(flat),
    )


def return_edges(part_below, part_above, part_left, part_right, columns):
    lower = lax.ppermute(part_left, "row", along("row", -1))
    upper = lax.ppermute(part_right, "row", along("row", 1))
    from_above = lax.ppermute(part_below, "af", along("af", -1))
    from_below = lax.ppermute(part_above, "af", along("af", 1))
    corner_below, corner_above = corners_along(upper, lower, columns)
    return from_below, from_above, upper, lower, corner_below, corner_above


def image_kernel(
    main, from_below, from_above, upper, lower, corner_below, corner_above,
    table, note, out, image,
):
    slices, frames, rows, twice = main.shape
    columns = twice // 2
    row = lax.broadcasted_iota(jnp.int32, (rows, columns), 0)
    for s in range(slices):
        tops = upper[s].astype(jnp.float32)
        ends = lower[s].astype(jnp.float32)
        corners = {
            0: corner_below[s].astype(jnp.float32),
            frames - 1: corner_above[s].astype(jnp.float32),
        }
        for f in range(frames):
            at = slice((f + 1) * columns, (f + 2) * columns)
            for o in range(2):
                here = slice(o * columns, (o + 1) * columns)
                value = main[s, f, :, here]
                if f == 0:
                    value = value + from_below[s, o].astype(jnp.float32)
                if f == frames - 1:
                    value = value + from_above[s, o].astype(jnp.float32)
                top, end = tops[o : o + 1, at], ends[o : o + 1, at]
                if f in corners:
                    top = top + corners[f][o : o + 1]
                    end = end + corners[f][2 + o : 3 + o]
                value = value + jnp.where(row == 0, top, 0.0)
                value = value + jnp.where(row == rows - 1, end, 0.0)
                start = (s * frames + f) * rows
                image[start : start + rows, here] = value.astype(jnp.bfloat16)
    size = slices * frames * rows
    for start in range(0, size, 512):
        stop = min(start + 512, size)
        out[:, start:stop] = lax.dot_general(
            table[...], image[start:stop, :], NT, preferred_element_type=jnp.float32
        ).astype(jnp.bfloat16)
    rest = out.shape[1] - size
    if rest:
        lane = lax.broadcasted_iota(jnp.int32, (out.shape[0], rest), 1)
        out[:, size:] = jnp.where(lane == 0, note[0, 0], 0.0).astype(jnp.bfloat16)


def image_to_hybrid(main, added, table, note, lanes):
    slices, frames, rows, twice = main.shape
    return pl.pallas_call(
        image_kernel,
        in_specs=[pl.BlockSpec(memory_space=pltpu.VMEM)] * (2 + EDGES)
        + [pl.BlockSpec(memory_space=pltpu.SMEM)],
        out_shape=jax.ShapeDtypeStruct((twice, lanes), jnp.bfloat16),
        scratch_shapes=[pltpu.VMEM((slices * frames * rows, twice), jnp.bfloat16)],
        compiler_params=pltpu.CompilerParams(vmem_limit_bytes=VMEM),
        cost_estimate=expected(slices / 2),
        name="image_to_hybrid",
    )(main, *added, table, note)


def grad_image_kernel(hybrid, table, out, low, high, first, last, sums):
    slices, _, frames, rows, columns = out.shape
    sums[...] = jnp.zeros_like(sums)
    for s in range(slices):
        size = frames * rows
        start = s * size // 128 * 128
        stop = -(-(s + 1) * size // 128) * 128
        value = lax.dot_general(
            hybrid[:, start:stop], table[...], TN, preferred_element_type=jnp.float32
        ).astype(jnp.bfloat16)
        for c in range(2):
            tops, ends = [], []
            for f in range(frames):
                at = s * size + f * rows - start
                piece = value[at : at + rows, c * columns : (c + 1) * columns]
                out[s, c, f] = piece
                if f == 0:
                    low[s, c] = piece
                if f == frames - 1:
                    high[s, c] = piece
                wide = piece.astype(jnp.float32)
                sums[c : c + 1, :] += jnp.sum(wide, axis=0, keepdims=True)
                tops.append(wide[0:1])
                ends.append(wide[rows - 1 :])
            first[s, c : c + 1, :] = jnp.concatenate(tops, axis=1)
            last[s, c : c + 1, :] = jnp.concatenate(ends, axis=1)


def hybrid_to_grad(hybrid, table, shape):
    slices, channels, frames, rows, columns = shape
    edge_frame = jax.ShapeDtypeStruct((slices, channels, rows, columns), jnp.bfloat16)
    edge_row = jax.ShapeDtypeStruct((slices, channels, frames * columns), jnp.float32)
    return pl.pallas_call(
        grad_image_kernel,
        out_shape=[
            jax.ShapeDtypeStruct(shape, jnp.bfloat16),
            edge_frame,
            edge_frame,
            edge_row,
            edge_row,
            jax.ShapeDtypeStruct((2, columns), jnp.float32),
        ],
        compiler_params=pltpu.CompilerParams(vmem_limit_bytes=VMEM),
        cost_estimate=expected(slices / 2),
        name="hybrid_to_grad",
    )(hybrid, table)


def chunk_transpose(pieces, low_half, even):
    a, c, b, d = pieces
    a, b = (
        jnp.where(low_half, a, pltpu.roll(b, 64, axis=1)),
        jnp.where(low_half, pltpu.roll(a, 64, axis=1), b),
    )
    c, d = (
        jnp.where(low_half, c, pltpu.roll(d, 64, axis=1)),
        jnp.where(low_half, pltpu.roll(c, 64, axis=1), d),
    )
    return (
        jnp.where(even, a, pltpu.roll(c, 32, axis=1)),
        jnp.where(even, pltpu.roll(a, 96, axis=1), c),
        jnp.where(even, b, pltpu.roll(d, 32, axis=1)),
        jnp.where(even, pltpu.roll(b, 96, axis=1), d),
    )


def kspace_slice(
    k, index, frames_here, n_af, measured, target, sampled, share, scale, table,
    spectrum, grads, loss_lanes,
):
    frames = n_af * frames_here
    twice = table.shape[0]
    first = index * frames_here
    size = frames * 8
    here = spectrum[pl.ds(first, frames_here)].reshape(size, twice).astype(jnp.bfloat16)
    kspace = jnp.dot(here, table[...], preferred_element_type=jnp.float32)

    def place(t):
        return (t % frames_here) * n_af + t // frames_here

    filled = []
    for t in range(frames):
        mask = sampled[t]
        filled.append(mask * measured[k, t] + (1.0 - mask) * kspace[place(t) * 8 : place(t) * 8 + 8])
    slopes = []
    for t in range(frames):
        mask = sampled[t]
        near = range(max(t - 2, 0), min(t + 3, frames))
        shared = sum(share[t, s] * filled[s] for s in near)
        differ = mask * measured[k, t] + (1.0 - mask) * shared - target[k, t]
        square = differ * differ + 1.0
        inverse = lax.rsqrt(square)
        loss_lanes[...] += (1.0 - mask) * (square * inverse - 1.0)
        slopes.append((1.0 - mask) * differ * inverse * scale[0, 0])
    for s in range(frames):
        near = range(max(s - 2, 0), min(s + 3, frames))
        grad = sum(share[t, s] * slopes[t] for t in near)
        grads[k, place(s) * 8 : place(s) * 8 + 8, :] = (1.0 - sampled[s]) * grad
    grad = grads[k]
    high = grad.astype(jnp.bfloat16)
    low = (grad - high.astype(jnp.float32)).astype(jnp.bfloat16)
    back = lax.dot_general(high, table[...], NT, preferred_element_type=jnp.float32)
    back += lax.dot_general(low, table[...], NT, preferred_element_type=jnp.float32)
    spectrum[pl.ds(first, frames_here)] = back.reshape(frames_here, n_af, 8, twice)


def kspace_kernel(
    frames_here, received, measured, target, sampled, share, scale, table, out, loss,
    spectrum, grads, loss_lanes,
):
    groups, _, lanes = received.shape
    pairs, n_af, _, twice = spectrum.shape
    rows = twice // 2
    n_row = groups // n_af
    step = pl.program_id(0)
    lane = lax.broadcasted_iota(jnp.int32, (SIDE, 128), 1)
    low_half = lane < 64
    even = lane % 64 < 32

    @pl.when(step == 0)
    def _():
        loss_lanes[...] = jnp.zeros_like(loss_lanes)
        def gather(af, carry):
            for tile in range(lanes // 128):
                for h in range(n_row // 4):
                    source = [
                        received[af * n_row + h * 4 + m, :, tile * 128 : (tile + 1) * 128]
                        for m in range(4)
                    ]
                    moved = chunk_transpose(source, low_half, even)
                    for k in range(4):
                        if tile * 4 + k < pairs:
                            wide = moved[k].astype(jnp.float32)
                            for c in range(2):
                                at = c * rows + h * 128
                                spectrum[tile * 4 + k, af, :, at : at + 128] = wide[
                                    c * 8 : (c + 1) * 8
                                ]
            return carry

        lax.fori_loop(0, n_af, gather, 0)

    each = measured.shape[0]
    for k in range(each):
        kspace_slice(
            k, step * each + k, frames_here, n_af, measured, target, sampled, share, scale, table,
            spectrum, grads, loss_lanes,
        )

    @pl.when(step == pl.num_programs(0) - 1)
    def _():
        loss[...] = loss_lanes[...]

        def scatter(af, carry):
            for tile in range(lanes // 128):
                for h in range(n_row // 4):
                    source = []
                    for k in range(4):
                        pair = min(tile * 4 + k, pairs - 1)
                        both = [
                            spectrum[pair, af, :, c * rows + h * 128 : c * rows + h * 128 + 128]
                            for c in range(2)
                        ]
                        source.append(jnp.concatenate(both, axis=0).astype(jnp.bfloat16))
                    moved = chunk_transpose(source, low_half, even)
                    for m in range(4):
                        out[af * n_row + h * 4 + m, :, tile * 128 : (tile + 1) * 128] = moved[m]
            return carry

        lax.fori_loop(0, n_af, scatter, 0)


def kspace_step(received, measured, target, sampled, share, scale, table, frames_here, group):
    _, frames, lines, twice = measured.shape
    first, slices = group
    n_af = frames // frames_here
    each = 2 if slices % 2 == 0 and first % 2 == 0 else 1

    def some(shape):
        start = first // each
        return pl.BlockSpec((each,) + tuple(shape[1:]), lambda s: (s + start, 0, 0, 0))

    smem = pl.BlockSpec(memory_space=pltpu.SMEM)
    return pl.pallas_call(
        functools.partial(kspace_kernel, frames_here),
        grid=(slices // each,),
        in_specs=[
            whole(received.shape),
            some(measured.shape),
            some(target.shape),
            whole(sampled.shape),
            smem,
            smem,
            whole(table.shape),
        ],
        out_specs=[whole(received.shape), whole((lines, twice))],
        out_shape=[
            jax.ShapeDtypeStruct(received.shape, jnp.bfloat16),
            jax.ShapeDtypeStruct((lines, twice), jnp.float32),
        ],
        scratch_shapes=[
            pltpu.VMEM((slices * frames_here, n_af, lines, twice), jnp.float32),
            pltpu.VMEM((each, frames * lines, twice), jnp.float32),
            pltpu.VMEM((lines, twice), jnp.float32),
        ],
        compiler_params=pltpu.CompilerParams(vmem_limit_bytes=VMEM),
        cost_estimate=expected(3 * slices),
        name="kspace",
    )(received, measured, target, sampled, share, scale, table)


def middle_plain(main, added, measured, target, sampled, share, table_y, table_x):
    highest = lax.Precision.HIGHEST
    slices, frames_here, rows_here, twice = main.shape
    count = lax.psum(jnp.sum(1.0 - sampled) * (2.0 * slices * measured.shape[3] / 2), AXES)
    columns = twice // 2
    frames, lines = measured.shape[1:3]
    rows = measured.shape[3] // 2
    table_y = jnp.asarray(table_y, jnp.bfloat16)
    table_x = jnp.asarray(table_x, jnp.bfloat16)
    image = main.reshape(slices, frames_here, rows_here, 2, columns)
    below, above, upper, lower, *corners = (one.astype(jnp.float32) for one in added)
    image = image.at[:, 0].add(below.transpose(0, 2, 1, 3))
    image = image.at[:, frames_here - 1].add(above.transpose(0, 2, 1, 3))
    for at, line in ((0, upper), (rows_here - 1, lower)):
        line = line[:, :, columns:-columns].reshape(slices, 2, frames_here, columns)
        image = image.at[:, :, at].add(line.transpose(0, 2, 1, 3))
    for f, corner in ((0, corners[0]), (frames_here - 1, corners[1])):
        image = image.at[:, f, 0].add(corner[:, 0:2])
        image = image.at[:, f, rows_here - 1].add(corner[:, 2:4])
    flat = image.reshape(slices, frames_here, rows_here, twice).astype(jnp.bfloat16)
    hybrid = jnp.dot(flat, table_y, preferred_element_type=jnp.float32).astype(jnp.bfloat16)
    hybrid = hybrid.reshape(slices, frames_here, rows_here, 2, columns)
    part = lax.all_to_all(hybrid, "af", split_axis=4, concat_axis=1, tiled=True)
    spread = lax.all_to_all(part, "row", split_axis=4, concat_axis=2, tiled=True)
    spectrum = jnp.transpose(spread, (0, 1, 4, 3, 2)).reshape(slices, frames, lines, 2 * rows)
    kspace = jnp.dot(spectrum, table_x, preferred_element_type=jnp.float32)
    mask = sampled[None, :, :, None]
    filled = mask * measured + (1.0 - mask) * kspace
    shared = jnp.einsum("ts,bslk->btlk", share, filled, precision=highest)
    differ = mask * measured + (1.0 - mask) * shared - target
    root = jnp.sqrt(differ * differ + 1.0)
    loss = jnp.sum((1.0 - mask) * (root - 1.0))
    slope = (1.0 - mask) * differ / root / count
    grad = (1.0 - mask) * jnp.einsum("ts,btlk->bslk", share, slope, precision=highest)
    back = jnp.dot(grad, table_x.T.astype(jnp.float32), precision=highest).astype(jnp.bfloat16)
    back = jnp.transpose(back.reshape(slices, frames, lines, 2, rows), (0, 1, 4, 3, 2))
    part = lax.all_to_all(back, "row", split_axis=2, concat_axis=4, tiled=True)
    whole_rows = lax.all_to_all(part, "af", split_axis=1, concat_axis=4, tiled=True)
    grad = jnp.dot(
        whole_rows.reshape(slices, frames_here, rows_here, twice),
        table_y.T,
        preferred_element_type=jnp.float32,
    ).reshape(slices, frames_here, rows_here, 2, columns)
    grad = jnp.transpose(grad, (0, 3, 1, 2, 4)).astype(jnp.bfloat16)
    return loss, count, grad, jnp.sum(grad.astype(jnp.float32), axis=(0, 2, 3, 4))


def update_kernel(total, *refs):
    ins, outs = refs[:12], refs[12:]
    taps, width = ins[0].shape
    turned = total[0:width, :].T

    def step(kind, at, grad):
        master, first, second, smooth = (one[at] for one in ins[kind::3])
        rate = (rate_in, rate_out, rate_bias)[kind]
        first, second, master = adam_step(master, grad, first, second, rate)
        average = average_keep * smooth + (1.0 - average_keep) * master
        for out, value in zip(outs[kind::3], (first, second, master, average, master)):
            out[at] = value.astype(out.dtype)

    step(0, ..., turned[0:taps, :])
    for tap in range(ins[1].shape[0]):
        start = PACKED // 2 + 2 * tap
        step(1, tap, turned[start : start + 2, :])
    step(2, (slice(0, 1), slice(0, width)), turned[54:55, :])
    step(2, (slice(0, 1), slice(width, width + 2)), total[width : width + 1, 1:3])


def update(total, weights, firsts, seconds, smooths):
    arrays = [*weights, *firsts, *seconds, *smooths]
    turn = {1: lambda one: one.reshape(1, -1), 2: jnp.transpose, 3: lambda one: one}
    arrays = [turn[one.ndim](one) for one in arrays]
    kinds = [jnp.float32] * 4 + [jnp.bfloat16]
    outs = pl.pallas_call(
        update_kernel,
        out_shape=[jax.ShapeDtypeStruct(one.shape, kind) for kind in kinds for one in arrays[:3]],
        name="update",
    )(total, *arrays)
    back = (jnp.transpose, lambda one: one, lambda one: one.reshape(-1))
    return [back[k % 3](one) for k, one in enumerate(outs)]


def packed_extras(width, loss, sums):
    row = jnp.concatenate([loss.reshape(1), sums])
    return jnp.pad(row.reshape(1, 3), ((width, 7), (0, PACKED - 3)))


def middle_fast(
    main, added, measured, target, sampled, share, table_y, table_x, between, after
):
    devices = lax.axis_size("af") * lax.axis_size("row")
    slices, frames_here, rows, twice = main.shape
    lines, readout = measured.shape[2:]
    size = slices * frames_here * rows
    order = np.arange(twice).reshape(2, devices, lines).transpose(1, 0, 2).reshape(-1)
    permuted = jnp.asarray(np.ascontiguousarray(table_y[:, order].T), jnp.bfloat16)
    mask = jnp.broadcast_to(sampled[:, :, None], sampled.shape + (readout,))
    note = jnp.sum(1.0 - sampled).reshape(1, 1)
    lanes = (size // 128 + 1) * 128
    hybrid = image_to_hybrid(main, added, permuted, note, lanes)
    received = lax.all_to_all(
        hybrid.reshape(devices, 2 * lines, lanes), AXES, 0, 0, tiled=True
    )
    first = between(hybrid)
    received, first = lax.optimization_barrier((received, first))
    notes = received[:, 0, size].astype(jnp.float32)
    count = jnp.sum(notes) * (1.0 * slices * readout)
    back, loss = kspace_step(
        received, measured, target, mask, share, (1.0 / count).reshape(1, 1),
        jnp.asarray(table_x, jnp.bfloat16), frames_here, (0, slices),
    )
    returned = lax.all_to_all(back, AXES, 0, 0, tiled=True)
    second = after(back, first)
    returned, second = lax.optimization_barrier((returned, second))
    shape = (slices, 2, frames_here, rows, twice // 2)
    grad, *grad_edge, sums = hybrid_to_grad(returned.reshape(twice, lanes), permuted, shape)
    return jnp.sum(loss), count, grad, grad_edge, jnp.sum(sums, axis=1), second


def train_step(
    image_in, measured, target, sampled, share, table_y, table_x, w_in, w_out, w_back, bias_out
):
    slices, _, frames_here, rows, columns = image_in.shape
    frames, lines = measured.shape[1:3]
    cut = (slices + 1) // 2
    groups = [(0, cut), (cut, slices - cut)]
    edges = image_edges(image_in, (0, slices))
    main, *part = conv_forward(image_in, edges, (0, slices), w_in, w_out, bias_out)
    added = return_edges(*part, columns)

    def again(group, after, kept=()):
        held, _ = lax.optimization_barrier((w_in.T, after))
        return hidden_again(image_in, edges, group, held, kept)

    fits = rows == 32 and lines == 8 and lax.axis_size("row") % 4 == 0
    fits = fits and frames * lines <= 256
    if fits:
        loss, count, grad, grad_edge, sums, kept = middle_fast(
            main, added, measured, target, sampled, share, table_y, table_x,
            functools.partial(again, groups[0]), functools.partial(again, groups[1]),
        )
    else:
        loss, count, grad, sums = middle_plain(
            main, added, measured, target, sampled, share, table_y, table_x
        )
        flat = (slices, 2, frames_here * columns)
        grad_edge = (
            grad[:, :, 0], grad[:, :, frames_here - 1],
            grad[:, :, :, 0].reshape(flat), grad[:, :, :, rows - 1].reshape(flat),
        )
        kept = None
    around = share_edges(*grad_edge)
    total = packed_extras(w_in.shape[0] // BLOCK, loss, sums)
    if kept is not None:
        return count, conv_backward(image_in, edges, grad, around, *kept, w_back, total)
    for first, size in groups:
        own, *sides = (one[first : first + size] for one in (image_in, *edges, grad, *around))
        held, _ = lax.optimization_barrier((w_in.T, total))
        kept = hidden_again(own, sides[:EDGES], (0, size), held)
        total = conv_backward(
            own, sides[:EDGES], sides[EDGES], sides[EDGES + 1 :], *kept, w_back, total
        )
    return count, total


def on_device(
    image_in, measured, target, line_mask, window_half, in_kernel, out_kernel, biases,
    in_moment, out_moment, bias_moment, in_square, out_square, bias_square,
    in_smooth, out_smooth, bias_smooth,
):
    slices, _, frames_here, rows_here, columns = image_in.shape
    frames = measured.shape[1]
    width = in_kernel.shape[0]
    rows = rows_here * lax.axis_size("row")
    table_y = dft_table(columns)
    table_x = dft_table(rows)
    share = share_matrix(window_half, frames)
    sampled = line_mask.astype(jnp.float32)
    w_in = conv_in_weights(in_kernel, biases[:width])
    w_out = conv_out_weights(out_kernel)
    w_back = conv_back_weights(out_kernel)

    count, total = train_step(
        image_in, measured, target, sampled, share, table_y, table_x,
        w_in, w_out, w_back, biases[width:],
    )
    total = sum_over(sum_over(total, "row"), "af")
    outs = update(
        total,
        (in_kernel, out_kernel, biases),
        (in_moment, out_moment, bias_moment),
        (in_square, out_square, bias_square),
        (in_smooth, out_smooth, bias_smooth),
    )
    return (total[width, 0], count, *outs)


def solution(mesh):
    in_specs = (
        P(None, None, "af", "row", None),
        P(None, None, ("af", "row"), None),
        P(None, None, ("af", "row"), None),
        P(None, ("af", "row")),
    ) + (P(),) * 13
    return jax.shard_map(
        on_device, mesh=mesh, in_specs=in_specs, out_specs=(P(),) * 17, check_vma=False
    )
```

```python
import functools
import math

import jax
import jax.numpy as jnp
import numpy as np
from jax import lax
from jax.experimental import pallas as pl
from jax.experimental.pallas import tpu as pltpu
from jax.sharding import PartitionSpec as P

STEP = 5
AXES = ("af", "row")
BLOCK = 4
WIN = 8
SIDE = 16
DEPTH = 9 * SIDE
ONES_ROW = BLOCK + 2
PACKED = 128
EDGES = 6
BIAS_LANE = WIN - 1
VMEM = 60 * 2**20
GELU = math.sqrt(2.0 / math.pi)
CUBE = 0.044715

beta_first = 0.5
beta_second = 0.5
rate_in = 0.2
rate_out = 0.04
rate_bias = 0.3
decay_weight = 0.01
average_keep = 0.9
epsilon = 1e-08

NT = (((1,), (1,)), ((), ()))
TN = (((0,), (0,)), ((), ()))


def dft_table(length):
    index = np.arange(length)
    phase = (index[:, None] * index[None, :] % length) * (2.0 * math.pi / length)
    cosine = np.cos(phase) / math.sqrt(length)
    sine = np.sin(phase) / math.sqrt(length)
    upper = np.concatenate([cosine, -sine], axis=1)
    lower = np.concatenate([sine, cosine], axis=1)
    return np.concatenate([upper, lower], axis=0).astype(np.float32)


def share_matrix(window_half, frames):
    index = jnp.arange(frames, dtype=jnp.int32)
    inside = (jnp.abs(index[None, :] - index[:, None]) <= window_half[:, None]).astype(jnp.float32)
    return inside / jnp.sum(inside, axis=1, keepdims=True)


def adam_step(master, grad, first, second, rate):
    first_new = beta_first * first + (1.0 - beta_first) * grad
    second_new = beta_second * second + (1.0 - beta_second) * grad * grad
    first_hat = first_new / (1.0 - beta_first**STEP)
    second_hat = second_new / (1.0 - beta_second**STEP)
    master_new = master - rate * (
        first_hat / (jnp.sqrt(second_hat) + epsilon) + decay_weight * master
    )
    return (first_new, second_new, master_new)


def conv_in_weights(kernel, bias):
    width = kernel.shape[0]
    taps = kernel.astype(jnp.bfloat16).astype(jnp.float32).reshape(width, 2, 3, 3, 3)
    rows = []
    for j in range(BLOCK):
        row = jnp.pad(taps, ((0, 0), (0, 0), (0, 0), (j, WIN - 3 - j), (0, 0)))
        rows.append(row.transpose(0, 2, 4, 1, 3))
    spread = jnp.stack(rows)
    high = lax.reduce_precision(bias, 8, 7)
    rest = bias - high
    middle = lax.reduce_precision(rest, 8, 7)
    parts = jnp.stack([high, middle, rest - middle], axis=1)
    spread = spread.at[:, :, :, 0, 0, ONES_ROW].set(jnp.broadcast_to(parts, (BLOCK, width, 3)))
    return 0.5 * spread.reshape(BLOCK * width, DEPTH)


def conv_out_weights(kernel):
    width = kernel.shape[2]
    taps = kernel.astype(jnp.bfloat16).reshape(3, 3, 3, 2, width)[:, ::-1]
    columns = []
    for j in range(BLOCK):
        column = jnp.pad(taps, ((0, 0), (j, WIN - 3 - j), (0, 0), (0, 0), (0, 0)))
        columns.append(column.transpose(0, 2, 3, 1, 4))
    return jnp.stack(columns, axis=4).reshape(DEPTH, BLOCK * width)


def conv_back_weights(kernel):
    width = kernel.shape[2]
    taps = kernel.astype(jnp.bfloat16).reshape(3, 3, 3, 2, width)[::-1, ::-1, ::-1]
    rows = []
    for j in range(BLOCK):
        row = jnp.pad(taps, ((0, 0), (j, WIN - 3 - j), (0, 0), (0, 0), (0, 0)))
        rows.append(row.transpose(0, 2, 3, 1, 4))
    return 0.5 * jnp.stack(rows, axis=4).reshape(DEPTH, BLOCK * width)


def pick_table():
    table = np.zeros((2, 256, PACKED), np.float32)
    for a, b, e, c in np.ndindex(3, 3, 3, 2):
        lane = ((a * 3 + e) * 2 + c) * WIN + b
        table[0, lane, 27 * c + 9 * a + 3 * b + e] = 1.0
        tap = 9 * (2 - a) + 3 * (2 - b) + 2 - e
        table[1, lane, PACKED // 2 + 2 * tap + c] = 1.0
    table[0, BIAS_LANE, 54] = 1.0
    return jnp.asarray(table, jnp.bfloat16)


def load_volume(volume, own, below, above, left, right, corner_below, corner_above):
    _, channels, frames, rows, columns = own.shape
    lanes = (frames + 2) * columns
    for c in range(channels):
        volume[c, rows + 8 : rows + 16, :] = jnp.zeros((8, lanes), jnp.float32)
        for t in range(frames + 2):
            if t == 0:
                piece = below[0, c]
            elif t == frames + 1:
                piece = above[0, c]
            else:
                piece = own[0, c, t - 1]
            volume[c, 8 : 8 + rows, t * columns : (t + 1) * columns] = piece.astype(jnp.float32)
    low = corner_below[0].astype(jnp.float32)
    high = corner_above[0].astype(jnp.float32)
    for side, at, line in ((0, 7, left), (1, rows + 8, right)):
        middle = line[0].astype(jnp.float32)
        for c in range(channels):
            k = 2 * side + c
            volume[c, at : at + 1, 0:columns] = low[k : k + 1]
            volume[c, at : at + 1, columns : lanes - columns] = middle[c : c + 1]
            volume[c, at : at + 1, lanes - columns :] = high[k : k + 1]


def build_windows(volume, windows, columns, ones):
    blocks, _, lanes = windows.shape
    column = lax.broadcasted_iota(jnp.int32, (SIDE, columns), 1)
    row = lax.broadcasted_iota(jnp.int32, (SIDE, columns), 0)
    zero = jnp.zeros((SIDE, columns), jnp.bfloat16)
    for block in range(blocks):
        for t in range(lanes // columns):
            here = slice(t * columns, (t + 1) * columns)
            start = 7 + BLOCK * block
            window = jnp.concatenate(
                [volume[c, start : start + WIN, here] for c in range(2)], axis=0
            ).astype(jnp.bfloat16)
            for e in range(3):
                shifted = window
                if e != 1:
                    shifted = pltpu.roll(window, (1 - e) % columns, axis=1)
                    shifted = jnp.where(column == (0 if e == 0 else columns - 1), zero, shifted)
                if ones and e == 0:
                    shifted = jnp.where(row == ONES_ROW, zero + 1.0, shifted)
                windows[block, e * SIDE : (e + 1) * SIDE, here] = shifted


def forward_kernel(
    own, *refs,
):
    edges, refs = refs[:EDGES], refs[EDGES:]
    (
    w_in, w_out, bias_out,
    main, part_below, part_above, part_left, part_right,
    volume, windows, total, hidden, mixed, spread,
    ) = refs
    _, _, frames, rows, columns = own.shape
    blocks = windows.shape[0]
    load_volume(volume, own, *edges)
    build_windows(volume, windows, columns, True)
    column = lax.broadcasted_iota(jnp.int32, (SIDE, columns), 1)

    def step(block, carry):
        for f in range(frames):
            here = slice(f * columns, (f + 1) * columns)
            patch = jnp.concatenate(
                [windows[block, :, (f + a) * columns : (f + a + 1) * columns] for a in range(3)],
                axis=0,
            )
            half = jnp.dot(w_in[...], patch, preferred_element_type=jnp.float32)
            t = jnp.tanh(half * (2.0 * GELU + (8.0 * GELU * CUBE) * (half * half)))
            hidden[:, here] = (half + half * t).astype(jnp.bfloat16)
        for f in range(frames):
            here = slice(f * columns, (f + 1) * columns)
            mixed[f] = jnp.dot(w_out[...], hidden[:, here], preferred_element_type=jnp.float32)
        for t in range(frames + 2):
            window = None
            for e in range(3):
                summed = None
                for a in range(3):
                    f = t - 2 + a
                    if 0 <= f < frames:
                        start = (a * 3 + e) * SIDE
                        piece = mixed[f, start : start + SIDE, :]
                        summed = piece if summed is None else summed + piece
                if e != 1:
                    summed = pltpu.roll(summed, (1 - e) % columns, axis=1)
                    summed = jnp.where(column == (0 if e == 0 else columns - 1), 0.0, summed)
                window = summed if window is None else window + summed
            spread[block, :, t * columns : (t + 1) * columns] = window
        return carry

    lax.fori_loop(0, blocks, step, 0, unroll=True)
    total[...] = jnp.zeros_like(total)
    for block in range(blocks):
        for o in range(2):
            start = 7 + BLOCK * block
            total[o, start : start + WIN, :] = (
                total[o, start : start + WIN, :] + spread[block, o * WIN : (o + 1) * WIN, :]
            )
    for o in range(2):
        for t in range(frames + 2):
            here = total[o, 8 : 8 + rows, t * columns : (t + 1) * columns]
            if t == 0:
                part_below[0, o] = here.astype(jnp.bfloat16)
            elif t == frames + 1:
                part_above[0, o] = here.astype(jnp.bfloat16)
            else:
                base = volume[o, 8 : 8 + rows, t * columns : (t + 1) * columns] + bias_out[bias_out.shape[0] - 2 + o]
                main[0, t - 1, :, o * columns : (o + 1) * columns] = base + here
    for at, out in ((7, part_left), (8 + rows, part_right)):
        both = [total[o, at : at + 1, :] for o in range(2)]
        out[0] = jnp.concatenate(both, axis=0).astype(jnp.bfloat16)


def patches(source, block, frames, columns):
    return jnp.concatenate(
        [source[block, :, a * columns : (a + frames) * columns] for a in range(3)], axis=0
    )


def hidden_kernel(own, *refs):
    edges, (w_in, *_, hidden, slopes, volume, windows) = refs[:EDGES], refs[EDGES:]
    _, _, frames, rows, columns = own.shape
    load_volume(volume, own, *edges)
    build_windows(volume, windows, columns, True)

    def step(block, carry):
        patch = patches(windows, block, frames, columns)
        for f in range(frames):
            here = slice(f * columns, (f + 1) * columns)
            half = lax.dot_general(
                patch[:, here], w_in[...], TN, preferred_element_type=jnp.float32
            )
            u = half * half
            t = jnp.tanh(half * (2.0 * GELU + (8.0 * GELU * CUBE) * u))
            up = 1.0 + t
            hidden[0, block, here, :] = (half * up).astype(jnp.bfloat16)
            slope = half * (2.0 * GELU + (24.0 * GELU * CUBE) * u)
            slopes[0, block, here, :] = (up + (up * (1.0 - t)) * slope).astype(jnp.bfloat16)
        return carry

    lax.fori_loop(0, windows.shape[0], step, 0, unroll=True)


def backward_kernel(
    own, *refs,
):
    edges, grad, grad_edges = refs[:EDGES], refs[EDGES], refs[EDGES + 1 : 2 * EDGES + 1]
    (
        hidden, slopes, w_back, pick, loss, sums, out,
        volume, windows, grad_windows, grads, sum_in, sum_out,
    ) = refs[2 * EDGES + 1 :]
    _, _, frames, rows, columns = own.shape

    part = pl.program_id(1)

    @pl.when((pl.program_id(0) == 0) & (part == 0))
    def _():
        sum_in[...] = jnp.zeros_like(sum_in)
        sum_out[...] = jnp.zeros_like(sum_out)

    @pl.when(part == 0)
    def _():
        load_volume(volume, own, *edges)
        build_windows(volume, windows, columns, True)
        load_volume(volume, grad, *grad_edges)
        build_windows(volume, grad_windows, columns, False)

    blocks = hidden.shape[1]

    def step(at):
        block = part * blocks + at
        patch = patches(windows, block, frames, columns)
        grad_patch = patches(grad_windows, block, frames, columns)
        for f in range(frames):
            here = slice(f * columns, (f + 1) * columns)
            gh = lax.dot_general(
                grad_patch[:, here], w_back[...], TN, preferred_element_type=jnp.float32
            )
            grads[here, :] = (slopes[0, at, here, :].astype(jnp.float32) * gh).astype(
                jnp.bfloat16
            )
        sum_in[:DEPTH, :] += jnp.dot(patch, grads[...], preferred_element_type=jnp.float32)
        sum_out[:DEPTH, :] += jnp.dot(
            grad_patch, hidden[0, at], preferred_element_type=jnp.float32
        )

    for at in range(blocks):
        step(at)

    @pl.when((pl.program_id(0) == pl.num_programs(0) - 1) & (part == pl.num_programs(1) - 1))
    def _():
        width = sum_in.shape[1] // BLOCK
        lanes = sum_in.shape[0]
        lane = lax.broadcasted_iota(jnp.int32, (width, lanes), 1)
        picked = jnp.zeros((width, pick.shape[2]), jnp.float32)
        for index, source in enumerate((sum_in[...].T, sum_out[...].T)):
            folded = source[0:width, :]
            bias = folded
            for j in range(1, BLOCK):
                piece = source[j * width : (j + 1) * width, :]
                folded = folded + pltpu.roll(piece, lanes - j, axis=1)
                bias = bias + piece
            if index == 0:
                moved = pltpu.roll(bias, BIAS_LANE - ONES_ROW, axis=1)
                folded = jnp.where(lane == BIAS_LANE, moved, folded)
            for _ in range(3):
                piece = folded.astype(jnp.bfloat16)
                folded = folded - piece.astype(jnp.float32)
                picked = picked + jnp.dot(piece, pick[index], preferred_element_type=jnp.float32)
        out[0:width, :] = picked
        spot = lax.broadcasted_iota(jnp.int32, (8, PACKED), 1)
        both = jnp.sum(sums[...], axis=1, keepdims=True)
        values = (jnp.sum(loss[...], axis=(0, 1), keepdims=True), both[0:1], both[1:2])
        row = jnp.zeros((8, PACKED), jnp.float32)
        for k, value in enumerate(values):
            row = jnp.where(spot == k, value, row)
        out[width:, :] = row


def whole(shape):
    return pl.BlockSpec(tuple(shape), lambda s: (0,) * len(shape))


def a_slice(shape, first=0):
    rest = (0,) * (len(shape) - 1)
    return pl.BlockSpec((1,) + tuple(shape[1:]), lambda s: (s + first,) + rest)


def expected(microseconds):
    return pl.CostEstimate(
        flops=int(microseconds * 1.15e9), bytes_accessed=0, transcendentals=0
    )


def conv_scratch(frames, rows, columns):
    lanes = (frames + 2) * columns
    return (
        pltpu.VMEM((2, rows + 16, lanes), jnp.float32),
        pltpu.VMEM((rows // BLOCK, 3 * SIDE, lanes), jnp.bfloat16),
    )


def conv_forward(own, edges, group, w_in, w_out, bias_out):
    _, _, frames, rows, columns = own.shape
    first, slices = group
    lanes = (frames + 2) * columns
    span = w_in.shape[0]
    volume, windows = conv_scratch(frames, rows, columns)
    out_shape = [
        jax.ShapeDtypeStruct((slices, frames, rows, 2 * columns), jnp.float32),
        jax.ShapeDtypeStruct((slices, 2, rows, columns), jnp.bfloat16),
        jax.ShapeDtypeStruct((slices, 2, rows, columns), jnp.bfloat16),
        jax.ShapeDtypeStruct((slices, 2, lanes), jnp.bfloat16),
        jax.ShapeDtypeStruct((slices, 2, lanes), jnp.bfloat16),
    ]
    return pl.pallas_call(
        forward_kernel,
        grid=(slices,),
        in_specs=[a_slice(own.shape, first)]
        + [a_slice(one.shape) for one in edges]
        + [whole(w_in.shape), whole(w_out.shape), pl.BlockSpec(memory_space=pltpu.SMEM)],
        out_specs=[a_slice(one.shape) for one in out_shape],
        out_shape=out_shape,
        scratch_shapes=[
            volume,
            windows,
            volume,
            pltpu.VMEM((span, frames * columns), jnp.bfloat16),
            pltpu.VMEM((frames, DEPTH, columns), jnp.float32),
            pltpu.VMEM((rows // BLOCK, SIDE, lanes), jnp.float32),
        ],
        compiler_params=pltpu.CompilerParams(vmem_limit_bytes=VMEM),
        cost_estimate=expected(6 * slices),
        name="conv_forward",
    )(own, *edges, w_in, w_out, bias_out)


def hidden_again(own, edges, group, w_in, kept=()):
    _, _, frames, rows, columns = own.shape
    first, slices = group
    volume, windows = conv_scratch(frames, rows, columns)
    shape = (own.shape[0], rows // BLOCK, frames * columns, w_in.shape[1])
    return pl.pallas_call(
        hidden_kernel,
        grid=(slices,),
        in_specs=[a_slice(own.shape, first)]
        + [a_slice(one.shape, first) for one in edges]
        + [whole(w_in.shape)]
        + [pl.BlockSpec(memory_space=pl.ANY)] * len(kept),
        out_specs=[a_slice(shape, first)] * 2,
        out_shape=[jax.ShapeDtypeStruct(shape, jnp.bfloat16)] * 2,
        input_output_aliases={2 + EDGES + k: k for k in range(len(kept))},
        scratch_shapes=[volume, windows],
        compiler_params=pltpu.CompilerParams(vmem_limit_bytes=VMEM),
        cost_estimate=expected(5 * slices),
        name="hidden_again",
    )(own, *edges, w_in, *kept)


def conv_backward(own, edges, grad, grad_edges, hidden, slopes, w_back, loss, sums):
    slices, _, frames, rows, columns = own.shape
    span = w_back.shape[1]
    volume, windows = conv_scratch(frames, rows, columns)
    total = pltpu.VMEM((2 * 128, span), jnp.float32)
    fixed = (w_back, pick_table(), loss, sums)
    out_shape = jax.ShapeDtypeStruct((span // BLOCK + 8, PACKED), jnp.float32)
    here = (own, *edges, grad, *grad_edges)
    blocks = rows // BLOCK
    parts = 1

    def of_slice(shape):
        rest = (0,) * (len(shape) - 1)
        return pl.BlockSpec((1,) + tuple(shape[1:]), lambda s, part: (s,) + rest)

    def part_of_slice(shape):
        size = (1, blocks // parts) + tuple(shape[2:])
        return pl.BlockSpec(size, lambda s, part: (s, part, 0, 0))

    def all_of(shape):
        return pl.BlockSpec(tuple(shape), lambda s, part: (0,) * len(shape))

    return pl.pallas_call(
        backward_kernel,
        grid=(slices, parts),
        in_specs=[of_slice(one.shape) for one in here]
        + [part_of_slice(one.shape) for one in (hidden, slopes)]
        + [all_of(one.shape) for one in fixed],
        out_specs=all_of(out_shape.shape),
        out_shape=out_shape,
        scratch_shapes=[
            volume,
            windows,
            windows,
            pltpu.VMEM((frames * columns, span), jnp.bfloat16),
            total,
            total,
        ],
        compiler_params=pltpu.CompilerParams(vmem_limit_bytes=VMEM),
        cost_estimate=expected(5 * slices),
        name="conv_backward",
    )(*here, hidden, slopes, *fixed)


def last_parts(array, axis):
    if lax.axis_size(axis) != 4:
        return [sum_over(array, axis)]
    others = [
        lax.ppermute(array, axis, [(i, i ^ k) for i in range(4)]) for k in (1, 2, 3)
    ]
    return [array, *others]


def in_vmem(array):
    return pltpu.with_memory_space_constraint(array, pltpu.VMEM)


def along(axis, step):
    count = lax.axis_size(axis)
    return [(i, i + step) for i in range(count) if 0 <= i + step < count]


def sum_over(array, axis):
    size = lax.axis_size(axis)
    if size & (size - 1):
        return lax.psum(array, axis)

    def other(values, bits):
        return lax.ppermute(values, axis, [(i, i ^ bits) for i in range(size)])

    bit = 1
    if size.bit_length() % 2 == 0:
        array = array + other(array, bit)
        bit = 2
    while bit < size:
        one, two, three = (other(array, bit * k) for k in (1, 2, 3))
        array = (array + one) + (two + three)
        bit *= 4
    return array


def corners_along(left, right, columns):
    both = jnp.concatenate([left, right], axis=1)
    lanes = both.shape[2]
    below = lax.ppermute(both[:, :, lanes - columns :], "af", along("af", 1))
    above = lax.ppermute(both[:, :, :columns], "af", along("af", -1))
    return below, above


def share_edges(low, high, first, last):
    left = lax.ppermute(last, "row", along("row", 1))
    right = lax.ppermute(first, "row", along("row", -1))
    below = lax.ppermute(high, "af", along("af", 1))
    above = lax.ppermute(low, "af", along("af", -1))
    return below, above, left, right, *corners_along(left, right, low.shape[3])


def image_edges(image, group):
    start, slices = group
    part = image[start : start + slices]
    _, _, frames, rows, columns = part.shape
    flat = (slices, 2, frames * columns)
    return share_edges(
        part[:, :, 0], part[:, :, frames - 1],
        part[:, :, :, 0].reshape(flat), part[:, :, :, rows - 1].reshape(flat),
    )


def return_edges(part_below, part_above, part_left, part_right, columns):
    lower = lax.ppermute(part_left, "row", along("row", -1))
    upper = lax.ppermute(part_right, "row", along("row", 1))
    from_above = lax.ppermute(part_below, "af", along("af", -1))
    from_below = lax.ppermute(part_above, "af", along("af", 1))
    corner_below, corner_above = corners_along(upper, lower, columns)
    return from_below, from_above, upper, lower, corner_below, corner_above


def image_kernel(
    main, from_below, from_above, upper, lower, corner_below, corner_above,
    table, note, out, image,
):
    slices, frames, rows, twice = main.shape
    columns = twice // 2
    row = lax.broadcasted_iota(jnp.int32, (rows, columns), 0)
    for s in range(slices):
        tops = upper[s].astype(jnp.float32)
        ends = lower[s].astype(jnp.float32)
        corners = {
            0: corner_below[s].astype(jnp.float32),
            frames - 1: corner_above[s].astype(jnp.float32),
        }
        for f in range(frames):
            at = slice((f + 1) * columns, (f + 2) * columns)
            for o in range(2):
                here = slice(o * columns, (o + 1) * columns)
                value = main[s, f, :, here]
                if f == 0:
                    value = value + from_below[s, o].astype(jnp.float32)
                if f == frames - 1:
                    value = value + from_above[s, o].astype(jnp.float32)
                top, end = tops[o : o + 1, at], ends[o : o + 1, at]
                if f in corners:
                    top = top + corners[f][o : o + 1]
                    end = end + corners[f][2 + o : 3 + o]
                value = value + jnp.where(row == 0, top, 0.0)
                value = value + jnp.where(row == rows - 1, end, 0.0)
                start = (s * frames + f) * rows
                image[start : start + rows, here] = value.astype(jnp.bfloat16)
    size = slices * frames * rows
    for start in range(0, size, 512):
        stop = min(start + 512, size)
        out[:, start:stop] = lax.dot_general(
            table[...], image[start:stop, :], NT, preferred_element_type=jnp.float32
        ).astype(jnp.bfloat16)
    rest = out.shape[1] - size
    if rest:
        lane = lax.broadcasted_iota(jnp.int32, (out.shape[0], rest), 1)
        out[:, size:] = jnp.where(lane == 0, note[0, 0], 0.0).astype(jnp.bfloat16)


def image_to_hybrid(main, added, table, note, lanes):
    slices, frames, rows, twice = main.shape
    return pl.pallas_call(
        image_kernel,
        in_specs=[pl.BlockSpec(memory_space=pltpu.VMEM)] * (2 + EDGES)
        + [pl.BlockSpec(memory_space=pltpu.SMEM)],
        out_shape=jax.ShapeDtypeStruct((twice, lanes), jnp.bfloat16),
        scratch_shapes=[pltpu.VMEM((slices * frames * rows, twice), jnp.bfloat16)],
        compiler_params=pltpu.CompilerParams(vmem_limit_bytes=VMEM),
        cost_estimate=expected(slices / 2),
        name="image_to_hybrid",
    )(main, *map(in_vmem, added), table, note)


def grad_image_kernel(hybrid, table, out, low, high, first, last, sums):
    slices, _, frames, rows, columns = out.shape
    sums[...] = jnp.zeros_like(sums)
    for s in range(slices):
        size = frames * rows
        start = s * size // 128 * 128
        stop = -(-(s + 1) * size // 128) * 128
        value = lax.dot_general(
            hybrid[:, start:stop], table[...], TN, preferred_element_type=jnp.float32
        ).astype(jnp.bfloat16)
        for c in range(2):
            tops, ends = [], []
            for f in range(frames):
                at = s * size + f * rows - start
                piece = value[at : at + rows, c * columns : (c + 1) * columns]
                out[s, c, f] = piece
                if f == 0:
                    low[s, c] = piece
                if f == frames - 1:
                    high[s, c] = piece
                wide = piece.astype(jnp.float32)
                sums[c : c + 1, :] += jnp.sum(wide, axis=0, keepdims=True)
                tops.append(wide[0:1])
                ends.append(wide[rows - 1 :])
            first[s, c : c + 1, :] = jnp.concatenate(tops, axis=1)
            last[s, c : c + 1, :] = jnp.concatenate(ends, axis=1)


def hybrid_to_grad(hybrid, table, shape):
    slices, channels, frames, rows, columns = shape
    edge_frame = jax.ShapeDtypeStruct((slices, channels, rows, columns), jnp.bfloat16)
    edge_row = jax.ShapeDtypeStruct((slices, channels, frames * columns), jnp.float32)
    return pl.pallas_call(
        grad_image_kernel,
        out_shape=[
            jax.ShapeDtypeStruct(shape, jnp.bfloat16),
            edge_frame,
            edge_frame,
            edge_row,
            edge_row,
            jax.ShapeDtypeStruct((2, columns), jnp.float32),
        ],
        compiler_params=pltpu.CompilerParams(vmem_limit_bytes=VMEM),
        cost_estimate=expected(slices / 2),
        name="hybrid_to_grad",
    )(in_vmem(hybrid), table)


def chunk_table():
    index = np.arange(512).reshape(4, 4, 32)
    return jnp.asarray(np.eye(512)[index.transpose(1, 0, 2).reshape(-1)], jnp.bfloat16)


def beside(pieces):
    return jnp.concatenate(pieces, axis=1)


def kspace_slice(
    k, index, frames_here, n_af, measured, target, sampled, share, scale, table,
    spectrum, grads, loss_lanes,
):
    frames = n_af * frames_here
    twice = table.shape[0]
    first = index * frames_here
    size = frames * 8
    here = spectrum[pl.ds(first, frames_here)].reshape(size, twice).astype(jnp.bfloat16)
    kspace = jnp.dot(here, table[...], preferred_element_type=jnp.float32)

    def place(t):
        return (t % frames_here) * n_af + t // frames_here

    filled = []
    for t in range(frames):
        mask = sampled[t]
        filled.append(mask * measured[k, t] + (1.0 - mask) * kspace[place(t) * 8 : place(t) * 8 + 8])
    slopes = []
    for t in range(frames):
        mask = sampled[t]
        near = range(max(t - 2, 0), min(t + 3, frames))
        shared = sum(share[t, s] * filled[s] for s in near)
        differ = mask * measured[k, t] + (1.0 - mask) * shared - target[k, t]
        square = differ * differ + 1.0
        inverse = lax.rsqrt(square)
        loss_lanes[...] += (1.0 - mask) * (square * inverse - 1.0)
        slopes.append((1.0 - mask) * differ * inverse * scale[...])
    for s in range(frames):
        near = range(max(s - 2, 0), min(s + 3, frames))
        grad = sum(share[t, s] * slopes[t] for t in near)
        grads[k, place(s) * 8 : place(s) * 8 + 8, :] = (1.0 - sampled[s]) * grad
    grad = grads[k]
    high = grad.astype(jnp.bfloat16)
    low = (grad - high.astype(jnp.float32)).astype(jnp.bfloat16)
    back = lax.dot_general(high, table[...], NT, preferred_element_type=jnp.float32)
    back += lax.dot_general(low, table[...], NT, preferred_element_type=jnp.float32)
    spectrum[pl.ds(first, frames_here)] = back.reshape(frames_here, n_af, 8, twice)


def kspace_kernel(
    frames_here, factor, received, measured, target, sampled, share, table, chunks,
    out, loss, count, spectrum, grads, loss_lanes, scale,
):
    groups, _, lanes = received.shape
    pairs, n_af, _, twice = spectrum.shape
    rows = twice // 2
    n_row = groups // n_af
    step = pl.program_id(0)
    tiles = lanes // 128
    size = out.shape[1]

    @pl.when(step == 0)
    def _():
        loss_lanes[...] = jnp.zeros_like(loss_lanes)
        last = slice((tiles - 1) * 128, lanes)
        notes = sum(received[group, 0:size, last].astype(jnp.float32) for group in range(groups))
        at = pairs * (128 // 4) - (tiles - 1) * 128
        total = notes[0:1, at : at + 1] * factor
        count[...] = jnp.broadcast_to(total, count.shape)
        scale[...] = jnp.broadcast_to(1.0 / total, scale.shape)
        for h in range(n_row // 4):
            for af in range(n_af):
                source = [
                    beside(
                        [
                            received[af * n_row + h * 4 + m, :, tile * 128 : (tile + 1) * 128]
                            for m in range(4)
                        ]
                    )
                    for tile in range(tiles)
                ]
                moved = jnp.dot(
                    jnp.concatenate(source, axis=0),
                    chunks[...],
                    preferred_element_type=jnp.float32,
                )
                for pair in range(pairs):
                    tile, k = pair // 4, pair % 4
                    for c in range(2):
                        at = c * rows + h * 128
                        start = tile * size + c * 8
                        spectrum[pair, af, :, at : at + 128] = moved[
                            start : start + 8, k * 128 : (k + 1) * 128
                        ]

    each = measured.shape[0]
    for k in range(each):
        kspace_slice(
            k, step * each + k, frames_here, n_af, measured, target, sampled, share, scale, table,
            spectrum, grads, loss_lanes,
        )

    @pl.when(step == pl.num_programs(0) - 1)
    def _():
        loss[...] = loss_lanes[...]

        for h in range(n_row // 4):
            for af in range(n_af):
                source = []
                for tile in range(tiles):
                    four = []
                    for k in range(4):
                        pair = min(tile * 4 + k, pairs - 1)
                        both = [
                            spectrum[pair, af, :, c * rows + h * 128 : c * rows + h * 128 + 128]
                            for c in range(2)
                        ]
                        four.append(jnp.concatenate(both, axis=0).astype(jnp.bfloat16))
                    source.append(beside(four))
                moved = jnp.dot(
                    jnp.concatenate(source, axis=0),
                    chunks[...],
                    preferred_element_type=jnp.float32,
                ).astype(jnp.bfloat16)
                for m in range(4):
                    for tile in range(tiles):
                        out[af * n_row + h * 4 + m, :, tile * 128 : (tile + 1) * 128] = moved[
                            tile * size : (tile + 1) * size, m * 128 : (m + 1) * 128
                        ]


def kspace_step(received, measured, target, sampled, share, table, frames_here, factor):
    _, frames, lines, twice = measured.shape
    slices = measured.shape[0]
    n_af = frames // frames_here
    each = 2 if slices % 2 == 0 else 1
    chunks = chunk_table()

    def some(shape):
        return pl.BlockSpec((each,) + tuple(shape[1:]), lambda s: (s, 0, 0, 0))

    return pl.pallas_call(
        functools.partial(kspace_kernel, frames_here, factor),
        grid=(slices // each,),
        in_specs=[
            pl.BlockSpec(memory_space=pltpu.VMEM),
            some(measured.shape),
            some(target.shape),
            whole(sampled.shape),
            pl.BlockSpec(memory_space=pltpu.SMEM),
            whole(table.shape),
            whole(chunks.shape),
        ],
        out_specs=[whole(received.shape), whole((lines, twice)), whole((8, 128))],
        out_shape=[
            jax.ShapeDtypeStruct(received.shape, jnp.bfloat16),
            jax.ShapeDtypeStruct((lines, twice), jnp.float32),
            jax.ShapeDtypeStruct((8, 128), jnp.float32),
        ],
        scratch_shapes=[
            pltpu.VMEM((slices * frames_here, n_af, lines, twice), jnp.float32),
            pltpu.VMEM((each, frames * lines, twice), jnp.float32),
            pltpu.VMEM((lines, twice), jnp.float32),
            pltpu.VMEM((lines, twice), jnp.float32),
        ],
        compiler_params=pltpu.CompilerParams(vmem_limit_bytes=VMEM),
        cost_estimate=expected(3 * slices),
        name="kspace",
    )(in_vmem(received), measured, target, sampled, share, table, chunks)


def middle_plain(main, added, measured, target, sampled, share, table_y, table_x):
    highest = lax.Precision.HIGHEST
    slices, frames_here, rows_here, twice = main.shape
    count = lax.psum(jnp.sum(1.0 - sampled) * (2.0 * slices * measured.shape[3] / 2), AXES)
    columns = twice // 2
    frames, lines = measured.shape[1:3]
    rows = measured.shape[3] // 2
    table_y = jnp.asarray(table_y, jnp.bfloat16)
    table_x = jnp.asarray(table_x, jnp.bfloat16)
    image = main.reshape(slices, frames_here, rows_here, 2, columns)
    below, above, upper, lower, *corners = (one.astype(jnp.float32) for one in added)
    image = image.at[:, 0].add(below.transpose(0, 2, 1, 3))
    image = image.at[:, frames_here - 1].add(above.transpose(0, 2, 1, 3))
    for at, line in ((0, upper), (rows_here - 1, lower)):
        line = line[:, :, columns:-columns].reshape(slices, 2, frames_here, columns)
        image = image.at[:, :, at].add(line.transpose(0, 2, 1, 3))
    for f, corner in ((0, corners[0]), (frames_here - 1, corners[1])):
        image = image.at[:, f, 0].add(corner[:, 0:2])
        image = image.at[:, f, rows_here - 1].add(corner[:, 2:4])
    flat = image.reshape(slices, frames_here, rows_here, twice).astype(jnp.bfloat16)
    hybrid = jnp.dot(flat, table_y, preferred_element_type=jnp.float32).astype(jnp.bfloat16)
    hybrid = hybrid.reshape(slices, frames_here, rows_here, 2, columns)
    part = lax.all_to_all(hybrid, "af", split_axis=4, concat_axis=1, tiled=True)
    spread = lax.all_to_all(part, "row", split_axis=4, concat_axis=2, tiled=True)
    spectrum = jnp.transpose(spread, (0, 1, 4, 3, 2)).reshape(slices, frames, lines, 2 * rows)
    kspace = jnp.dot(spectrum, table_x, preferred_element_type=jnp.float32)
    mask = sampled[None, :, :, None]
    filled = mask * measured + (1.0 - mask) * kspace
    shared = jnp.einsum("ts,bslk->btlk", share, filled, precision=highest)
    differ = mask * measured + (1.0 - mask) * shared - target
    root = jnp.sqrt(differ * differ + 1.0)
    loss = jnp.sum((1.0 - mask) * (root - 1.0))
    slope = (1.0 - mask) * differ / root / count
    grad = (1.0 - mask) * jnp.einsum("ts,btlk->bslk", share, slope, precision=highest)
    back = jnp.dot(grad, table_x.T.astype(jnp.float32), precision=highest).astype(jnp.bfloat16)
    back = jnp.transpose(back.reshape(slices, frames, lines, 2, rows), (0, 1, 4, 3, 2))
    part = lax.all_to_all(back, "row", split_axis=2, concat_axis=4, tiled=True)
    whole_rows = lax.all_to_all(part, "af", split_axis=1, concat_axis=4, tiled=True)
    grad = jnp.dot(
        whole_rows.reshape(slices, frames_here, rows_here, twice),
        table_y.T,
        preferred_element_type=jnp.float32,
    ).reshape(slices, frames_here, rows_here, 2, columns)
    grad = jnp.transpose(grad, (0, 3, 1, 2, 4)).astype(jnp.bfloat16)
    return loss, jnp.broadcast_to(count, (8, 128)), grad, jnp.sum(grad.astype(jnp.float32), axis=(0, 2, 3, 4))


def update_kernel(parts, *refs):
    count, *ins = refs[parts : parts + 13]
    outs = refs[parts + 13 :]
    total = refs[0][...]
    if parts == 4:
        total = (total + refs[1][...]) + (refs[2][...] + refs[3][...])
    *outs, loss, unsampled = outs
    taps, width = ins[0].shape
    turned = total[0:width, :].T

    def step(kind, at, grad):
        master, first, second, smooth = (one[at] for one in ins[kind::3])
        rate = (rate_in, rate_out, rate_bias)[kind]
        first, second, master = adam_step(master, grad, first, second, rate)
        average = average_keep * smooth + (1.0 - average_keep) * master
        for out, value in zip(outs[kind::3], (first, second, master, average, master)):
            out[at] = value.astype(out.dtype)

    step(0, ..., turned[0:taps, :])
    for tap in range(ins[1].shape[0]):
        start = PACKED // 2 + 2 * tap
        step(1, tap, turned[start : start + 2, :])
    step(2, (slice(0, 1), slice(0, width)), turned[54:55, :])
    step(2, (slice(0, 1), slice(width, width + 2)), total[width : width + 1, 1:3])
    loss[...] = total[width : width + 1, 0:1]
    unsampled[...] = count[0:1, 0:1]


def update(parts, count, weights, firsts, seconds, smooths):
    arrays = [*weights, *firsts, *seconds, *smooths]
    turn = {1: lambda one: one.reshape(1, -1), 2: jnp.transpose, 3: lambda one: one}
    arrays = [turn[one.ndim](one) for one in arrays]
    kinds = [jnp.float32] * 4 + [jnp.bfloat16]
    *outs, loss, unsampled = pl.pallas_call(
        functools.partial(update_kernel, len(parts)),
        out_shape=[jax.ShapeDtypeStruct(one.shape, kind) for kind in kinds for one in arrays[:3]]
        + [jax.ShapeDtypeStruct((1, 1), jnp.float32)] * 2,
        name="update",
    )(*map(in_vmem, parts), count, *arrays)
    back = (jnp.transpose, lambda one: one, lambda one: one.reshape(-1))
    return loss[0, 0], unsampled[0, 0], *[back[k % 3](one) for k, one in enumerate(outs)]


def middle_fast(
    main, added, measured, target, sampled, share, table_y, table_x, between, after
):
    devices = lax.axis_size("af") * lax.axis_size("row")
    slices, frames_here, rows, twice = main.shape
    lines, readout = measured.shape[2:]
    size = slices * frames_here * rows
    order = np.arange(twice).reshape(2, devices, lines).transpose(1, 0, 2).reshape(-1)
    permuted = jnp.asarray(np.ascontiguousarray(table_y[:, order].T), jnp.bfloat16)
    mask = jnp.broadcast_to(sampled[:, :, None], sampled.shape + (readout,))
    note = jnp.sum(1.0 - sampled).reshape(1, 1)
    mask, share, *added = lax.optimization_barrier((mask, share, *added))
    lanes = (size // 128 + 1) * 128
    hybrid = image_to_hybrid(main, added, permuted, note, lanes)
    received = lax.all_to_all(
        hybrid.reshape(devices, 2 * lines, lanes), AXES, 0, 0, tiled=True
    )
    first = between(hybrid)
    received, first = lax.optimization_barrier((received, first))
    back, loss, count = kspace_step(
        received, measured, target, mask, share, jnp.asarray(table_x, jnp.bfloat16),
        frames_here, 1.0 * slices * readout,
    )
    returned = lax.all_to_all(back, AXES, 0, 0, tiled=True)
    second = after(back, first)
    returned, second = lax.optimization_barrier((returned, second))
    shape = (slices, 2, frames_here, rows, twice // 2)
    grad, *grad_edge, sums = hybrid_to_grad(returned.reshape(twice, lanes), permuted, shape)
    return loss, count, grad, grad_edge, sums, second


def train_step(
    image_in, measured, target, sampled, share, table_y, table_x, w_in, w_out, w_back, bias_out
):
    slices, _, frames_here, rows, columns = image_in.shape
    frames, lines = measured.shape[1:3]
    cut = (slices + 1) // 2
    groups = [(0, cut), (cut, slices - cut)]
    edges = image_edges(image_in, (0, slices))
    main, *part = conv_forward(image_in, edges, (0, slices), w_in, w_out, bias_out)
    added = return_edges(*part, columns)

    def again(group, after, kept=()):
        held, _ = lax.optimization_barrier((w_in.T, after))
        return hidden_again(image_in, edges, group, held, kept)

    fits = rows == 32 and lines == 8 and lax.axis_size("row") % 4 == 0
    fits = fits and frames * lines <= 256
    if fits:
        loss, count, grad, grad_edge, sums, kept = middle_fast(
            main, added, measured, target, sampled, share, table_y, table_x,
            functools.partial(again, groups[0]), functools.partial(again, groups[1]),
        )
    else:
        loss, count, grad, sums = middle_plain(
            main, added, measured, target, sampled, share, table_y, table_x
        )
        flat = (slices, 2, frames_here * columns)
        grad_edge = (
            grad[:, :, 0], grad[:, :, frames_here - 1],
            grad[:, :, :, 0].reshape(flat), grad[:, :, :, rows - 1].reshape(flat),
        )
        kept = None
    around = share_edges(*grad_edge)
    if kept is not None:
        return count, conv_backward(image_in, edges, grad, around, *kept, w_back, loss, sums)
    total = 0.0
    loss, sums = loss.reshape(1, 1), sums.reshape(2, 1)
    for first, size in groups:
        own, *sides = (one[first : first + size] for one in (image_in, *edges, grad, *around))
        held, _ = lax.optimization_barrier((w_in.T, total))
        kept = hidden_again(own, sides[:EDGES], (0, size), held)
        total += conv_backward(
            own, sides[:EDGES], sides[EDGES], sides[EDGES + 1 :], *kept, w_back, loss, sums
        )
        loss, sums = 0.0 * loss, 0.0 * sums
    return count, total


def on_device(
    image_in, measured, target, line_mask, window_half, in_kernel, out_kernel, biases,
    in_moment, out_moment, bias_moment, in_square, out_square, bias_square,
    in_smooth, out_smooth, bias_smooth,
):
    slices, _, frames_here, rows_here, columns = image_in.shape
    frames = measured.shape[1]
    width = in_kernel.shape[0]
    rows = rows_here * lax.axis_size("row")
    table_y = dft_table(columns)
    table_x = dft_table(rows)
    share = share_matrix(window_half, frames)
    sampled = line_mask.astype(jnp.float32)
    w_in = conv_in_weights(in_kernel, biases[:width])
    w_out = conv_out_weights(out_kernel)
    w_back = conv_back_weights(out_kernel)

    count, total = train_step(
        image_in, measured, target, sampled, share, table_y, table_x,
        w_in, w_out, w_back, biases,
    )
    return update(
        last_parts(sum_over(total, "row"), "af"),
        count,
        (in_kernel, out_kernel, biases),
        (in_moment, out_moment, bias_moment),
        (in_square, out_square, bias_square),
        (in_smooth, out_smooth, bias_smooth),
    )


def solution(mesh):
    in_specs = (
        P(None, None, "af", "row", None),
        P(None, None, ("af", "row"), None),
        P(None, None, ("af", "row"), None),
        P(None, ("af", "row")),
    ) + (P(),) * 13
    return jax.shard_map(
        on_device, mesh=mesh, in_specs=in_specs, out_specs=(P(),) * 17, check_vma=False
    )
```

```python
import functools
import math

import jax
import jax.numpy as jnp
import numpy as np
from jax import lax
from jax.experimental import pallas as pl
from jax.experimental.pallas import tpu as pltpu
from jax.sharding import PartitionSpec as P

STEP = 5
AXES = ("af", "row")
BLOCK = 4
WIN = 8
SIDE = 16
DEPTH = 9 * SIDE
ONES_ROW = BLOCK + 2
PACKED = 128
EDGES = 6
BIAS_LANE = WIN - 1
VMEM = 60 * 2**20
GELU = math.sqrt(2.0 / math.pi)
CUBE = 0.044715

beta_first = 0.5
beta_second = 0.5
rate_in = 0.2
rate_out = 0.04
rate_bias = 0.3
decay_weight = 0.01
average_keep = 0.9
epsilon = 1e-08

NT = (((1,), (1,)), ((), ()))
TN = (((0,), (0,)), ((), ()))


def dft_table(length):
    index = np.arange(length)
    phase = (index[:, None] * index[None, :] % length) * (2.0 * math.pi / length)
    cosine = np.cos(phase) / math.sqrt(length)
    sine = np.sin(phase) / math.sqrt(length)
    upper = np.concatenate([cosine, -sine], axis=1)
    lower = np.concatenate([sine, cosine], axis=1)
    return np.concatenate([upper, lower], axis=0).astype(np.float32)


def share_matrix(window_half, frames):
    index = jnp.arange(frames, dtype=jnp.int32)
    inside = (jnp.abs(index[None, :] - index[:, None]) <= window_half[:, None]).astype(jnp.float32)
    return inside / jnp.sum(inside, axis=1, keepdims=True)


def adam_step(master, grad, first, second, rate):
    first_new = beta_first * first + (1.0 - beta_first) * grad
    second_new = beta_second * second + (1.0 - beta_second) * grad * grad
    first_hat = first_new / (1.0 - beta_first**STEP)
    second_hat = second_new / (1.0 - beta_second**STEP)
    master_new = master - rate * (
        first_hat / (jnp.sqrt(second_hat) + epsilon) + decay_weight * master
    )
    return (first_new, second_new, master_new)


def conv_in_weights(kernel, bias):
    width = kernel.shape[0]
    taps = kernel.astype(jnp.bfloat16).astype(jnp.float32).reshape(width, 2, 3, 3, 3)
    rows = []
    for j in range(BLOCK):
        row = jnp.pad(taps, ((0, 0), (0, 0), (0, 0), (j, WIN - 3 - j), (0, 0)))
        rows.append(row.transpose(0, 2, 4, 1, 3))
    spread = jnp.stack(rows)
    high = lax.reduce_precision(bias, 8, 7)
    rest = bias - high
    middle = lax.reduce_precision(rest, 8, 7)
    parts = jnp.stack([high, middle, rest - middle], axis=1)
    spread = spread.at[:, :, :, 0, 0, ONES_ROW].set(jnp.broadcast_to(parts, (BLOCK, width, 3)))
    return 0.5 * spread.reshape(BLOCK * width, DEPTH)


def conv_out_weights(kernel):
    width = kernel.shape[2]
    taps = kernel.astype(jnp.bfloat16).reshape(3, 3, 3, 2, width)[:, ::-1]
    columns = []
    for j in range(BLOCK):
        column = jnp.pad(taps, ((0, 0), (j, WIN - 3 - j), (0, 0), (0, 0), (0, 0)))
        columns.append(column.transpose(0, 2, 3, 1, 4))
    return jnp.stack(columns, axis=4).reshape(DEPTH, BLOCK * width)


def conv_back_weights(kernel):
    width = kernel.shape[2]
    taps = kernel.astype(jnp.bfloat16).reshape(3, 3, 3, 2, width)[::-1, ::-1, ::-1]
    rows = []
    for j in range(BLOCK):
        row = jnp.pad(taps, ((0, 0), (j, WIN - 3 - j), (0, 0), (0, 0), (0, 0)))
        rows.append(row.transpose(0, 2, 3, 1, 4))
    return 0.5 * jnp.stack(rows, axis=4).reshape(DEPTH, BLOCK * width)


def pick_table():
    table = np.zeros((2, 256, PACKED), np.float32)
    for a, b, e, c in np.ndindex(3, 3, 3, 2):
        lane = ((a * 3 + e) * 2 + c) * WIN + b
        table[0, lane, 27 * c + 9 * a + 3 * b + e] = 1.0
        tap = 9 * (2 - a) + 3 * (2 - b) + 2 - e
        table[1, lane, PACKED // 2 + 2 * tap + c] = 1.0
    table[0, BIAS_LANE, 54] = 1.0
    return jnp.asarray(table, jnp.bfloat16)


def load_volume(volume, own, below, above, left, right, corner_below, corner_above):
    _, channels, frames, rows, columns = own.shape
    lanes = (frames + 2) * columns
    for c in range(channels):
        volume[c, rows + 8 : rows + 16, :] = jnp.zeros((8, lanes), jnp.float32)
        for t in range(frames + 2):
            if t == 0:
                piece = below[0, c]
            elif t == frames + 1:
                piece = above[0, c]
            else:
                piece = own[0, c, t - 1]
            volume[c, 8 : 8 + rows, t * columns : (t + 1) * columns] = piece.astype(jnp.float32)
    low = corner_below[0].astype(jnp.float32)
    high = corner_above[0].astype(jnp.float32)
    for side, at, line in ((0, 7, left), (1, rows + 8, right)):
        middle = line[0].astype(jnp.float32)
        for c in range(channels):
            k = 2 * side + c
            volume[c, at : at + 1, 0:columns] = low[k : k + 1]
            volume[c, at : at + 1, columns : lanes - columns] = middle[c : c + 1]
            volume[c, at : at + 1, lanes - columns :] = high[k : k + 1]


def build_windows(volume, windows, columns, ones):
    blocks, _, lanes = windows.shape
    column = lax.broadcasted_iota(jnp.int32, (SIDE, columns), 1)
    row = lax.broadcasted_iota(jnp.int32, (SIDE, columns), 0)
    zero = jnp.zeros((SIDE, columns), jnp.bfloat16)
    for block in range(blocks):
        for t in range(lanes // columns):
            here = slice(t * columns, (t + 1) * columns)
            start = 7 + BLOCK * block
            window = jnp.concatenate(
                [volume[c, start : start + WIN, here] for c in range(2)], axis=0
            ).astype(jnp.bfloat16)
            for e in range(3):
                shifted = window
                if e != 1:
                    shifted = pltpu.roll(window, (1 - e) % columns, axis=1)
                    shifted = jnp.where(column == (0 if e == 0 else columns - 1), zero, shifted)
                if ones and e == 0:
                    shifted = jnp.where(row == ONES_ROW, zero + 1.0, shifted)
                windows[block, e * SIDE : (e + 1) * SIDE, here] = shifted


def forward_kernel(
    own, *refs,
):
    edges, refs = of_step(refs[:EDGES], pl.program_id(0)), refs[EDGES:]
    (
    w_in, w_out, bias_out,
    main, part_below, part_above, part_left, part_right,
    volume, windows, total, hidden, mixed, spread,
    ) = refs
    _, _, frames, rows, columns = own.shape
    blocks = windows.shape[0]
    load_volume(volume, own, *edges)
    build_windows(volume, windows, columns, True)
    column = lax.broadcasted_iota(jnp.int32, (SIDE, columns), 1)

    def step(block, carry):
        for f in range(frames):
            here = slice(f * columns, (f + 1) * columns)
            patch = jnp.concatenate(
                [windows[block, :, (f + a) * columns : (f + a + 1) * columns] for a in range(3)],
                axis=0,
            )
            half = jnp.dot(w_in[...], patch, preferred_element_type=jnp.float32)
            t = jnp.tanh(half * (2.0 * GELU + (8.0 * GELU * CUBE) * (half * half)))
            hidden[:, here] = (half + half * t).astype(jnp.bfloat16)
        for f in range(frames):
            here = slice(f * columns, (f + 1) * columns)
            mixed[f] = jnp.dot(w_out[...], hidden[:, here], preferred_element_type=jnp.float32)
        for t in range(frames + 2):
            window = None
            for e in range(3):
                summed = None
                for a in range(3):
                    f = t - 2 + a
                    if 0 <= f < frames:
                        start = (a * 3 + e) * SIDE
                        piece = mixed[f, start : start + SIDE, :]
                        summed = piece if summed is None else summed + piece
                if e != 1:
                    summed = pltpu.roll(summed, (1 - e) % columns, axis=1)
                    summed = jnp.where(column == (0 if e == 0 else columns - 1), 0.0, summed)
                window = summed if window is None else window + summed
            spread[block, :, t * columns : (t + 1) * columns] = window
        return carry

    lax.fori_loop(0, blocks, step, 0, unroll=True)
    total[...] = jnp.zeros_like(total)
    for block in range(blocks):
        for o in range(2):
            start = 7 + BLOCK * block
            total[o, start : start + WIN, :] = (
                total[o, start : start + WIN, :] + spread[block, o * WIN : (o + 1) * WIN, :]
            )
    for o in range(2):
        for t in range(frames + 2):
            here = total[o, 8 : 8 + rows, t * columns : (t + 1) * columns]
            if t == 0:
                part_below[0, o] = here.astype(jnp.bfloat16)
            elif t == frames + 1:
                part_above[0, o] = here.astype(jnp.bfloat16)
            else:
                base = volume[o, 8 : 8 + rows, t * columns : (t + 1) * columns] + bias_out[bias_out.shape[0] - 2 + o]
                main[0, t - 1, :, o * columns : (o + 1) * columns] = base + here
    for at, out in ((7, part_left), (8 + rows, part_right)):
        both = [total[o, at : at + 1, :] for o in range(2)]
        out[0] = jnp.concatenate(both, axis=0).astype(jnp.bfloat16)


def patches(source, block, frames, columns):
    return jnp.concatenate(
        [source[block, :, a * columns : (a + frames) * columns] for a in range(3)], axis=0
    )


def hidden_kernel(start, own, *refs):
    edges, (w_in, *_, hidden, slopes, volume, windows) = refs[:EDGES], refs[EDGES:]
    _, _, frames, rows, columns = own.shape
    load_volume(volume, own, *of_step(edges, start + pl.program_id(0)))
    build_windows(volume, windows, columns, True)

    def step(block, carry):
        patch = patches(windows, block, frames, columns)
        for f in range(frames):
            here = slice(f * columns, (f + 1) * columns)
            half = lax.dot_general(
                patch[:, here], w_in[...], TN, preferred_element_type=jnp.float32
            )
            u = half * half
            t = jnp.tanh(half * (2.0 * GELU + (8.0 * GELU * CUBE) * u))
            up = 1.0 + t
            hidden[0, block, here, :] = (half * up).astype(jnp.bfloat16)
            slope = half * (2.0 * GELU + (24.0 * GELU * CUBE) * u)
            slopes[0, block, here, :] = (up + (up * (1.0 - t)) * slope).astype(jnp.bfloat16)
        return carry

    lax.fori_loop(0, windows.shape[0], step, 0, unroll=True)


def backward_kernel(
    own, *refs,
):
    edges, grad, grad_edges = refs[:EDGES], refs[EDGES], refs[EDGES + 1 : 2 * EDGES + 1]
    (
        hidden, slopes, w_back, pick, loss, sums, out,
        volume, windows, grad_windows, grads, sum_in, sum_out,
    ) = refs[2 * EDGES + 1 :]
    _, _, frames, rows, columns = own.shape

    part = pl.program_id(1)

    @pl.when((pl.program_id(0) == 0) & (part == 0))
    def _():
        sum_in[...] = jnp.zeros_like(sum_in)
        sum_out[...] = jnp.zeros_like(sum_out)

    @pl.when(part == 0)
    def _():
        load_volume(volume, own, *of_step(edges, pl.program_id(0)))
        build_windows(volume, windows, columns, True)
        load_volume(volume, grad, *of_step(grad_edges, pl.program_id(0)))
        build_windows(volume, grad_windows, columns, False)

    blocks = hidden.shape[1]

    def step(at):
        block = part * blocks + at
        patch = patches(windows, block, frames, columns)
        grad_patch = patches(grad_windows, block, frames, columns)
        for f in range(frames):
            here = slice(f * columns, (f + 1) * columns)
            gh = lax.dot_general(
                grad_patch[:, here], w_back[...], TN, preferred_element_type=jnp.float32
            )
            grads[here, :] = (slopes[0, at, here, :].astype(jnp.float32) * gh).astype(
                jnp.bfloat16
            )
        sum_in[:DEPTH, :] += jnp.dot(patch, grads[...], preferred_element_type=jnp.float32)
        sum_out[:DEPTH, :] += jnp.dot(
            grad_patch, hidden[0, at], preferred_element_type=jnp.float32
        )

    for at in range(blocks):
        step(at)

    @pl.when((pl.program_id(0) == pl.num_programs(0) - 1) & (part == pl.num_programs(1) - 1))
    def _():
        width = sum_in.shape[1] // BLOCK
        lanes = sum_in.shape[0]
        lane = lax.broadcasted_iota(jnp.int32, (width, lanes), 1)
        picked = jnp.zeros((width, pick.shape[2]), jnp.float32)
        for index, source in enumerate((sum_in[...].T, sum_out[...].T)):
            folded = source[0:width, :]
            bias = folded
            for j in range(1, BLOCK):
                piece = source[j * width : (j + 1) * width, :]
                folded = folded + pltpu.roll(piece, lanes - j, axis=1)
                bias = bias + piece
            if index == 0:
                moved = pltpu.roll(bias, BIAS_LANE - ONES_ROW, axis=1)
                folded = jnp.where(lane == BIAS_LANE, moved, folded)
            for _ in range(3):
                piece = folded.astype(jnp.bfloat16)
                folded = folded - piece.astype(jnp.float32)
                picked = picked + jnp.dot(piece, pick[index], preferred_element_type=jnp.float32)
        out[0:width, :] = picked
        spot = lax.broadcasted_iota(jnp.int32, (8, PACKED), 1)
        both = jnp.sum(sums[...], axis=1, keepdims=True)
        values = (jnp.sum(loss[...], axis=(0, 1), keepdims=True), both[0:1], both[1:2])
        row = jnp.zeros((8, PACKED), jnp.float32)
        for k, value in enumerate(values):
            row = jnp.where(spot == k, value, row)
        out[width:, :] = row


def of_step(refs, step):
    return [ref.at[pl.ds(step, 1)] for ref in refs]


def whole(shape):
    return pl.BlockSpec(tuple(shape), lambda s: (0,) * len(shape))


def a_slice(shape, first=0):
    rest = (0,) * (len(shape) - 1)
    return pl.BlockSpec((1,) + tuple(shape[1:]), lambda s: (s + first,) + rest)


def expected(microseconds):
    return pl.CostEstimate(
        flops=int(microseconds * 1.15e9), bytes_accessed=0, transcendentals=0
    )


def conv_scratch(frames, rows, columns):
    lanes = (frames + 2) * columns
    return (
        pltpu.VMEM((2, rows + 16, lanes), jnp.float32),
        pltpu.VMEM((rows // BLOCK, 3 * SIDE, lanes), jnp.bfloat16),
    )


def conv_forward(own, edges, group, w_in, w_out, bias_out):
    _, _, frames, rows, columns = own.shape
    first, slices = group
    lanes = (frames + 2) * columns
    span = w_in.shape[0]
    volume, windows = conv_scratch(frames, rows, columns)
    out_shape = [
        jax.ShapeDtypeStruct((slices, frames, rows, 2 * columns), jnp.float32),
        jax.ShapeDtypeStruct((slices, 2, rows, columns), jnp.bfloat16),
        jax.ShapeDtypeStruct((slices, 2, rows, columns), jnp.bfloat16),
        jax.ShapeDtypeStruct((slices, 2, lanes), jnp.bfloat16),
        jax.ShapeDtypeStruct((slices, 2, lanes), jnp.bfloat16),
    ]
    return pl.pallas_call(
        forward_kernel,
        grid=(slices,),
        in_specs=[a_slice(own.shape, first)]
        + [pl.BlockSpec(memory_space=pltpu.VMEM)] * EDGES
        + [whole(w_in.shape), whole(w_out.shape), pl.BlockSpec(memory_space=pltpu.SMEM)],
        out_specs=[a_slice(one.shape) for one in out_shape],
        out_shape=out_shape,
        scratch_shapes=[
            volume,
            windows,
            volume,
            pltpu.VMEM((span, frames * columns), jnp.bfloat16),
            pltpu.VMEM((frames, DEPTH, columns), jnp.float32),
            pltpu.VMEM((rows // BLOCK, SIDE, lanes), jnp.float32),
        ],
        compiler_params=pltpu.CompilerParams(vmem_limit_bytes=VMEM),
        cost_estimate=expected(6 * slices),
        name="conv_forward",
    )(own, *map(in_vmem, edges), w_in, w_out, bias_out)


def hidden_again(own, edges, group, w_in, kept=()):
    _, _, frames, rows, columns = own.shape
    first, slices = group
    volume, windows = conv_scratch(frames, rows, columns)
    shape = (own.shape[0], rows // BLOCK, frames * columns, w_in.shape[1])
    return pl.pallas_call(
        functools.partial(hidden_kernel, first),
        grid=(slices,),
        in_specs=[a_slice(own.shape, first)]
        + [pl.BlockSpec(memory_space=pltpu.VMEM)] * EDGES
        + [whole(w_in.shape)]
        + [pl.BlockSpec(memory_space=pl.ANY)] * len(kept),
        out_specs=[a_slice(shape, first)] * 2,
        out_shape=[jax.ShapeDtypeStruct(shape, jnp.bfloat16)] * 2,
        input_output_aliases={2 + EDGES + k: k for k in range(len(kept))},
        scratch_shapes=[volume, windows],
        compiler_params=pltpu.CompilerParams(vmem_limit_bytes=VMEM),
        cost_estimate=expected(5 * slices),
        name="hidden_again",
    )(own, *map(in_vmem, edges), w_in, *kept)


def conv_backward(own, edges, grad, grad_edges, hidden, slopes, w_back, loss, sums):
    slices, _, frames, rows, columns = own.shape
    span = w_back.shape[1]
    volume, windows = conv_scratch(frames, rows, columns)
    total = pltpu.VMEM((2 * 128, span), jnp.float32)
    fixed = (w_back, pick_table(), loss, sums)
    out_shape = jax.ShapeDtypeStruct((span // BLOCK + 8, PACKED), jnp.float32)
    sides = [pl.BlockSpec(memory_space=pltpu.VMEM)] * EDGES
    here = (own, *map(in_vmem, edges), grad, *map(in_vmem, grad_edges))
    blocks = rows // BLOCK
    parts = 1

    def of_slice(shape):
        rest = (0,) * (len(shape) - 1)
        return pl.BlockSpec((1,) + tuple(shape[1:]), lambda s, part: (s,) + rest)

    def part_of_slice(shape):
        size = (1, blocks // parts) + tuple(shape[2:])
        return pl.BlockSpec(size, lambda s, part: (s, part, 0, 0))

    def all_of(shape):
        return pl.BlockSpec(tuple(shape), lambda s, part: (0,) * len(shape))

    return pl.pallas_call(
        backward_kernel,
        grid=(slices, parts),
        in_specs=[of_slice(own.shape), *sides, of_slice(grad.shape), *sides]
        + [part_of_slice(one.shape) for one in (hidden, slopes)]
        + [all_of(one.shape) for one in fixed],
        out_specs=all_of(out_shape.shape),
        out_shape=out_shape,
        scratch_shapes=[
            volume,
            windows,
            windows,
            pltpu.VMEM((frames * columns, span), jnp.bfloat16),
            total,
            total,
        ],
        compiler_params=pltpu.CompilerParams(vmem_limit_bytes=VMEM),
        cost_estimate=expected(5 * slices),
        name="conv_backward",
    )(*here, hidden, slopes, *fixed)


def last_parts(array, axis):
    if lax.axis_size(axis) != 4:
        return [sum_over(array, axis)]
    others = [
        lax.ppermute(array, axis, [(i, i ^ k) for i in range(4)]) for k in (1, 2, 3)
    ]
    return [array, *others]


def in_vmem(array):
    return pltpu.with_memory_space_constraint(array, pltpu.VMEM)


def along(axis, step):
    count = lax.axis_size(axis)
    return [(i, i + step) for i in range(count) if 0 <= i + step < count]


def sum_over(array, axis):
    size = lax.axis_size(axis)
    if size & (size - 1):
        return lax.psum(array, axis)

    def other(values, bits):
        return lax.ppermute(values, axis, [(i, i ^ bits) for i in range(size)])

    bit = 1
    if size.bit_length() % 2 == 0:
        array = array + other(array, bit)
        bit = 2
    while bit < size:
        one, two, three = (other(array, bit * k) for k in (1, 2, 3))
        array = (array + one) + (two + three)
        bit *= 4
    return array


def corners_along(left, right, columns):
    both = jnp.concatenate([left, right], axis=1)
    lanes = both.shape[2]
    below = lax.ppermute(both[:, :, lanes - columns :], "af", along("af", 1))
    above = lax.ppermute(both[:, :, :columns], "af", along("af", -1))
    return below, above


def share_edges(low, high, first, last):
    left = lax.ppermute(last, "row", along("row", 1))
    right = lax.ppermute(first, "row", along("row", -1))
    below = lax.ppermute(high, "af", along("af", 1))
    above = lax.ppermute(low, "af", along("af", -1))
    return below, above, left, right, *corners_along(left, right, low.shape[3])


def image_edges(image, group):
    start, slices = group
    part = image[start : start + slices]
    _, _, frames, rows, columns = part.shape
    flat = (slices, 2, frames * columns)
    return share_edges(
        part[:, :, 0], part[:, :, frames - 1],
        part[:, :, :, 0].reshape(flat), part[:, :, :, rows - 1].reshape(flat),
    )


def return_edges(part_below, part_above, part_left, part_right, columns):
    from_above = lax.ppermute(part_below, "af", along("af", -1))
    from_below = lax.ppermute(part_above, "af", along("af", 1))
    lower = lax.ppermute(part_left, "row", along("row", -1))
    upper = lax.ppermute(part_right, "row", along("row", 1))
    corner_below, corner_above = corners_along(upper, lower, columns)
    return from_below, from_above, upper, lower, corner_below, corner_above


def image_kernel(
    main, from_below, from_above, upper, lower, corner_below, corner_above,
    table, note, out, image,
):
    slices, frames, rows, twice = main.shape
    columns = twice // 2
    row = lax.broadcasted_iota(jnp.int32, (rows, columns), 0)
    for s in range(slices):
        tops = upper[s].astype(jnp.float32)
        ends = lower[s].astype(jnp.float32)
        corners = {
            0: corner_below[s].astype(jnp.float32),
            frames - 1: corner_above[s].astype(jnp.float32),
        }
        for f in range(frames):
            at = slice((f + 1) * columns, (f + 2) * columns)
            for o in range(2):
                here = slice(o * columns, (o + 1) * columns)
                value = main[s, f, :, here]
                if f == 0:
                    value = value + from_below[s, o].astype(jnp.float32)
                if f == frames - 1:
                    value = value + from_above[s, o].astype(jnp.float32)
                top, end = tops[o : o + 1, at], ends[o : o + 1, at]
                if f in corners:
                    top = top + corners[f][o : o + 1]
                    end = end + corners[f][2 + o : 3 + o]
                value = value + jnp.where(row == 0, top, 0.0)
                value = value + jnp.where(row == rows - 1, end, 0.0)
                start = (s * frames + f) * rows
                image[start : start + rows, here] = value.astype(jnp.bfloat16)
    size = slices * frames * rows
    for start in range(0, size, 512):
        stop = min(start + 512, size)
        out[:, start:stop] = lax.dot_general(
            table[...], image[start:stop, :], NT, preferred_element_type=jnp.float32
        ).astype(jnp.bfloat16)
    rest = out.shape[1] - size
    if rest:
        lane = lax.broadcasted_iota(jnp.int32, (out.shape[0], rest), 1)
        out[:, size:] = jnp.where(lane == 0, note[0, 0], 0.0).astype(jnp.bfloat16)


def image_to_hybrid(main, added, table, note, lanes):
    slices, frames, rows, twice = main.shape
    return pl.pallas_call(
        image_kernel,
        in_specs=[pl.BlockSpec(memory_space=pltpu.VMEM)] * (2 + EDGES)
        + [pl.BlockSpec(memory_space=pltpu.SMEM)],
        out_shape=jax.ShapeDtypeStruct((twice, lanes), jnp.bfloat16),
        scratch_shapes=[pltpu.VMEM((slices * frames * rows, twice), jnp.bfloat16)],
        compiler_params=pltpu.CompilerParams(vmem_limit_bytes=VMEM),
        cost_estimate=expected(slices / 2),
        name="image_to_hybrid",
    )(main, *map(in_vmem, added), table, note)


def grad_image_kernel(hybrid, table, out, low, high, first, last, sums):
    slices, _, frames, rows, columns = out.shape
    sums[...] = jnp.zeros_like(sums)
    for s in range(slices):
        size = frames * rows
        start = s * size // 128 * 128
        stop = -(-(s + 1) * size // 128) * 128
        value = lax.dot_general(
            hybrid[:, start:stop], table[...], TN, preferred_element_type=jnp.float32
        ).astype(jnp.bfloat16)
        for c in range(2):
            tops, ends = [], []
            for f in range(frames):
                at = s * size + f * rows - start
                piece = value[at : at + rows, c * columns : (c + 1) * columns]
                out[s, c, f] = piece
                if f == 0:
                    low[s, c] = piece
                if f == frames - 1:
                    high[s, c] = piece
                wide = piece.astype(jnp.float32)
                sums[c : c + 1, :] += jnp.sum(wide, axis=0, keepdims=True)
                tops.append(wide[0:1])
                ends.append(wide[rows - 1 :])
            first[s, c : c + 1, :] = jnp.concatenate(tops, axis=1)
            last[s, c : c + 1, :] = jnp.concatenate(ends, axis=1)


def hybrid_to_grad(hybrid, table, shape):
    slices, channels, frames, rows, columns = shape
    edge_frame = jax.ShapeDtypeStruct((slices, channels, rows, columns), jnp.bfloat16)
    edge_row = jax.ShapeDtypeStruct((slices, channels, frames * columns), jnp.float32)
    return pl.pallas_call(
        grad_image_kernel,
        out_shape=[
            jax.ShapeDtypeStruct(shape, jnp.bfloat16),
            edge_frame,
            edge_frame,
            edge_row,
            edge_row,
            jax.ShapeDtypeStruct((2, columns), jnp.float32),
        ],
        compiler_params=pltpu.CompilerParams(vmem_limit_bytes=VMEM),
        cost_estimate=expected(slices / 2),
        name="hybrid_to_grad",
    )(in_vmem(hybrid), table)


def chunk_table():
    index = np.arange(512).reshape(4, 4, 32)
    return jnp.asarray(np.eye(512)[index.transpose(1, 0, 2).reshape(-1)], jnp.bfloat16)


def beside(pieces):
    return jnp.concatenate(pieces, axis=1)


def weighed(weights, arrays):
    total = weights[0] * arrays[0]
    for weight, array in zip(weights[1:], arrays[1:]):
        total = total + weight * array
    return total


def kspace_slice(
    k, frames_here, n_af, kspace, measured, target, sampled, share, scale, grads, loss_lanes
):
    frames = n_af * frames_here
    near = [range(max(t - 2, 0), min(t + 3, frames)) for t in range(frames)]

    def rows_of(t):
        start = (k * frames + (t % frames_here) * n_af + t // frames_here) * 8
        return slice(start, start + 8)

    factor = scale[...]
    free = [1.0 - sampled[t] for t in range(frames)]
    kept = [sampled[t] * measured[k, t] for t in range(frames)]
    filled = [kept[t] + free[t] * kspace[rows_of(t)] for t in range(frames)]
    slopes = []
    terms = None
    for t in range(frames):
        shared = weighed([share[t, s] for s in near[t]], [filled[s] for s in near[t]])
        differ = kept[t] + free[t] * shared - target[k, t]
        square = differ * differ + 1.0
        inverse = lax.rsqrt(square)
        term = free[t] * (square * inverse - 1.0)
        terms = term if terms is None else terms + term
        slopes.append(free[t] * differ * inverse * factor)
    loss_lanes[...] += terms
    for s in range(frames):
        grad = weighed([share[t, s] for t in near[s]], [slopes[t] for t in near[s]])
        grads[rows_of(s), :] = free[s] * grad


def kspace_kernel(
    frames_here, factor, received, measured, target, sampled, share, table, chunks,
    out, loss, count, spectrum, grads, loss_lanes, scale,
):
    groups, _, lanes = received.shape
    pairs, n_af, _, twice = spectrum.shape
    rows = twice // 2
    n_row = groups // n_af
    step = pl.program_id(0)
    tiles = lanes // 128
    size = out.shape[1]

    @pl.when(step == 0)
    def _():
        loss_lanes[...] = jnp.zeros_like(loss_lanes)
        last = slice((tiles - 1) * 128, lanes)
        notes = sum(received[group, 0:size, last].astype(jnp.float32) for group in range(groups))
        at = pairs * (128 // 4) - (tiles - 1) * 128
        total = notes[0:1, at : at + 1] * factor
        count[...] = jnp.broadcast_to(total, count.shape)
        scale[...] = jnp.broadcast_to(1.0 / total, scale.shape)
        for h in range(n_row // 4):
            for af in range(n_af):
                source = [
                    beside(
                        [
                            received[af * n_row + h * 4 + m, :, tile * 128 : (tile + 1) * 128]
                            for m in range(4)
                        ]
                    )
                    for tile in range(tiles)
                ]
                moved = jnp.dot(
                    jnp.concatenate(source, axis=0),
                    chunks[...],
                    preferred_element_type=jnp.float32,
                )
                for pair in range(pairs):
                    tile, k = pair // 4, pair % 4
                    for c in range(2):
                        at = c * rows + h * 128
                        start = tile * size + c * 8
                        spectrum[pair, af, :, at : at + 128] = moved[
                            start : start + 8, k * 128 : (k + 1) * 128
                        ]

    each = measured.shape[0]
    here = pl.ds(step * each * frames_here, each * frames_here)
    block = spectrum[here].reshape(grads.shape).astype(jnp.bfloat16)
    kspace = jnp.dot(block, table[...], preferred_element_type=jnp.float32)
    for k in range(each):
        kspace_slice(
            k, frames_here, n_af, kspace, measured, target, sampled, share, scale, grads, loss_lanes
        )
    back = lax.dot_general(
        grads[...].astype(jnp.bfloat16), table[...], NT, preferred_element_type=jnp.float32
    )
    spectrum[here] = back.reshape(each * frames_here, n_af, 8, twice)

    @pl.when(step == pl.num_programs(0) - 1)
    def _():
        loss[...] = loss_lanes[...]

        for h in range(n_row // 4):
            for af in range(n_af):
                source = []
                for tile in range(tiles):
                    four = []
                    for k in range(4):
                        pair = min(tile * 4 + k, pairs - 1)
                        both = [
                            spectrum[pair, af, :, c * rows + h * 128 : c * rows + h * 128 + 128]
                            for c in range(2)
                        ]
                        four.append(jnp.concatenate(both, axis=0).astype(jnp.bfloat16))
                    source.append(beside(four))
                moved = jnp.dot(
                    jnp.concatenate(source, axis=0),
                    chunks[...],
                    preferred_element_type=jnp.float32,
                ).astype(jnp.bfloat16)
                for m in range(4):
                    for tile in range(tiles):
                        out[af * n_row + h * 4 + m, :, tile * 128 : (tile + 1) * 128] = moved[
                            tile * size : (tile + 1) * size, m * 128 : (m + 1) * 128
                        ]


def kspace_step(received, measured, target, sampled, share, table, frames_here, factor):
    _, frames, lines, twice = measured.shape
    slices = measured.shape[0]
    n_af = frames // frames_here
    each = 2 if slices % 2 == 0 else 1
    chunks = chunk_table()

    def some(shape):
        return pl.BlockSpec((each,) + tuple(shape[1:]), lambda s: (s, 0, 0, 0))

    return pl.pallas_call(
        functools.partial(kspace_kernel, frames_here, factor),
        grid=(slices // each,),
        in_specs=[
            pl.BlockSpec(memory_space=pltpu.VMEM),
            some(measured.shape),
            some(target.shape),
            whole(sampled.shape),
            pl.BlockSpec(memory_space=pltpu.SMEM),
            whole(table.shape),
            whole(chunks.shape),
        ],
        out_specs=[whole(received.shape), whole((lines, twice)), whole((8, 128))],
        out_shape=[
            jax.ShapeDtypeStruct(received.shape, jnp.bfloat16),
            jax.ShapeDtypeStruct((lines, twice), jnp.float32),
            jax.ShapeDtypeStruct((8, 128), jnp.float32),
        ],
        scratch_shapes=[
            pltpu.VMEM((slices * frames_here, n_af, lines, twice), jnp.float32),
            pltpu.VMEM((each * frames * lines, twice), jnp.float32),
            pltpu.VMEM((lines, twice), jnp.float32),
            pltpu.VMEM((lines, twice), jnp.float32),
        ],
        compiler_params=pltpu.CompilerParams(vmem_limit_bytes=VMEM),
        cost_estimate=expected(3 * slices),
        name="kspace",
    )(in_vmem(received), measured, target, sampled, share, table, chunks)


def middle_plain(main, added, measured, target, sampled, share, table_y, table_x):
    highest = lax.Precision.HIGHEST
    slices, frames_here, rows_here, twice = main.shape
    count = lax.psum(jnp.sum(1.0 - sampled) * (2.0 * slices * measured.shape[3] / 2), AXES)
    columns = twice // 2
    frames, lines = measured.shape[1:3]
    rows = measured.shape[3] // 2
    table_y = jnp.asarray(table_y, jnp.bfloat16)
    table_x = jnp.asarray(table_x, jnp.bfloat16)
    image = main.reshape(slices, frames_here, rows_here, 2, columns)
    below, above, upper, lower, *corners = (one.astype(jnp.float32) for one in added)
    image = image.at[:, 0].add(below.transpose(0, 2, 1, 3))
    image = image.at[:, frames_here - 1].add(above.transpose(0, 2, 1, 3))
    for at, line in ((0, upper), (rows_here - 1, lower)):
        line = line[:, :, columns:-columns].reshape(slices, 2, frames_here, columns)
        image = image.at[:, :, at].add(line.transpose(0, 2, 1, 3))
    for f, corner in ((0, corners[0]), (frames_here - 1, corners[1])):
        image = image.at[:, f, 0].add(corner[:, 0:2])
        image = image.at[:, f, rows_here - 1].add(corner[:, 2:4])
    flat = image.reshape(slices, frames_here, rows_here, twice).astype(jnp.bfloat16)
    hybrid = jnp.dot(flat, table_y, preferred_element_type=jnp.float32).astype(jnp.bfloat16)
    hybrid = hybrid.reshape(slices, frames_here, rows_here, 2, columns)
    part = lax.all_to_all(hybrid, "af", split_axis=4, concat_axis=1, tiled=True)
    spread = lax.all_to_all(part, "row", split_axis=4, concat_axis=2, tiled=True)
    spectrum = jnp.transpose(spread, (0, 1, 4, 3, 2)).reshape(slices, frames, lines, 2 * rows)
    kspace = jnp.dot(spectrum, table_x, preferred_element_type=jnp.float32)
    mask = sampled[None, :, :, None]
    filled = mask * measured + (1.0 - mask) * kspace
    shared = jnp.einsum("ts,bslk->btlk", share, filled, precision=highest)
    differ = mask * measured + (1.0 - mask) * shared - target
    root = jnp.sqrt(differ * differ + 1.0)
    loss = jnp.sum((1.0 - mask) * (root - 1.0))
    slope = (1.0 - mask) * differ / root / count
    grad = (1.0 - mask) * jnp.einsum("ts,btlk->bslk", share, slope, precision=highest)
    back = jnp.dot(grad, table_x.T.astype(jnp.float32), precision=highest).astype(jnp.bfloat16)
    back = jnp.transpose(back.reshape(slices, frames, lines, 2, rows), (0, 1, 4, 3, 2))
    part = lax.all_to_all(back, "row", split_axis=2, concat_axis=4, tiled=True)
    whole_rows = lax.all_to_all(part, "af", split_axis=1, concat_axis=4, tiled=True)
    grad = jnp.dot(
        whole_rows.reshape(slices, frames_here, rows_here, twice),
        table_y.T,
        preferred_element_type=jnp.float32,
    ).reshape(slices, frames_here, rows_here, 2, columns)
    grad = jnp.transpose(grad, (0, 3, 1, 2, 4)).astype(jnp.bfloat16)
    return loss, jnp.broadcast_to(count, (8, 128)), grad, jnp.sum(grad.astype(jnp.float32), axis=(0, 2, 3, 4))


def update_kernel(parts, *refs):
    count, *ins = refs[parts : parts + 13]
    outs = refs[parts + 13 :]
    total = refs[0][...]
    if parts == 4:
        total = (total + refs[1][...]) + (refs[2][...] + refs[3][...])
    *outs, loss, unsampled = outs
    taps, width = ins[0].shape
    turned = total[0:width, :].T

    def step(kind, at, grad):
        master, first, second, smooth = (one[at] for one in ins[kind::3])
        rate = (rate_in, rate_out, rate_bias)[kind]
        first, second, master = adam_step(master, grad, first, second, rate)
        average = average_keep * smooth + (1.0 - average_keep) * master
        for out, value in zip(outs[kind::3], (first, second, master, average, master)):
            out[at] = value.astype(out.dtype)

    step(0, ..., turned[0:taps, :])
    for tap in range(ins[1].shape[0]):
        start = PACKED // 2 + 2 * tap
        step(1, tap, turned[start : start + 2, :])
    step(2, (slice(0, 1), slice(0, width)), turned[54:55, :])
    step(2, (slice(0, 1), slice(width, width + 2)), total[width : width + 1, 1:3])
    loss[...] = total[width : width + 1, 0:1]
    unsampled[...] = count[0:1, 0:1]


def update(parts, count, weights, firsts, seconds, smooths):
    arrays = [*weights, *firsts, *seconds, *smooths]
    turn = {1: lambda one: one.reshape(1, -1), 2: jnp.transpose, 3: lambda one: one}
    arrays = [turn[one.ndim](one) for one in arrays]
    kinds = [jnp.float32] * 4 + [jnp.bfloat16]
    *outs, loss, unsampled = pl.pallas_call(
        functools.partial(update_kernel, len(parts)),
        out_shape=[jax.ShapeDtypeStruct(one.shape, kind) for kind in kinds for one in arrays[:3]]
        + [jax.ShapeDtypeStruct((1, 1), jnp.float32)] * 2,
        name="update",
    )(*map(in_vmem, parts), count, *arrays)
    back = (jnp.transpose, lambda one: one, lambda one: one.reshape(-1))
    return loss[0, 0], unsampled[0, 0], *[back[k % 3](one) for k, one in enumerate(outs)]


def middle_fast(
    main, added, note, measured, target, sampled, window_half, table_y, table_x, between, after
):
    devices = lax.axis_size("af") * lax.axis_size("row")
    slices, frames_here, rows, twice = main.shape
    lines, readout = measured.shape[2:]
    size = slices * frames_here * rows
    order = np.arange(twice).reshape(2, devices, lines).transpose(1, 0, 2).reshape(-1)
    permuted = jnp.asarray(np.ascontiguousarray(table_y[:, order].T), jnp.bfloat16)
    mask = jnp.broadcast_to(sampled[:, :, None], sampled.shape + (readout,))
    share = share_matrix(window_half, measured.shape[1])
    mask, share, *added = lax.optimization_barrier((mask, share, *added))
    lanes = (size // 128 + 1) * 128
    hybrid = image_to_hybrid(main, added, permuted, note, lanes)
    received = lax.all_to_all(
        hybrid.reshape(devices, 2 * lines, lanes), AXES, 0, 0, tiled=True
    )
    first = between(hybrid)
    received, first = lax.optimization_barrier((received, first))
    back, loss, count = kspace_step(
        received, measured, target, mask, share, jnp.asarray(table_x, jnp.bfloat16),
        frames_here, 1.0 * slices * readout,
    )
    returned = lax.all_to_all(back, AXES, 0, 0, tiled=True)
    second = after(back, first)
    returned, second = lax.optimization_barrier((returned, second))
    shape = (slices, 2, frames_here, rows, twice // 2)
    grad, *grad_edge, sums = hybrid_to_grad(returned.reshape(twice, lanes), permuted, shape)
    return loss, count, grad, grad_edge, sums, second


def train_step(
    image_in, measured, target, sampled, window_half, table_y, table_x, w_in, w_out, w_back, bias_out
):
    slices, _, frames_here, rows, columns = image_in.shape
    frames, lines = measured.shape[1:3]
    cut = (slices + 1) // 2
    groups = [(0, cut), (cut, slices - cut)]
    edges = image_edges(image_in, (0, slices))
    main, *part = conv_forward(image_in, edges, (0, slices), w_in, w_out, bias_out)
    note = jnp.sum(1.0 - sampled).reshape(1, 1)
    added = return_edges(*part, columns)

    def again(group, after, kept=()):
        held, _ = lax.optimization_barrier((w_in.T, after))
        return hidden_again(image_in, edges, group, held, kept)

    fits = rows == 32 and lines == 8 and lax.axis_size("row") % 4 == 0
    fits = fits and frames * lines <= 256
    if fits:
        loss, count, grad, grad_edge, sums, kept = middle_fast(
            main, added, note, measured, target, sampled, window_half, table_y, table_x,
            functools.partial(again, groups[0]), functools.partial(again, groups[1]),
        )
    else:
        loss, count, grad, sums = middle_plain(
            main, added, measured, target, sampled, share_matrix(window_half, frames),
            table_y, table_x,
        )
        flat = (slices, 2, frames_here * columns)
        grad_edge = (
            grad[:, :, 0], grad[:, :, frames_here - 1],
            grad[:, :, :, 0].reshape(flat), grad[:, :, :, rows - 1].reshape(flat),
        )
        kept = None
    around = share_edges(*grad_edge)
    if kept is not None:
        return count, conv_backward(image_in, edges, grad, around, *kept, w_back, loss, sums)
    total = 0.0
    loss, sums = loss.reshape(1, 1), sums.reshape(2, 1)
    for first, size in groups:
        own, *sides = (one[first : first + size] for one in (image_in, *edges, grad, *around))
        held, _ = lax.optimization_barrier((w_in.T, total))
        kept = hidden_again(own, sides[:EDGES], (0, size), held)
        total += conv_backward(
            own, sides[:EDGES], sides[EDGES], sides[EDGES + 1 :], *kept, w_back, loss, sums
        )
        loss, sums = 0.0 * loss, 0.0 * sums
    return count, total


def on_device(
    image_in, measured, target, line_mask, window_half, in_kernel, out_kernel, biases,
    in_moment, out_moment, bias_moment, in_square, out_square, bias_square,
    in_smooth, out_smooth, bias_smooth,
):
    slices, _, frames_here, rows_here, columns = image_in.shape
    frames = measured.shape[1]
    width = in_kernel.shape[0]
    rows = rows_here * lax.axis_size("row")
    table_y = dft_table(columns)
    table_x = dft_table(rows)
    sampled = line_mask.astype(jnp.float32)
    w_in = conv_in_weights(in_kernel, biases[:width])
    w_out = conv_out_weights(out_kernel)
    w_back = conv_back_weights(out_kernel)

    count, total = train_step(
        image_in, measured, target, sampled, window_half, table_y, table_x,
        w_in, w_out, w_back, biases,
    )
    return update(
        last_parts(sum_over(total, "row"), "af"),
        count,
        (in_kernel, out_kernel, biases),
        (in_moment, out_moment, bias_moment),
        (in_square, out_square, bias_square),
        (in_smooth, out_smooth, bias_smooth),
    )


def solution(mesh):
    in_specs = (
        P(None, None, "af", "row", None),
        P(None, None, ("af", "row"), None),
        P(None, None, ("af", "row"), None),
        P(None, ("af", "row")),
    ) + (P(),) * 13
    return jax.shard_map(
        on_device, mesh=mesh, in_specs=in_specs, out_specs=(P(),) * 17, check_vma=False
    )
```

```python
import functools
import math

import jax
import jax.numpy as jnp
import numpy as np
from jax import lax
from jax.experimental import pallas as pl
from jax.experimental.pallas import tpu as pltpu
from jax.sharding import PartitionSpec as P

STEP = 5
AXES = ("af", "row")
BLOCK = 4
WIN = 8
SIDE = 16
DEPTH = 9 * SIDE
ONES_ROW = BLOCK + 2
PACKED = 128
EDGES = 6
BIAS_LANE = WIN - 1
VMEM = 60 * 2**20
GELU = math.sqrt(2.0 / math.pi)
CUBE = 0.044715

beta_first = 0.5
beta_second = 0.5
rate_in = 0.2
rate_out = 0.04
rate_bias = 0.3
decay_weight = 0.01
average_keep = 0.9
epsilon = 1e-08

NT = (((1,), (1,)), ((), ()))
TN = (((0,), (0,)), ((), ()))


def dft_table(length):
    index = np.arange(length)
    phase = (index[:, None] * index[None, :] % length) * (2.0 * math.pi / length)
    cosine = np.cos(phase) / math.sqrt(length)
    sine = np.sin(phase) / math.sqrt(length)
    upper = np.concatenate([cosine, -sine], axis=1)
    lower = np.concatenate([sine, cosine], axis=1)
    return np.concatenate([upper, lower], axis=0).astype(np.float32)


def share_matrix(window_half, frames):
    index = jnp.arange(frames, dtype=jnp.int32)
    inside = (jnp.abs(index[None, :] - index[:, None]) <= window_half[:, None]).astype(jnp.float32)
    return inside / jnp.sum(inside, axis=1, keepdims=True)


def adam_step(master, grad, first, second, rate):
    first_new = beta_first * first + (1.0 - beta_first) * grad
    second_new = beta_second * second + (1.0 - beta_second) * grad * grad
    first_hat = first_new / (1.0 - beta_first**STEP)
    second_hat = second_new / (1.0 - beta_second**STEP)
    master_new = master - rate * (
        first_hat / (jnp.sqrt(second_hat) + epsilon) + decay_weight * master
    )
    return (first_new, second_new, master_new)


def conv_in_weights(kernel, bias):
    width = kernel.shape[0]
    taps = kernel.astype(jnp.bfloat16).astype(jnp.float32).reshape(width, 2, 3, 3, 3)
    rows = []
    for j in range(BLOCK):
        row = jnp.pad(taps, ((0, 0), (0, 0), (0, 0), (j, WIN - 3 - j), (0, 0)))
        rows.append(row.transpose(0, 2, 4, 1, 3))
    spread = jnp.stack(rows)
    high = lax.reduce_precision(bias, 8, 7)
    rest = bias - high
    middle = lax.reduce_precision(rest, 8, 7)
    parts = jnp.stack([high, middle, rest - middle], axis=1)
    spread = spread.at[:, :, :, 0, 0, ONES_ROW].set(jnp.broadcast_to(parts, (BLOCK, width, 3)))
    return 0.5 * spread.reshape(BLOCK * width, DEPTH)


def conv_out_weights(kernel):
    width = kernel.shape[2]
    taps = kernel.astype(jnp.bfloat16).reshape(3, 3, 3, 2, width)[:, ::-1]
    columns = []
    for j in range(BLOCK):
        column = jnp.pad(taps, ((0, 0), (j, WIN - 3 - j), (0, 0), (0, 0), (0, 0)))
        columns.append(column.transpose(0, 2, 3, 1, 4))
    return jnp.stack(columns, axis=4).reshape(DEPTH, BLOCK * width)


def conv_back_weights(kernel):
    width = kernel.shape[2]
    taps = kernel.astype(jnp.bfloat16).reshape(3, 3, 3, 2, width)[::-1, ::-1, ::-1]
    rows = []
    for j in range(BLOCK):
        row = jnp.pad(taps, ((0, 0), (j, WIN - 3 - j), (0, 0), (0, 0), (0, 0)))
        rows.append(row.transpose(0, 2, 3, 1, 4))
    return 0.5 * jnp.stack(rows, axis=4).reshape(DEPTH, BLOCK * width)


def pick_table():
    table = np.zeros((2, 256, PACKED), np.float32)
    for a, b, e, c in np.ndindex(3, 3, 3, 2):
        lane = ((a * 3 + e) * 2 + c) * WIN + b
        table[0, lane, 27 * c + 9 * a + 3 * b + e] = 1.0
        tap = 9 * (2 - a) + 3 * (2 - b) + 2 - e
        table[1, lane, PACKED // 2 + 2 * tap + c] = 1.0
    table[0, BIAS_LANE, 54] = 1.0
    return jnp.asarray(table, jnp.bfloat16)


def load_volume(volume, own, below, above, left, right, corner_below, corner_above):
    _, channels, frames, rows, columns = own.shape
    lanes = (frames + 2) * columns
    for c in range(channels):
        volume[c, rows + 8 : rows + 16, :] = jnp.zeros((8, lanes), jnp.float32)
        for t in range(frames + 2):
            if t == 0:
                piece = below[0, c]
            elif t == frames + 1:
                piece = above[0, c]
            else:
                piece = own[0, c, t - 1]
            volume[c, 8 : 8 + rows, t * columns : (t + 1) * columns] = piece.astype(jnp.float32)
    low = corner_below[0].astype(jnp.float32)
    high = corner_above[0].astype(jnp.float32)
    for side, at, line in ((0, 7, left), (1, rows + 8, right)):
        middle = line[0].astype(jnp.float32)
        for c in range(channels):
            k = 2 * side + c
            volume[c, at : at + 1, 0:columns] = low[k : k + 1]
            volume[c, at : at + 1, columns : lanes - columns] = middle[c : c + 1]
            volume[c, at : at + 1, lanes - columns :] = high[k : k + 1]


def build_windows(volume, windows, columns, ones):
    blocks, _, lanes = windows.shape
    column = lax.broadcasted_iota(jnp.int32, (SIDE, columns), 1)
    row = lax.broadcasted_iota(jnp.int32, (SIDE, columns), 0)
    zero = jnp.zeros((SIDE, columns), jnp.bfloat16)
    for block in range(blocks):
        for t in range(lanes // columns):
            here = slice(t * columns, (t + 1) * columns)
            start = 7 + BLOCK * block
            window = jnp.concatenate(
                [volume[c, start : start + WIN, here] for c in range(2)], axis=0
            ).astype(jnp.bfloat16)
            for e in range(3):
                shifted = window
                if e != 1:
                    shifted = pltpu.roll(window, (1 - e) % columns, axis=1)
                    shifted = jnp.where(column == (0 if e == 0 else columns - 1), zero, shifted)
                if ones and e == 0:
                    shifted = jnp.where(row == ONES_ROW, zero + 1.0, shifted)
                windows[block, e * SIDE : (e + 1) * SIDE, here] = shifted


def forward_kernel(own, *refs):
    each = own.shape[0]
    edges, fixed, rest = refs[:EDGES], refs[EDGES : EDGES + 3], refs[EDGES + 3 :]
    slices = []
    for k in range(each):
        sides = of_step(edges, pl.program_id(0) * each + k)
        outs = of_step(rest[:5], k)
        slices.append(forward_slice(own.at[pl.ds(k, 1)], sides, *fixed, *outs, *(one.at[k] for one in rest[5:])))
    blocks = own.shape[3] // BLOCK
    slices[0][0]()
    for k, (_, step, finish) in enumerate(slices):
        for block in range(blocks):
            step(block)
            if block == blocks // 2 and k + 1 < each:
                slices[k + 1][0]()
            if block == 0 and k:
                slices[k - 1][2]()
    slices[-1][2]()


def forward_slice(
    own, edges, w_in, w_out, bias_out, main, part_below, part_above, part_left, part_right,
    volume, windows, total, hidden, mixed, spread,
):
    _, _, frames, rows, columns = own.shape
    blocks = windows.shape[0]

    def prepare():
        load_volume(volume, own, *edges)
        build_windows(volume, windows, columns, True)

    column = lax.broadcasted_iota(jnp.int32, (SIDE, columns), 1)

    def step(block):
        for f in range(frames):
            here = slice(f * columns, (f + 1) * columns)
            patch = jnp.concatenate(
                [windows[block, :, (f + a) * columns : (f + a + 1) * columns] for a in range(3)],
                axis=0,
            )
            half = jnp.dot(w_in[...], patch, preferred_element_type=jnp.float32)
            t = jnp.tanh(half * (2.0 * GELU + (8.0 * GELU * CUBE) * (half * half)))
            hidden[:, here] = (half + half * t).astype(jnp.bfloat16)
        for f in range(frames):
            here = slice(f * columns, (f + 1) * columns)
            mixed[f] = jnp.dot(w_out[...], hidden[:, here], preferred_element_type=jnp.float32)
        for t in range(frames + 2):
            window = None
            for e in range(3):
                summed = None
                for a in range(3):
                    f = t - 2 + a
                    if 0 <= f < frames:
                        start = (a * 3 + e) * SIDE
                        piece = mixed[f, start : start + SIDE, :]
                        summed = piece if summed is None else summed + piece
                if e != 1:
                    summed = pltpu.roll(summed, (1 - e) % columns, axis=1)
                    summed = jnp.where(column == (0 if e == 0 else columns - 1), 0.0, summed)
                window = summed if window is None else window + summed
            spread[block, :, t * columns : (t + 1) * columns] = window

    def finish():
        total[...] = jnp.zeros_like(total)
        for block in range(blocks):
            for o in range(2):
                start = 7 + BLOCK * block
                total[o, start : start + WIN, :] = (
                    total[o, start : start + WIN, :] + spread[block, o * WIN : (o + 1) * WIN, :]
                )
        for o in range(2):
            for t in range(frames + 2):
                here = total[o, 8 : 8 + rows, t * columns : (t + 1) * columns]
                if t == 0:
                    part_below[0, o] = here.astype(jnp.bfloat16)
                elif t == frames + 1:
                    part_above[0, o] = here.astype(jnp.bfloat16)
                else:
                    base = volume[o, 8 : 8 + rows, t * columns : (t + 1) * columns]
                    base = base + bias_out[bias_out.shape[0] - 2 + o]
                    main[0, t - 1, :, o * columns : (o + 1) * columns] = base + here
        for at, out in ((7, part_left), (8 + rows, part_right)):
            both = [total[o, at : at + 1, :] for o in range(2)]
            out[0] = jnp.concatenate(both, axis=0).astype(jnp.bfloat16)

    return prepare, step, finish


def patches(source, block, frames, columns):
    return jnp.concatenate(
        [source[block, :, a * columns : (a + frames) * columns] for a in range(3)], axis=0
    )


def hidden_kernel(start, own, *refs):
    edges, (w_in, *_, hidden, slopes, volume, windows) = refs[:EDGES], refs[EDGES:]
    _, _, frames, rows, columns = own.shape
    load_volume(volume, own, *of_step(edges, start + pl.program_id(0)))
    build_windows(volume, windows, columns, True)

    def step(block, carry):
        patch = patches(windows, block, frames, columns)
        for f in range(frames):
            here = slice(f * columns, (f + 1) * columns)
            half = lax.dot_general(
                patch[:, here], w_in[...], TN, preferred_element_type=jnp.float32
            )
            u = half * half
            t = jnp.tanh(half * (2.0 * GELU + (8.0 * GELU * CUBE) * u))
            up = 1.0 + t
            hidden[0, block, here, :] = (half * up).astype(jnp.bfloat16)
            slope = half * (2.0 * GELU + (24.0 * GELU * CUBE) * u)
            slopes[0, block, here, :] = (up + (up * (1.0 - t)) * slope).astype(jnp.bfloat16)
        return carry

    lax.fori_loop(0, windows.shape[0], step, 0, unroll=True)


def backward_kernel(
    own, *refs,
):
    edges, grad, grad_edges = refs[:EDGES], refs[EDGES], refs[EDGES + 1 : 2 * EDGES + 1]
    (
        hidden, slopes, w_back, pick, loss, sums, out,
        volume, windows, grad_windows, grads, sum_in, sum_out,
    ) = refs[2 * EDGES + 1 :]
    _, _, frames, rows, columns = own.shape

    part = pl.program_id(1)

    @pl.when((pl.program_id(0) == 0) & (part == 0))
    def _():
        sum_in[...] = jnp.zeros_like(sum_in)
        sum_out[...] = jnp.zeros_like(sum_out)

    @pl.when(part == 0)
    def _():
        load_volume(volume, own, *of_step(edges, pl.program_id(0)))
        build_windows(volume, windows, columns, True)
        load_volume(volume, grad, *of_step(grad_edges, pl.program_id(0)))
        build_windows(volume, grad_windows, columns, False)

    blocks = hidden.shape[1]

    def step(at):
        block = part * blocks + at
        patch = patches(windows, block, frames, columns)
        grad_patch = patches(grad_windows, block, frames, columns)
        for f in range(frames):
            here = slice(f * columns, (f + 1) * columns)
            gh = lax.dot_general(
                grad_patch[:, here], w_back[...], TN, preferred_element_type=jnp.float32
            )
            grads[here, :] = (slopes[0, at, here, :].astype(jnp.float32) * gh).astype(
                jnp.bfloat16
            )
        sum_in[:DEPTH, :] += jnp.dot(patch, grads[...], preferred_element_type=jnp.float32)
        sum_out[:DEPTH, :] += jnp.dot(
            grad_patch, hidden[0, at], preferred_element_type=jnp.float32
        )

    for at in range(blocks):
        step(at)

    @pl.when((pl.program_id(0) == pl.num_programs(0) - 1) & (part == pl.num_programs(1) - 1))
    def _():
        width = sum_in.shape[1] // BLOCK
        lanes = sum_in.shape[0]
        lane = lax.broadcasted_iota(jnp.int32, (width, lanes), 1)
        picked = jnp.zeros((width, pick.shape[2]), jnp.float32)
        for index, source in enumerate((sum_in[...].T, sum_out[...].T)):
            folded = source[0:width, :]
            bias = folded
            for j in range(1, BLOCK):
                piece = source[j * width : (j + 1) * width, :]
                folded = folded + pltpu.roll(piece, lanes - j, axis=1)
                bias = bias + piece
            if index == 0:
                moved = pltpu.roll(bias, BIAS_LANE - ONES_ROW, axis=1)
                folded = jnp.where(lane == BIAS_LANE, moved, folded)
            for _ in range(3):
                piece = folded.astype(jnp.bfloat16)
                folded = folded - piece.astype(jnp.float32)
                picked = picked + jnp.dot(piece, pick[index], preferred_element_type=jnp.float32)
        out[0:width, :] = picked
        spot = lax.broadcasted_iota(jnp.int32, (8, PACKED), 1)
        both = jnp.sum(sums[...], axis=1, keepdims=True)
        values = (jnp.sum(loss[...], axis=(0, 1), keepdims=True), both[0:1], both[1:2])
        row = jnp.zeros((8, PACKED), jnp.float32)
        for k, value in enumerate(values):
            row = jnp.where(spot == k, value, row)
        out[width:, :] = row


def of_step(refs, step):
    return [ref.at[pl.ds(step, 1)] for ref in refs]


def whole(shape):
    return pl.BlockSpec(tuple(shape), lambda s: (0,) * len(shape))


def a_slice(shape, first=0):
    rest = (0,) * (len(shape) - 1)
    return pl.BlockSpec((1,) + tuple(shape[1:]), lambda s: (s + first,) + rest)


def expected(microseconds):
    return pl.CostEstimate(
        flops=int(microseconds * 1.15e9), bytes_accessed=0, transcendentals=0
    )


def conv_scratch(frames, rows, columns):
    lanes = (frames + 2) * columns
    return (
        pltpu.VMEM((2, rows + 16, lanes), jnp.float32),
        pltpu.VMEM((rows // BLOCK, 3 * SIDE, lanes), jnp.bfloat16),
    )


def conv_forward(own, edges, w_in, w_out, bias_out):
    _, _, frames, rows, columns = own.shape
    slices = own.shape[0]
    each = 2 if slices % 2 == 0 else 1

    def some(shape):
        rest = (0,) * (len(shape) - 1)
        return pl.BlockSpec((each,) + tuple(shape[1:]), lambda s: (s,) + rest)

    lanes = (frames + 2) * columns
    span = w_in.shape[0]
    volume, windows = conv_scratch(frames, rows, columns)
    out_shape = [
        jax.ShapeDtypeStruct((slices, frames, rows, 2 * columns), jnp.float32),
        jax.ShapeDtypeStruct((slices, 2, rows, columns), jnp.bfloat16),
        jax.ShapeDtypeStruct((slices, 2, rows, columns), jnp.bfloat16),
        jax.ShapeDtypeStruct((slices, 2, lanes), jnp.bfloat16),
        jax.ShapeDtypeStruct((slices, 2, lanes), jnp.bfloat16),
    ]
    return pl.pallas_call(
        forward_kernel,
        grid=(slices // each,),
        in_specs=[some(own.shape)]
        + [pl.BlockSpec(memory_space=pltpu.VMEM)] * EDGES
        + [whole(w_in.shape), whole(w_out.shape), pl.BlockSpec(memory_space=pltpu.SMEM)],
        out_specs=[some(one.shape) for one in out_shape],
        out_shape=out_shape,
        scratch_shapes=[
            pltpu.VMEM((each,) + tuple(shape), kind)
            for shape, kind in (
                (volume.shape, jnp.float32),
                (windows.shape, jnp.bfloat16),
                (volume.shape, jnp.float32),
                ((span, frames * columns), jnp.bfloat16),
                ((frames, DEPTH, columns), jnp.float32),
                ((rows // BLOCK, SIDE, lanes), jnp.float32),
            )
        ],
        compiler_params=pltpu.CompilerParams(vmem_limit_bytes=VMEM),
        cost_estimate=expected(6 * slices),
        name="conv_forward",
    )(own, *map(in_vmem, edges), w_in, w_out, bias_out)


def hidden_again(own, edges, group, w_in, kept=()):
    _, _, frames, rows, columns = own.shape
    first, slices = group
    volume, windows = conv_scratch(frames, rows, columns)
    shape = (own.shape[0], rows // BLOCK, frames * columns, w_in.shape[1])
    return pl.pallas_call(
        functools.partial(hidden_kernel, first),
        grid=(slices,),
        in_specs=[a_slice(own.shape, first)]
        + [pl.BlockSpec(memory_space=pltpu.VMEM)] * EDGES
        + [whole(w_in.shape)]
        + [pl.BlockSpec(memory_space=pl.ANY)] * len(kept),
        out_specs=[a_slice(shape, first)] * 2,
        out_shape=[jax.ShapeDtypeStruct(shape, jnp.bfloat16)] * 2,
        input_output_aliases={2 + EDGES + k: k for k in range(len(kept))},
        scratch_shapes=[volume, windows],
        compiler_params=pltpu.CompilerParams(vmem_limit_bytes=VMEM),
        cost_estimate=expected(5 * slices),
        name="hidden_again",
    )(own, *map(in_vmem, edges), w_in, *kept)


def conv_backward(own, edges, grad, grad_edges, hidden, slopes, w_back, loss, sums):
    slices, _, frames, rows, columns = own.shape
    span = w_back.shape[1]
    volume, windows = conv_scratch(frames, rows, columns)
    total = pltpu.VMEM((2 * 128, span), jnp.float32)
    fixed = (w_back, pick_table(), loss, sums)
    out_shape = jax.ShapeDtypeStruct((span // BLOCK + 8, PACKED), jnp.float32)
    sides = [pl.BlockSpec(memory_space=pltpu.VMEM)] * EDGES
    here = (own, *map(in_vmem, edges), grad, *map(in_vmem, grad_edges))
    blocks = rows // BLOCK
    parts = 1

    def of_slice(shape):
        rest = (0,) * (len(shape) - 1)
        return pl.BlockSpec((1,) + tuple(shape[1:]), lambda s, part: (s,) + rest)

    def part_of_slice(shape):
        size = (1, blocks // parts) + tuple(shape[2:])
        return pl.BlockSpec(size, lambda s, part: (s, part, 0, 0))

    def all_of(shape):
        return pl.BlockSpec(tuple(shape), lambda s, part: (0,) * len(shape))

    return pl.pallas_call(
        backward_kernel,
        grid=(slices, parts),
        in_specs=[of_slice(own.shape), *sides, of_slice(grad.shape), *sides]
        + [part_of_slice(one.shape) for one in (hidden, slopes)]
        + [all_of(one.shape) for one in fixed],
        out_specs=all_of(out_shape.shape),
        out_shape=out_shape,
        scratch_shapes=[
            volume,
            windows,
            windows,
            pltpu.VMEM((frames * columns, span), jnp.bfloat16),
            total,
            total,
        ],
        compiler_params=pltpu.CompilerParams(vmem_limit_bytes=VMEM),
        cost_estimate=expected(5 * slices),
        name="conv_backward",
    )(*here, hidden, slopes, *fixed)


def last_parts(array, axis):
    if lax.axis_size(axis) != 4:
        return [sum_over(array, axis)]
    others = [
        lax.ppermute(array, axis, [(i, i ^ k) for i in range(4)]) for k in (1, 2, 3)
    ]
    return [array, *others]


def in_vmem(array):
    return pltpu.with_memory_space_constraint(array, pltpu.VMEM)


def along(axis, step):
    count = lax.axis_size(axis)
    return [(i, i + step) for i in range(count) if 0 <= i + step < count]


def sum_over(array, axis):
    size = lax.axis_size(axis)
    if size & (size - 1):
        return lax.psum(array, axis)

    def other(values, bits):
        return lax.ppermute(values, axis, [(i, i ^ bits) for i in range(size)])

    bit = 1
    if size.bit_length() % 2 == 0:
        array = array + other(array, bit)
        bit = 2
    while bit < size:
        one, two, three = (other(array, bit * k) for k in (1, 2, 3))
        array = (array + one) + (two + three)
        bit *= 4
    return array


def corners_along(left, right, columns):
    both = jnp.concatenate([left, right], axis=1)
    lanes = both.shape[2]
    below = lax.ppermute(both[:, :, lanes - columns :], "af", along("af", 1))
    above = lax.ppermute(both[:, :, :columns], "af", along("af", -1))
    return below, above


def share_edges(low, high, first, last):
    left = lax.ppermute(last, "row", along("row", 1))
    right = lax.ppermute(first, "row", along("row", -1))
    below = lax.ppermute(high, "af", along("af", 1))
    above = lax.ppermute(low, "af", along("af", -1))
    return below, above, left, right, *corners_along(left, right, low.shape[3])


def image_edges(image, group):
    start, slices = group
    part = image[start : start + slices]
    _, _, frames, rows, columns = part.shape
    flat = (slices, 2, frames * columns)
    return share_edges(
        part[:, :, 0], part[:, :, frames - 1],
        part[:, :, :, 0].reshape(flat), part[:, :, :, rows - 1].reshape(flat),
    )


def return_edges(part_below, part_above, part_left, part_right, columns):
    from_above = lax.ppermute(part_below, "af", along("af", -1))
    from_below = lax.ppermute(part_above, "af", along("af", 1))
    lower = lax.ppermute(part_left, "row", along("row", -1))
    upper = lax.ppermute(part_right, "row", along("row", 1))
    corner_below, corner_above = corners_along(upper, lower, columns)
    return from_below, from_above, upper, lower, corner_below, corner_above


def image_kernel(
    main, from_below, from_above, upper, lower, corner_below, corner_above,
    table, note, out, image,
):
    slices, frames, rows, twice = main.shape
    columns = twice // 2
    row = lax.broadcasted_iota(jnp.int32, (rows, columns), 0)
    for s in range(slices):
        tops = upper[s].astype(jnp.float32)
        ends = lower[s].astype(jnp.float32)
        corners = {
            0: corner_below[s].astype(jnp.float32),
            frames - 1: corner_above[s].astype(jnp.float32),
        }
        for f in range(frames):
            at = slice((f + 1) * columns, (f + 2) * columns)
            for o in range(2):
                here = slice(o * columns, (o + 1) * columns)
                value = main[s, f, :, here]
                if f == 0:
                    value = value + from_below[s, o].astype(jnp.float32)
                if f == frames - 1:
                    value = value + from_above[s, o].astype(jnp.float32)
                top, end = tops[o : o + 1, at], ends[o : o + 1, at]
                if f in corners:
                    top = top + corners[f][o : o + 1]
                    end = end + corners[f][2 + o : 3 + o]
                value = value + jnp.where(row == 0, top, 0.0)
                value = value + jnp.where(row == rows - 1, end, 0.0)
                start = (s * frames + f) * rows
                image[start : start + rows, here] = value.astype(jnp.bfloat16)
    size = slices * frames * rows
    for start in range(0, size, 512):
        stop = min(start + 512, size)
        out[:, start:stop] = lax.dot_general(
            table[...], image[start:stop, :], NT, preferred_element_type=jnp.float32
        ).astype(jnp.bfloat16)
    rest = out.shape[1] - size
    if rest:
        lane = lax.broadcasted_iota(jnp.int32, (out.shape[0], rest), 1)
        out[:, size:] = jnp.where(lane == 0, note[0, 0], 0.0).astype(jnp.bfloat16)


def image_to_hybrid(main, added, table, note, lanes):
    slices, frames, rows, twice = main.shape
    return pl.pallas_call(
        image_kernel,
        in_specs=[pl.BlockSpec(memory_space=pltpu.VMEM)] * (2 + EDGES)
        + [pl.BlockSpec(memory_space=pltpu.SMEM)],
        out_shape=jax.ShapeDtypeStruct((twice, lanes), jnp.bfloat16),
        scratch_shapes=[pltpu.VMEM((slices * frames * rows, twice), jnp.bfloat16)],
        compiler_params=pltpu.CompilerParams(vmem_limit_bytes=VMEM),
        cost_estimate=expected(slices / 2),
        name="image_to_hybrid",
    )(main, *map(in_vmem, added), table, note)


def grad_image_kernel(hybrid, table, out, low, high, first, last, sums):
    slices, _, frames, rows, columns = out.shape
    sums[...] = jnp.zeros_like(sums)
    for s in range(slices):
        size = frames * rows
        start = s * size // 128 * 128
        stop = -(-(s + 1) * size // 128) * 128
        value = lax.dot_general(
            hybrid[:, start:stop], table[...], TN, preferred_element_type=jnp.float32
        ).astype(jnp.bfloat16)
        for c in range(2):
            tops, ends = [], []
            for f in range(frames):
                at = s * size + f * rows - start
                piece = value[at : at + rows, c * columns : (c + 1) * columns]
                out[s, c, f] = piece
                if f == 0:
                    low[s, c] = piece
                if f == frames - 1:
                    high[s, c] = piece
                wide = piece.astype(jnp.float32)
                sums[c : c + 1, :] += jnp.sum(wide, axis=0, keepdims=True)
                tops.append(wide[0:1])
                ends.append(wide[rows - 1 :])
            first[s, c : c + 1, :] = jnp.concatenate(tops, axis=1)
            last[s, c : c + 1, :] = jnp.concatenate(ends, axis=1)


def hybrid_to_grad(hybrid, table, shape):
    slices, channels, frames, rows, columns = shape
    edge_frame = jax.ShapeDtypeStruct((slices, channels, rows, columns), jnp.bfloat16)
    edge_row = jax.ShapeDtypeStruct((slices, channels, frames * columns), jnp.float32)
    return pl.pallas_call(
        grad_image_kernel,
        out_shape=[
            jax.ShapeDtypeStruct(shape, jnp.bfloat16),
            edge_frame,
            edge_frame,
            edge_row,
            edge_row,
            jax.ShapeDtypeStruct((2, columns), jnp.float32),
        ],
        compiler_params=pltpu.CompilerParams(vmem_limit_bytes=VMEM),
        cost_estimate=expected(slices / 2),
        name="hybrid_to_grad",
    )(in_vmem(hybrid), table)


def chunk_table():
    index = np.arange(512).reshape(4, 4, 32)
    return jnp.asarray(np.eye(512)[index.transpose(1, 0, 2).reshape(-1)], jnp.bfloat16)


def beside(pieces):
    return jnp.concatenate(pieces, axis=1)


def weighed(weights, arrays):
    total = weights[0] * arrays[0]
    for weight, array in zip(weights[1:], arrays[1:]):
        total = total + weight * array
    return total


def kspace_slice(
    k, frames_here, n_af, kspace, measured, target, sampled, share, scale, grads, loss_lanes
):
    frames = n_af * frames_here
    near = [range(max(t - 2, 0), min(t + 3, frames)) for t in range(frames)]

    def rows_of(t):
        start = (k * frames + (t % frames_here) * n_af + t // frames_here) * 8
        return slice(start, start + 8)

    factor = scale[...]
    free = [1.0 - sampled[t] for t in range(frames)]
    kept = [sampled[t] * measured[k, t] for t in range(frames)]
    filled = [kept[t] + free[t] * kspace[rows_of(t)] for t in range(frames)]
    slopes = []
    terms = None
    for t in range(frames):
        shared = weighed([share[t, s] for s in near[t]], [filled[s] for s in near[t]])
        differ = kept[t] + free[t] * shared - target[k, t]
        square = differ * differ + 1.0
        inverse = lax.rsqrt(square)
        term = free[t] * (square * inverse - 1.0)
        terms = term if terms is None else terms + term
        slopes.append(free[t] * differ * inverse * factor)
    loss_lanes[...] += terms
    for s in range(frames):
        grad = weighed([share[t, s] for t in near[s]], [slopes[t] for t in near[s]])
        grads[rows_of(s), :] = free[s] * grad


def kspace_kernel(
    frames_here, factor, received, measured, target, sampled, share, table, chunks,
    out, loss, count, spectrum, grads, loss_lanes, scale,
):
    groups, _, lanes = received.shape
    pairs, n_af, _, twice = spectrum.shape
    rows = twice // 2
    n_row = groups // n_af
    step = pl.program_id(0)
    tiles = lanes // 128
    size = out.shape[1]

    @pl.when(step == 0)
    def _():
        loss_lanes[...] = jnp.zeros_like(loss_lanes)
        last = slice((tiles - 1) * 128, lanes)
        notes = sum(received[group, 0:size, last].astype(jnp.float32) for group in range(groups))
        at = pairs * (128 // 4) - (tiles - 1) * 128
        total = notes[0:1, at : at + 1] * factor
        count[...] = jnp.broadcast_to(total, count.shape)
        scale[...] = jnp.broadcast_to(1.0 / total, scale.shape)
        for h in range(n_row // 4):
            for af in range(n_af):
                source = [
                    beside(
                        [
                            received[af * n_row + h * 4 + m, :, tile * 128 : (tile + 1) * 128]
                            for m in range(4)
                        ]
                    )
                    for tile in range(tiles)
                ]
                moved = jnp.dot(
                    jnp.concatenate(source, axis=0),
                    chunks[...],
                    preferred_element_type=jnp.float32,
                )
                for pair in range(pairs):
                    tile, k = pair // 4, pair % 4
                    for c in range(2):
                        at = c * rows + h * 128
                        start = tile * size + c * 8
                        spectrum[pair, af, :, at : at + 128] = moved[
                            start : start + 8, k * 128 : (k + 1) * 128
                        ]

    each = measured.shape[0]
    here = pl.ds(step * each * frames_here, each * frames_here)
    block = spectrum[here].reshape(grads.shape).astype(jnp.bfloat16)
    kspace = jnp.dot(block, table[...], preferred_element_type=jnp.float32)
    for k in range(each):
        kspace_slice(
            k, frames_here, n_af, kspace, measured, target, sampled, share, scale, grads, loss_lanes
        )
    back = lax.dot_general(
        grads[...].astype(jnp.bfloat16), table[...], NT, preferred_element_type=jnp.float32
    )
    spectrum[here] = back.reshape(each * frames_here, n_af, 8, twice)

    @pl.when(step == pl.num_programs(0) - 1)
    def _():
        loss[...] = loss_lanes[...]

        for h in range(n_row // 4):
            for af in range(n_af):
                source = []
                for tile in range(tiles):
                    four = []
                    for k in range(4):
                        pair = min(tile * 4 + k, pairs - 1)
                        both = [
                            spectrum[pair, af, :, c * rows + h * 128 : c * rows + h * 128 + 128]
                            for c in range(2)
                        ]
                        four.append(jnp.concatenate(both, axis=0).astype(jnp.bfloat16))
                    source.append(beside(four))
                moved = jnp.dot(
                    jnp.concatenate(source, axis=0),
                    chunks[...],
                    preferred_element_type=jnp.float32,
                ).astype(jnp.bfloat16)
                for m in range(4):
                    for tile in range(tiles):
                        out[af * n_row + h * 4 + m, :, tile * 128 : (tile + 1) * 128] = moved[
                            tile * size : (tile + 1) * size, m * 128 : (m + 1) * 128
                        ]


def kspace_step(received, measured, target, sampled, share, table, frames_here, factor):
    _, frames, lines, twice = measured.shape
    slices = measured.shape[0]
    n_af = frames // frames_here
    each = 2 if slices % 2 == 0 else 1
    chunks = chunk_table()

    def some(shape):
        return pl.BlockSpec((each,) + tuple(shape[1:]), lambda s: (s, 0, 0, 0))

    return pl.pallas_call(
        functools.partial(kspace_kernel, frames_here, factor),
        grid=(slices // each,),
        in_specs=[
            pl.BlockSpec(memory_space=pltpu.VMEM),
            some(measured.shape),
            some(target.shape),
            whole(sampled.shape),
            pl.BlockSpec(memory_space=pltpu.SMEM),
            whole(table.shape),
            whole(chunks.shape),
        ],
        out_specs=[whole(received.shape), whole((lines, twice)), whole((8, 128))],
        out_shape=[
            jax.ShapeDtypeStruct(received.shape, jnp.bfloat16),
            jax.ShapeDtypeStruct((lines, twice), jnp.float32),
            jax.ShapeDtypeStruct((8, 128), jnp.float32),
        ],
        scratch_shapes=[
            pltpu.VMEM((slices * frames_here, n_af, lines, twice), jnp.float32),
            pltpu.VMEM((each * frames * lines, twice), jnp.float32),
            pltpu.VMEM((lines, twice), jnp.float32),
            pltpu.VMEM((lines, twice), jnp.float32),
        ],
        compiler_params=pltpu.CompilerParams(vmem_limit_bytes=VMEM),
        cost_estimate=expected(3 * slices),
        name="kspace",
    )(in_vmem(received), measured, target, sampled, share, table, chunks)


def middle_plain(main, added, measured, target, sampled, share, table_y, table_x):
    highest = lax.Precision.HIGHEST
    slices, frames_here, rows_here, twice = main.shape
    count = lax.psum(jnp.sum(1.0 - sampled) * (2.0 * slices * measured.shape[3] / 2), AXES)
    columns = twice // 2
    frames, lines = measured.shape[1:3]
    rows = measured.shape[3] // 2
    table_y = jnp.asarray(table_y, jnp.bfloat16)
    table_x = jnp.asarray(table_x, jnp.bfloat16)
    image = main.reshape(slices, frames_here, rows_here, 2, columns)
    below, above, upper, lower, *corners = (one.astype(jnp.float32) for one in added)
    image = image.at[:, 0].add(below.transpose(0, 2, 1, 3))
    image = image.at[:, frames_here - 1].add(above.transpose(0, 2, 1, 3))
    for at, line in ((0, upper), (rows_here - 1, lower)):
        line = line[:, :, columns:-columns].reshape(slices, 2, frames_here, columns)
        image = image.at[:, :, at].add(line.transpose(0, 2, 1, 3))
    for f, corner in ((0, corners[0]), (frames_here - 1, corners[1])):
        image = image.at[:, f, 0].add(corner[:, 0:2])
        image = image.at[:, f, rows_here - 1].add(corner[:, 2:4])
    flat = image.reshape(slices, frames_here, rows_here, twice).astype(jnp.bfloat16)
    hybrid = jnp.dot(flat, table_y, preferred_element_type=jnp.float32).astype(jnp.bfloat16)
    hybrid = hybrid.reshape(slices, frames_here, rows_here, 2, columns)
    part = lax.all_to_all(hybrid, "af", split_axis=4, concat_axis=1, tiled=True)
    spread = lax.all_to_all(part, "row", split_axis=4, concat_axis=2, tiled=True)
    spectrum = jnp.transpose(spread, (0, 1, 4, 3, 2)).reshape(slices, frames, lines, 2 * rows)
    kspace = jnp.dot(spectrum, table_x, preferred_element_type=jnp.float32)
    mask = sampled[None, :, :, None]
    filled = mask * measured + (1.0 - mask) * kspace
    shared = jnp.einsum("ts,bslk->btlk", share, filled, precision=highest)
    differ = mask * measured + (1.0 - mask) * shared - target
    root = jnp.sqrt(differ * differ + 1.0)
    loss = jnp.sum((1.0 - mask) * (root - 1.0))
    slope = (1.0 - mask) * differ / root / count
    grad = (1.0 - mask) * jnp.einsum("ts,btlk->bslk", share, slope, precision=highest)
    back = jnp.dot(grad, table_x.T.astype(jnp.float32), precision=highest).astype(jnp.bfloat16)
    back = jnp.transpose(back.reshape(slices, frames, lines, 2, rows), (0, 1, 4, 3, 2))
    part = lax.all_to_all(back, "row", split_axis=2, concat_axis=4, tiled=True)
    whole_rows = lax.all_to_all(part, "af", split_axis=1, concat_axis=4, tiled=True)
    grad = jnp.dot(
        whole_rows.reshape(slices, frames_here, rows_here, twice),
        table_y.T,
        preferred_element_type=jnp.float32,
    ).reshape(slices, frames_here, rows_here, 2, columns)
    grad = jnp.transpose(grad, (0, 3, 1, 2, 4)).astype(jnp.bfloat16)
    return loss, jnp.broadcast_to(count, (8, 128)), grad, jnp.sum(grad.astype(jnp.float32), axis=(0, 2, 3, 4))


def update_kernel(parts, *refs):
    count, *ins = refs[parts : parts + 13]
    outs = refs[parts + 13 :]
    total = refs[0][...]
    if parts == 4:
        total = (total + refs[1][...]) + (refs[2][...] + refs[3][...])
    *outs, loss, unsampled = outs
    taps, width = ins[0].shape
    turned = total[0:width, :].T

    def step(kind, at, grad):
        master, first, second, smooth = (one[at] for one in ins[kind::3])
        rate = (rate_in, rate_out, rate_bias)[kind]
        first, second, master = adam_step(master, grad, first, second, rate)
        average = average_keep * smooth + (1.0 - average_keep) * master
        for out, value in zip(outs[kind::3], (first, second, master, average, master)):
            out[at] = value.astype(out.dtype)

    step(0, ..., turned[0:taps, :])
    for tap in range(ins[1].shape[0]):
        start = PACKED // 2 + 2 * tap
        step(1, tap, turned[start : start + 2, :])
    step(2, (slice(0, 1), slice(0, width)), turned[54:55, :])
    step(2, (slice(0, 1), slice(width, width + 2)), total[width : width + 1, 1:3])
    loss[...] = total[width : width + 1, 0:1]
    unsampled[...] = count[0:1, 0:1]


def update(parts, count, weights, firsts, seconds, smooths):
    arrays = [*weights, *firsts, *seconds, *smooths]
    turn = {1: lambda one: one.reshape(1, -1), 2: jnp.transpose, 3: lambda one: one}
    arrays = [turn[one.ndim](one) for one in arrays]
    kinds = [jnp.float32] * 4 + [jnp.bfloat16]
    *outs, loss, unsampled = pl.pallas_call(
        functools.partial(update_kernel, len(parts)),
        out_shape=[jax.ShapeDtypeStruct(one.shape, kind) for kind in kinds for one in arrays[:3]]
        + [jax.ShapeDtypeStruct((1, 1), jnp.float32)] * 2,
        name="update",
    )(*map(in_vmem, parts), count, *arrays)
    back = (jnp.transpose, lambda one: one, lambda one: one.reshape(-1))
    return loss[0, 0], unsampled[0, 0], *[back[k % 3](one) for k, one in enumerate(outs)]


def middle_fast(
    main, added, note, measured, target, sampled, window_half, table_y, table_x, between, after
):
    devices = lax.axis_size("af") * lax.axis_size("row")
    slices, frames_here, rows, twice = main.shape
    lines, readout = measured.shape[2:]
    size = slices * frames_here * rows
    order = np.arange(twice).reshape(2, devices, lines).transpose(1, 0, 2).reshape(-1)
    permuted = jnp.asarray(np.ascontiguousarray(table_y[:, order].T), jnp.bfloat16)
    mask = jnp.broadcast_to(sampled[:, :, None], sampled.shape + (readout,))
    share = share_matrix(window_half, measured.shape[1])
    mask, share, *added = lax.optimization_barrier((mask, share, *added))
    lanes = (size // 128 + 1) * 128
    hybrid = image_to_hybrid(main, added, permuted, note, lanes)
    received = lax.all_to_all(
        hybrid.reshape(devices, 2 * lines, lanes), AXES, 0, 0, tiled=True
    )
    first = between(hybrid)
    received, first = lax.optimization_barrier((received, first))
    back, loss, count = kspace_step(
        received, measured, target, mask, share, jnp.asarray(table_x, jnp.bfloat16),
        frames_here, 1.0 * slices * readout,
    )
    returned = lax.all_to_all(back, AXES, 0, 0, tiled=True)
    second = after(back, first)
    returned, second = lax.optimization_barrier((returned, second))
    shape = (slices, 2, frames_here, rows, twice // 2)
    grad, *grad_edge, sums = hybrid_to_grad(returned.reshape(twice, lanes), permuted, shape)
    return loss, count, grad, grad_edge, sums, second


def train_step(
    image_in, measured, target, sampled, window_half, table_y, table_x, w_in, w_out, w_back, bias_out
):
    slices, _, frames_here, rows, columns = image_in.shape
    frames, lines = measured.shape[1:3]
    cut = (slices + 1) // 2
    groups = [(0, cut), (cut, slices - cut)]
    edges = image_edges(image_in, (0, slices))
    main, *part = conv_forward(image_in, edges, w_in, w_out, bias_out)
    note = jnp.sum(1.0 - sampled).reshape(1, 1)
    added = return_edges(*part, columns)

    def again(group, after, kept=()):
        held, _ = lax.optimization_barrier((w_in.T, after))
        return hidden_again(image_in, edges, group, held, kept)

    fits = rows == 32 and lines == 8 and lax.axis_size("row") % 4 == 0
    fits = fits and frames * lines <= 256
    if fits:
        loss, count, grad, grad_edge, sums, kept = middle_fast(
            main, added, note, measured, target, sampled, window_half, table_y, table_x,
            functools.partial(again, groups[0]), functools.partial(again, groups[1]),
        )
    else:
        loss, count, grad, sums = middle_plain(
            main, added, measured, target, sampled, share_matrix(window_half, frames),
            table_y, table_x,
        )
        flat = (slices, 2, frames_here * columns)
        grad_edge = (
            grad[:, :, 0], grad[:, :, frames_here - 1],
            grad[:, :, :, 0].reshape(flat), grad[:, :, :, rows - 1].reshape(flat),
        )
        kept = None
    around = share_edges(*grad_edge)
    if kept is not None:
        return count, conv_backward(image_in, edges, grad, around, *kept, w_back, loss, sums)
    total = 0.0
    loss, sums = loss.reshape(1, 1), sums.reshape(2, 1)
    for first, size in groups:
        own, *sides = (one[first : first + size] for one in (image_in, *edges, grad, *around))
        held, _ = lax.optimization_barrier((w_in.T, total))
        kept = hidden_again(own, sides[:EDGES], (0, size), held)
        total += conv_backward(
            own, sides[:EDGES], sides[EDGES], sides[EDGES + 1 :], *kept, w_back, loss, sums
        )
        loss, sums = 0.0 * loss, 0.0 * sums
    return count, total


def on_device(
    image_in, measured, target, line_mask, window_half, in_kernel, out_kernel, biases,
    in_moment, out_moment, bias_moment, in_square, out_square, bias_square,
    in_smooth, out_smooth, bias_smooth,
):
    slices, _, frames_here, rows_here, columns = image_in.shape
    frames = measured.shape[1]
    width = in_kernel.shape[0]
    rows = rows_here * lax.axis_size("row")
    table_y = dft_table(columns)
    table_x = dft_table(rows)
    sampled = line_mask.astype(jnp.float32)
    w_in = conv_in_weights(in_kernel, biases[:width])
    w_out = conv_out_weights(out_kernel)
    w_back = conv_back_weights(out_kernel)

    count, total = train_step(
        image_in, measured, target, sampled, window_half, table_y, table_x,
        w_in, w_out, w_back, biases,
    )
    return update(
        last_parts(sum_over(total, "row"), "af"),
        count,
        (in_kernel, out_kernel, biases),
        (in_moment, out_moment, bias_moment),
        (in_square, out_square, bias_square),
        (in_smooth, out_smooth, bias_smooth),
    )


def solution(mesh):
    in_specs = (
        P(None, None, "af", "row", None),
        P(None, None, ("af", "row"), None),
        P(None, None, ("af", "row"), None),
        P(None, ("af", "row")),
    ) + (P(),) * 13
    return jax.shard_map(
        on_device, mesh=mesh, in_specs=in_specs, out_specs=(P(),) * 17, check_vma=False
    )
```

```python
import functools
import math

import jax
import jax.numpy as jnp
import numpy as np
from jax import lax
from jax.experimental import pallas as pl
from jax.experimental.pallas import tpu as pltpu
from jax.sharding import PartitionSpec as P

STEP = 5
AXES = ("af", "row")
BLOCK = 4
WIN = 8
SIDE = 16
DEPTH = 9 * SIDE
ONES_ROW = BLOCK + 2
PACKED = 128
EDGES = 6
BIAS_LANE = WIN - 1
VMEM = 60 * 2**20
GELU = math.sqrt(2.0 / math.pi)
CUBE = 0.044715

beta_first = 0.5
beta_second = 0.5
rate_in = 0.2
rate_out = 0.04
rate_bias = 0.3
decay_weight = 0.01
average_keep = 0.9
epsilon = 1e-08

NT = (((1,), (1,)), ((), ()))
TN = (((0,), (0,)), ((), ()))


def dft_table(length):
    index = np.arange(length)
    phase = (index[:, None] * index[None, :] % length) * (2.0 * math.pi / length)
    cosine = np.cos(phase) / math.sqrt(length)
    sine = np.sin(phase) / math.sqrt(length)
    upper = np.concatenate([cosine, -sine], axis=1)
    lower = np.concatenate([sine, cosine], axis=1)
    return np.concatenate([upper, lower], axis=0).astype(np.float32)


def share_matrix(window_half, frames):
    index = jnp.arange(frames, dtype=jnp.int32)
    inside = (jnp.abs(index[None, :] - index[:, None]) <= window_half[:, None]).astype(jnp.float32)
    return inside / jnp.sum(inside, axis=1, keepdims=True)


def adam_step(master, grad, first, second, rate):
    first_new = beta_first * first + (1.0 - beta_first) * grad
    second_new = beta_second * second + (1.0 - beta_second) * grad * grad
    first_hat = first_new / (1.0 - beta_first**STEP)
    second_hat = second_new / (1.0 - beta_second**STEP)
    master_new = master - rate * (
        first_hat / (jnp.sqrt(second_hat) + epsilon) + decay_weight * master
    )
    return (first_new, second_new, master_new)


def conv_in_weights(kernel, bias):
    width = kernel.shape[0]
    taps = kernel.astype(jnp.bfloat16).astype(jnp.float32).reshape(width, 2, 3, 3, 3)
    rows = []
    for j in range(BLOCK):
        row = jnp.pad(taps, ((0, 0), (0, 0), (0, 0), (j, WIN - 3 - j), (0, 0)))
        rows.append(row.transpose(0, 2, 4, 1, 3))
    spread = jnp.stack(rows)
    high = lax.reduce_precision(bias, 8, 7)
    rest = bias - high
    middle = lax.reduce_precision(rest, 8, 7)
    parts = jnp.stack([high, middle, rest - middle], axis=1)
    spread = spread.at[:, :, :, 0, 0, ONES_ROW].set(jnp.broadcast_to(parts, (BLOCK, width, 3)))
    return 0.5 * spread.reshape(BLOCK * width, DEPTH)


def conv_out_weights(kernel):
    width = kernel.shape[2]
    taps = kernel.astype(jnp.bfloat16).reshape(3, 3, 3, 2, width)[:, ::-1]
    columns = []
    for j in range(BLOCK):
        column = jnp.pad(taps, ((0, 0), (j, WIN - 3 - j), (0, 0), (0, 0), (0, 0)))
        columns.append(column.transpose(0, 2, 3, 1, 4))
    return jnp.stack(columns, axis=4).reshape(DEPTH, BLOCK * width)


def conv_back_weights(kernel):
    width = kernel.shape[2]
    taps = kernel.astype(jnp.bfloat16).reshape(3, 3, 3, 2, width)[::-1, ::-1, ::-1]
    rows = []
    for j in range(BLOCK):
        row = jnp.pad(taps, ((0, 0), (j, WIN - 3 - j), (0, 0), (0, 0), (0, 0)))
        rows.append(row.transpose(0, 2, 3, 1, 4))
    return 0.5 * jnp.stack(rows, axis=4).reshape(DEPTH, BLOCK * width)


def pick_table():
    table = np.zeros((2, 256, PACKED), np.float32)
    for a, b, e, c in np.ndindex(3, 3, 3, 2):
        lane = ((a * 3 + e) * 2 + c) * WIN + b
        table[0, lane, 27 * c + 9 * a + 3 * b + e] = 1.0
        tap = 9 * (2 - a) + 3 * (2 - b) + 2 - e
        table[1, lane, PACKED // 2 + 2 * tap + c] = 1.0
    table[0, BIAS_LANE, 54] = 1.0
    return jnp.asarray(table, jnp.bfloat16)


def load_volume(volume, own, below, above, left, right, corner_below, corner_above):
    _, channels, frames, rows, columns = own.shape
    lanes = (frames + 2) * columns
    for c in range(channels):
        volume[c, rows + 8 : rows + 16, :] = jnp.zeros((8, lanes), jnp.float32)
        for t in range(frames + 2):
            if t == 0:
                piece = below[0, c]
            elif t == frames + 1:
                piece = above[0, c]
            else:
                piece = own[0, c, t - 1]
            volume[c, 8 : 8 + rows, t * columns : (t + 1) * columns] = piece.astype(jnp.float32)
    low = corner_below[0].astype(jnp.float32)
    high = corner_above[0].astype(jnp.float32)
    for side, at, line in ((0, 7, left), (1, rows + 8, right)):
        middle = line[0].astype(jnp.float32)
        for c in range(channels):
            k = 2 * side + c
            volume[c, at : at + 1, 0:columns] = low[k : k + 1]
            volume[c, at : at + 1, columns : lanes - columns] = middle[c : c + 1]
            volume[c, at : at + 1, lanes - columns :] = high[k : k + 1]


def build_windows(volume, windows, columns, ones):
    blocks, _, lanes = windows.shape
    column = lax.broadcasted_iota(jnp.int32, (SIDE, columns), 1)
    row = lax.broadcasted_iota(jnp.int32, (SIDE, columns), 0)
    zero = jnp.zeros((SIDE, columns), jnp.bfloat16)
    for block in range(blocks):
        for t in range(lanes // columns):
            here = slice(t * columns, (t + 1) * columns)
            start = 7 + BLOCK * block
            window = jnp.concatenate(
                [volume[c, start : start + WIN, here] for c in range(2)], axis=0
            ).astype(jnp.bfloat16)
            for e in range(3):
                shifted = window
                if e != 1:
                    shifted = pltpu.roll(window, (1 - e) % columns, axis=1)
                    shifted = jnp.where(column == (0 if e == 0 else columns - 1), zero, shifted)
                if ones and e == 0:
                    shifted = jnp.where(row == ONES_ROW, zero + 1.0, shifted)
                windows[block, e * SIDE : (e + 1) * SIDE, here] = shifted


def forward_kernel(own, *refs):
    each = own.shape[0]
    edges, fixed, rest = refs[:EDGES], refs[EDGES : EDGES + 3], refs[EDGES + 3 :]
    slices = []
    for k in range(each):
        sides = of_step(edges, pl.program_id(0) * each + k)
        outs = of_step(rest[:5], k)
        slices.append(forward_slice(own.at[pl.ds(k, 1)], sides, *fixed, *outs, *(one.at[k] for one in rest[5:])))
    blocks = own.shape[3] // BLOCK
    slices[0][0]()
    for k, (_, step, finish) in enumerate(slices):
        for block in range(blocks):
            step(block)
            if block == blocks // 2 and k + 1 < each:
                slices[k + 1][0]()
            if block == 0 and k:
                slices[k - 1][2]()
    slices[-1][2]()


def forward_slice(
    own, edges, w_in, w_out, bias_out, main, part_below, part_above, part_left, part_right,
    volume, windows, total, hidden, mixed, spread,
):
    _, _, frames, rows, columns = own.shape
    blocks = windows.shape[0]

    def prepare():
        load_volume(volume, own, *edges)
        build_windows(volume, windows, columns, True)

    column = lax.broadcasted_iota(jnp.int32, (SIDE, columns), 1)

    def step(block):
        for f in range(frames):
            here = slice(f * columns, (f + 1) * columns)
            patch = jnp.concatenate(
                [windows[block, :, (f + a) * columns : (f + a + 1) * columns] for a in range(3)],
                axis=0,
            )
            half = jnp.dot(w_in[...], patch, preferred_element_type=jnp.float32)
            t = jnp.tanh(half * (2.0 * GELU + (8.0 * GELU * CUBE) * (half * half)))
            hidden[:, here] = (half + half * t).astype(jnp.bfloat16)
        for f in range(frames):
            here = slice(f * columns, (f + 1) * columns)
            mixed[f] = jnp.dot(w_out[...], hidden[:, here], preferred_element_type=jnp.float32)
        for t in range(frames + 2):
            window = None
            for e in range(3):
                summed = None
                for a in range(3):
                    f = t - 2 + a
                    if 0 <= f < frames:
                        start = (a * 3 + e) * SIDE
                        piece = mixed[f, start : start + SIDE, :]
                        summed = piece if summed is None else summed + piece
                if e != 1:
                    summed = pltpu.roll(summed, (1 - e) % columns, axis=1)
                    summed = jnp.where(column == (0 if e == 0 else columns - 1), 0.0, summed)
                window = summed if window is None else window + summed
            spread[block, :, t * columns : (t + 1) * columns] = window

    def finish():
        total[...] = jnp.zeros_like(total)
        for block in range(blocks):
            for o in range(2):
                start = 7 + BLOCK * block
                total[o, start : start + WIN, :] = (
                    total[o, start : start + WIN, :] + spread[block, o * WIN : (o + 1) * WIN, :]
                )
        for o in range(2):
            for t in range(frames + 2):
                here = total[o, 8 : 8 + rows, t * columns : (t + 1) * columns]
                if t == 0:
                    part_below[0, o] = here.astype(jnp.bfloat16)
                elif t == frames + 1:
                    part_above[0, o] = here.astype(jnp.bfloat16)
                else:
                    base = volume[o, 8 : 8 + rows, t * columns : (t + 1) * columns]
                    base = base + bias_out[bias_out.shape[0] - 2 + o]
                    main[0, t - 1, :, o * columns : (o + 1) * columns] = base + here
        for at, out in ((7, part_left), (8 + rows, part_right)):
            both = [total[o, at : at + 1, :] for o in range(2)]
            out[0] = jnp.concatenate(both, axis=0).astype(jnp.bfloat16)

    return prepare, step, finish


def patches(source, block, frames, columns):
    return jnp.concatenate(
        [source[block, :, a * columns : (a + frames) * columns] for a in range(3)], axis=0
    )


def hidden_kernel(start, own, *refs):
    edges, (w_in, *_, hidden, slopes, volume, windows) = refs[:EDGES], refs[EDGES:]
    _, _, frames, rows, columns = own.shape
    load_volume(volume, own, *of_step(edges, start + pl.program_id(0)))
    build_windows(volume, windows, columns, True)

    def step(block, carry):
        patch = patches(windows, block, frames, columns)
        for f in range(frames):
            here = slice(f * columns, (f + 1) * columns)
            half = lax.dot_general(
                patch[:, here], w_in[...], TN, preferred_element_type=jnp.float32
            )
            u = half * half
            t = jnp.tanh(half * (2.0 * GELU + (8.0 * GELU * CUBE) * u))
            up = 1.0 + t
            hidden[0, block, here, :] = (half * up).astype(jnp.bfloat16)
            slope = half * (2.0 * GELU + (24.0 * GELU * CUBE) * u)
            slopes[0, block, here, :] = (up + (up * (1.0 - t)) * slope).astype(jnp.bfloat16)
        return carry

    lax.fori_loop(0, windows.shape[0], step, 0, unroll=True)


def backward_kernel(
    own, *refs,
):
    edges, grad, grad_edges = refs[:EDGES], refs[EDGES], refs[EDGES + 1 : 2 * EDGES + 1]
    (
        hidden, slopes, w_back, pick, loss, sums, out,
        volume, windows, grad_windows, grads, sum_in, sum_out,
    ) = refs[2 * EDGES + 1 :]
    _, _, frames, rows, columns = own.shape

    part = pl.program_id(1)

    @pl.when((pl.program_id(0) == 0) & (part == 0))
    def _():
        sum_in[...] = jnp.zeros_like(sum_in)
        sum_out[...] = jnp.zeros_like(sum_out)

    @pl.when(part == 0)
    def _():
        load_volume(volume, own, *of_step(edges, pl.program_id(0)))
        build_windows(volume, windows, columns, True)
        load_volume(volume, grad, *of_step(grad_edges, pl.program_id(0)))
        build_windows(volume, grad_windows, columns, False)

    blocks = hidden.shape[1]

    def step(at):
        block = part * blocks + at
        patch = patches(windows, block, frames, columns)
        grad_patch = patches(grad_windows, block, frames, columns)
        for f in range(frames):
            here = slice(f * columns, (f + 1) * columns)
            gh = lax.dot_general(
                grad_patch[:, here], w_back[...], TN, preferred_element_type=jnp.float32
            )
            grads[here, :] = (slopes[0, at, here, :].astype(jnp.float32) * gh).astype(
                jnp.bfloat16
            )
        sum_in[:DEPTH, :] += jnp.dot(patch, grads[...], preferred_element_type=jnp.float32)
        sum_out[:DEPTH, :] += jnp.dot(
            grad_patch, hidden[0, at], preferred_element_type=jnp.float32
        )

    for at in range(blocks):
        step(at)

    @pl.when((pl.program_id(0) == pl.num_programs(0) - 1) & (part == pl.num_programs(1) - 1))
    def _():
        width = sum_in.shape[1] // BLOCK
        lanes = sum_in.shape[0]
        lane = lax.broadcasted_iota(jnp.int32, (width, lanes), 1)
        picked = jnp.zeros((width, pick.shape[2]), jnp.float32)
        for index, source in enumerate((sum_in[...].T, sum_out[...].T)):
            folded = source[0:width, :]
            bias = folded
            for j in range(1, BLOCK):
                piece = source[j * width : (j + 1) * width, :]
                folded = folded + pltpu.roll(piece, lanes - j, axis=1)
                bias = bias + piece
            if index == 0:
                moved = pltpu.roll(bias, BIAS_LANE - ONES_ROW, axis=1)
                folded = jnp.where(lane == BIAS_LANE, moved, folded)
            for _ in range(3):
                piece = folded.astype(jnp.bfloat16)
                folded = folded - piece.astype(jnp.float32)
                picked = picked + jnp.dot(piece, pick[index], preferred_element_type=jnp.float32)
        out[0:width, :] = picked
        spot = lax.broadcasted_iota(jnp.int32, (8, PACKED), 1)
        both = jnp.sum(sums[...], axis=1, keepdims=True)
        values = (jnp.sum(loss[...], axis=(0, 1), keepdims=True), both[0:1], both[1:2])
        row = jnp.zeros((8, PACKED), jnp.float32)
        for k, value in enumerate(values):
            row = jnp.where(spot == k, value, row)
        out[width:, :] = row


def of_step(refs, step):
    return [ref.at[pl.ds(step, 1)] for ref in refs]


def whole(shape):
    return pl.BlockSpec(tuple(shape), lambda s: (0,) * len(shape))


def a_slice(shape, first=0):
    rest = (0,) * (len(shape) - 1)
    return pl.BlockSpec((1,) + tuple(shape[1:]), lambda s: (s + first,) + rest)


def expected(microseconds):
    return pl.CostEstimate(
        flops=int(microseconds * 1.15e9), bytes_accessed=0, transcendentals=0
    )


def conv_scratch(frames, rows, columns):
    lanes = (frames + 2) * columns
    return (
        pltpu.VMEM((2, rows + 16, lanes), jnp.float32),
        pltpu.VMEM((rows // BLOCK, 3 * SIDE, lanes), jnp.bfloat16),
    )


def conv_forward(own, edges, w_in, w_out, bias_out):
    _, _, frames, rows, columns = own.shape
    slices = own.shape[0]
    each = 2 if slices % 2 == 0 else 1

    def some(shape):
        rest = (0,) * (len(shape) - 1)
        return pl.BlockSpec((each,) + tuple(shape[1:]), lambda s: (s,) + rest)

    lanes = (frames + 2) * columns
    span = w_in.shape[0]
    volume, windows = conv_scratch(frames, rows, columns)
    out_shape = [
        jax.ShapeDtypeStruct((slices, frames, rows, 2 * columns), jnp.float32),
        jax.ShapeDtypeStruct((slices, 2, rows, columns), jnp.bfloat16),
        jax.ShapeDtypeStruct((slices, 2, rows, columns), jnp.bfloat16),
        jax.ShapeDtypeStruct((slices, 2, lanes), jnp.bfloat16),
        jax.ShapeDtypeStruct((slices, 2, lanes), jnp.bfloat16),
    ]
    return pl.pallas_call(
        forward_kernel,
        grid=(slices // each,),
        in_specs=[some(own.shape)]
        + [pl.BlockSpec(memory_space=pltpu.VMEM)] * EDGES
        + [whole(w_in.shape), whole(w_out.shape), pl.BlockSpec(memory_space=pltpu.SMEM)],
        out_specs=[some(one.shape) for one in out_shape],
        out_shape=out_shape,
        scratch_shapes=[
            pltpu.VMEM((each,) + tuple(shape), kind)
            for shape, kind in (
                (volume.shape, jnp.float32),
                (windows.shape, jnp.bfloat16),
                (volume.shape, jnp.float32),
                ((span, frames * columns), jnp.bfloat16),
                ((frames, DEPTH, columns), jnp.float32),
                ((rows // BLOCK, SIDE, lanes), jnp.float32),
            )
        ],
        compiler_params=pltpu.CompilerParams(vmem_limit_bytes=VMEM),
        cost_estimate=expected(6 * slices),
        name="conv_forward",
    )(own, *map(in_vmem, edges), w_in, w_out, bias_out)


def hidden_again(own, edges, group, w_in, kept=()):
    _, _, frames, rows, columns = own.shape
    first, slices = group
    volume, windows = conv_scratch(frames, rows, columns)
    shape = (own.shape[0], rows // BLOCK, frames * columns, w_in.shape[1])
    return pl.pallas_call(
        functools.partial(hidden_kernel, first),
        grid=(slices,),
        in_specs=[a_slice(own.shape, first)]
        + [pl.BlockSpec(memory_space=pltpu.VMEM)] * EDGES
        + [whole(w_in.shape)]
        + [pl.BlockSpec(memory_space=pl.ANY)] * len(kept),
        out_specs=[a_slice(shape, first)] * 2,
        out_shape=[jax.ShapeDtypeStruct(shape, jnp.bfloat16)] * 2,
        input_output_aliases={2 + EDGES + k: k for k in range(len(kept))},
        scratch_shapes=[volume, windows],
        compiler_params=pltpu.CompilerParams(vmem_limit_bytes=VMEM),
        cost_estimate=expected(5 * slices),
        name="hidden_again",
    )(own, *map(in_vmem, edges), w_in, *kept)


def conv_backward(own, edges, grad, grad_edges, hidden, slopes, w_back, loss, sums):
    slices, _, frames, rows, columns = own.shape
    span = w_back.shape[1]
    volume, windows = conv_scratch(frames, rows, columns)
    total = pltpu.VMEM((2 * 128, span), jnp.float32)
    fixed = (w_back, pick_table(), loss, sums)
    out_shape = jax.ShapeDtypeStruct((span // BLOCK + 8, PACKED), jnp.float32)
    sides = [pl.BlockSpec(memory_space=pltpu.VMEM)] * EDGES
    here = (own, *map(in_vmem, edges), grad, *map(in_vmem, grad_edges))
    blocks = rows // BLOCK
    parts = 1

    def of_slice(shape):
        rest = (0,) * (len(shape) - 1)
        return pl.BlockSpec((1,) + tuple(shape[1:]), lambda s, part: (s,) + rest)

    def part_of_slice(shape):
        size = (1, blocks // parts) + tuple(shape[2:])
        return pl.BlockSpec(size, lambda s, part: (s, part, 0, 0))

    def all_of(shape):
        return pl.BlockSpec(tuple(shape), lambda s, part: (0,) * len(shape))

    return pl.pallas_call(
        backward_kernel,
        grid=(slices, parts),
        in_specs=[of_slice(own.shape), *sides, of_slice(grad.shape), *sides]
        + [part_of_slice(one.shape) for one in (hidden, slopes)]
        + [all_of(one.shape) for one in fixed],
        out_specs=all_of(out_shape.shape),
        out_shape=out_shape,
        scratch_shapes=[
            volume,
            windows,
            windows,
            pltpu.VMEM((frames * columns, span), jnp.bfloat16),
            total,
            total,
        ],
        compiler_params=pltpu.CompilerParams(vmem_limit_bytes=VMEM),
        cost_estimate=expected(5 * slices),
        name="conv_backward",
    )(*here, hidden, slopes, *fixed)


def last_parts(array, axis):
    if lax.axis_size(axis) != 4:
        return [sum_over(array, axis)]
    others = [
        lax.ppermute(array, axis, [(i, i ^ k) for i in range(4)]) for k in (1, 2, 3)
    ]
    return [array, *others]


def in_vmem(array):
    return pltpu.with_memory_space_constraint(array, pltpu.VMEM)


def along(axis, step):
    count = lax.axis_size(axis)
    return [(i, i + step) for i in range(count) if 0 <= i + step < count]


def sum_over(array, axis):
    size = lax.axis_size(axis)
    if size & (size - 1):
        return lax.psum(array, axis)

    def other(values, bits):
        return lax.ppermute(values, axis, [(i, i ^ bits) for i in range(size)])

    bit = 1
    if size.bit_length() % 2 == 0:
        array = array + other(array, bit)
        bit = 2
    while bit < size:
        one, two, three = (other(array, bit * k) for k in (1, 2, 3))
        array = (array + one) + (two + three)
        bit *= 4
    return array


def corners_along(left, right, columns):
    both = jnp.concatenate([left, right], axis=1)
    lanes = both.shape[2]
    below = lax.ppermute(both[:, :, lanes - columns :], "af", along("af", 1))
    above = lax.ppermute(both[:, :, :columns], "af", along("af", -1))
    return below, above


def share_edges(low, high, first, last):
    left = lax.ppermute(last, "row", along("row", 1))
    right = lax.ppermute(first, "row", along("row", -1))
    below = lax.ppermute(high, "af", along("af", 1))
    above = lax.ppermute(low, "af", along("af", -1))
    return below, above, left, right, *corners_along(left, right, low.shape[3])


def image_edges(image, group):
    start, slices = group
    part = image[start : start + slices]
    _, _, frames, rows, columns = part.shape
    flat = (slices, 2, frames * columns)
    return share_edges(
        part[:, :, 0], part[:, :, frames - 1],
        part[:, :, :, 0].reshape(flat), part[:, :, :, rows - 1].reshape(flat),
    )


def return_edges(part_below, part_above, part_left, part_right, columns):
    from_above = lax.ppermute(part_below, "af", along("af", -1))
    from_below = lax.ppermute(part_above, "af", along("af", 1))
    lower = lax.ppermute(part_left, "row", along("row", -1))
    upper = lax.ppermute(part_right, "row", along("row", 1))
    corner_below, corner_above = corners_along(upper, lower, columns)
    return from_below, from_above, upper, lower, corner_below, corner_above


def image_kernel(
    main, from_below, from_above, upper, lower, corner_below, corner_above,
    table, note, out, image,
):
    slices, frames, rows, twice = main.shape
    columns = twice // 2
    row = lax.broadcasted_iota(jnp.int32, (8, columns), 0)
    for s in range(slices):
        tops = upper[s].astype(jnp.float32)
        ends = lower[s].astype(jnp.float32)
        corners = {
            0: corner_below[s].astype(jnp.float32),
            frames - 1: corner_above[s].astype(jnp.float32),
        }
        for f in range(frames):
            at = slice((f + 1) * columns, (f + 2) * columns)
            for o in range(2):
                here = slice(o * columns, (o + 1) * columns)
                value = main[s, f, :, here]
                if f == 0:
                    value = value + from_below[s, o].astype(jnp.float32)
                if f == frames - 1:
                    value = value + from_above[s, o].astype(jnp.float32)
                top, end = tops[o : o + 1, at], ends[o : o + 1, at]
                if f in corners:
                    top = top + corners[f][o : o + 1]
                    end = end + corners[f][2 + o : 3 + o]
                parts = (
                    value[0:8] + jnp.where(row == 0, top, 0.0),
                    value[8 : rows - 8],
                    value[rows - 8 :] + jnp.where(row == 7, end, 0.0),
                )
                value = jnp.concatenate(parts, axis=0)
                start = (s * frames + f) * rows
                image[start : start + rows, here] = value.astype(jnp.bfloat16)
    size = slices * frames * rows
    for start in range(0, size, 512):
        stop = min(start + 512, size)
        out[:, start:stop] = lax.dot_general(
            table[...], image[start:stop, :], NT, preferred_element_type=jnp.float32
        ).astype(jnp.bfloat16)
    rest = out.shape[1] - size
    if rest:
        lane = lax.broadcasted_iota(jnp.int32, (out.shape[0], rest), 1)
        out[:, size:] = jnp.where(lane == 0, note[0, 0], 0.0).astype(jnp.bfloat16)


def image_to_hybrid(main, added, table, note, lanes):
    slices, frames, rows, twice = main.shape
    return pl.pallas_call(
        image_kernel,
        in_specs=[pl.BlockSpec(memory_space=pltpu.VMEM)] * (2 + EDGES)
        + [pl.BlockSpec(memory_space=pltpu.SMEM)],
        out_shape=jax.ShapeDtypeStruct((twice, lanes), jnp.bfloat16),
        scratch_shapes=[pltpu.VMEM((slices * frames * rows, twice), jnp.bfloat16)],
        compiler_params=pltpu.CompilerParams(vmem_limit_bytes=VMEM),
        cost_estimate=expected(slices / 2),
        name="image_to_hybrid",
    )(main, *map(in_vmem, added), table, note)


def grad_image_kernel(hybrid, table, out, low, high, first, last, sums):
    slices, _, frames, rows, columns = out.shape
    partial = [jnp.zeros((8, columns), jnp.float32)] * 2
    for s in range(slices):
        size = frames * rows
        start = s * size // 128 * 128
        stop = -(-(s + 1) * size // 128) * 128
        value = lax.dot_general(
            hybrid[:, start:stop], table[...], TN, preferred_element_type=jnp.float32
        ).astype(jnp.bfloat16)
        for c in range(2):
            tops, ends = [], []
            for f in range(frames):
                at = s * size + f * rows - start
                piece = value[at : at + rows, c * columns : (c + 1) * columns]
                out[s, c, f] = piece
                if f == 0:
                    low[s, c] = piece
                if f == frames - 1:
                    high[s, c] = piece
                wide = piece.astype(jnp.float32)
                for at in range(0, rows, 8):
                    partial[c] = partial[c] + wide[at : at + 8]
                tops.append(wide[0:1])
                ends.append(wide[rows - 1 :])
            first[s, c : c + 1, :] = jnp.concatenate(tops, axis=1)
            last[s, c : c + 1, :] = jnp.concatenate(ends, axis=1)
    for c in range(2):
        sums[c : c + 1, :] = jnp.sum(partial[c], axis=0, keepdims=True)


def hybrid_to_grad(hybrid, table, shape):
    slices, channels, frames, rows, columns = shape
    edge_frame = jax.ShapeDtypeStruct((slices, channels, rows, columns), jnp.bfloat16)
    edge_row = jax.ShapeDtypeStruct((slices, channels, frames * columns), jnp.float32)
    return pl.pallas_call(
        grad_image_kernel,
        out_shape=[
            jax.ShapeDtypeStruct(shape, jnp.bfloat16),
            edge_frame,
            edge_frame,
            edge_row,
            edge_row,
            jax.ShapeDtypeStruct((2, columns), jnp.float32),
        ],
        compiler_params=pltpu.CompilerParams(vmem_limit_bytes=VMEM),
        cost_estimate=expected(slices / 2),
        name="hybrid_to_grad",
    )(in_vmem(hybrid), table)


def chunk_table():
    index = np.arange(512).reshape(4, 4, 32)
    return jnp.asarray(np.eye(512)[index.transpose(1, 0, 2).reshape(-1)], jnp.bfloat16)


def beside(pieces):
    return jnp.concatenate(pieces, axis=1)


def weighed(weights, arrays):
    total = weights[0] * arrays[0]
    for weight, array in zip(weights[1:], arrays[1:]):
        total = total + weight * array
    return total


def kspace_slice(
    k, frames_here, n_af, kspace, measured, target, sampled, share, scale, grads, loss_lanes
):
    frames = n_af * frames_here
    near = [range(max(t - 2, 0), min(t + 3, frames)) for t in range(frames)]

    def rows_of(t):
        start = (k * frames + (t % frames_here) * n_af + t // frames_here) * 8
        return slice(start, start + 8)

    factor = scale[...]
    free = [1.0 - sampled[t] for t in range(frames)]
    kept = [sampled[t] * measured[k, t] for t in range(frames)]
    filled = [kept[t] + free[t] * kspace[rows_of(t)] for t in range(frames)]
    slopes = []
    terms = None
    for t in range(frames):
        shared = weighed([share[t, s] for s in near[t]], [filled[s] for s in near[t]])
        differ = kept[t] + free[t] * shared - target[k, t]
        square = differ * differ + 1.0
        inverse = lax.rsqrt(square)
        term = free[t] * (square * inverse - 1.0)
        terms = term if terms is None else terms + term
        slopes.append(free[t] * differ * inverse * factor)
    loss_lanes[...] += terms
    for s in range(frames):
        grad = weighed([share[t, s] for t in near[s]], [slopes[t] for t in near[s]])
        grads[rows_of(s), :] = free[s] * grad


def kspace_kernel(
    frames_here, factor, received, measured, target, sampled, share, table, chunks,
    out, loss, count, spectrum, grads, loss_lanes, scale,
):
    groups, _, lanes = received.shape
    pairs, n_af, _, twice = spectrum.shape
    rows = twice // 2
    n_row = groups // n_af
    step = pl.program_id(0)
    tiles = lanes // 128
    size = out.shape[1]

    @pl.when(step == 0)
    def _():
        loss_lanes[...] = jnp.zeros_like(loss_lanes)
        last = slice((tiles - 1) * 128, lanes)
        notes = sum(received[group, 0:size, last].astype(jnp.float32) for group in range(groups))
        at = pairs * (128 // 4) - (tiles - 1) * 128
        total = notes[0:1, at : at + 1] * factor
        count[...] = jnp.broadcast_to(total, count.shape)
        scale[...] = jnp.broadcast_to(1.0 / total, scale.shape)
        for h in range(n_row // 4):
            for af in range(n_af):
                source = [
                    beside(
                        [
                            received[af * n_row + h * 4 + m, :, tile * 128 : (tile + 1) * 128]
                            for m in range(4)
                        ]
                    )
                    for tile in range(tiles)
                ]
                moved = jnp.dot(
                    jnp.concatenate(source, axis=0),
                    chunks[...],
                    preferred_element_type=jnp.float32,
                )
                for pair in range(pairs):
                    tile, k = pair // 4, pair % 4
                    for c in range(2):
                        at = c * rows + h * 128
                        start = tile * size + c * 8
                        spectrum[pair, af, :, at : at + 128] = moved[
                            start : start + 8, k * 128 : (k + 1) * 128
                        ]

    each = measured.shape[0]
    here = pl.ds(step * each * frames_here, each * frames_here)
    block = spectrum[here].reshape(grads.shape).astype(jnp.bfloat16)
    kspace = jnp.dot(block, table[...], preferred_element_type=jnp.float32)
    for k in range(each):
        kspace_slice(
            k, frames_here, n_af, kspace, measured, target, sampled, share, scale, grads, loss_lanes
        )
    back = lax.dot_general(
        grads[...].astype(jnp.bfloat16), table[...], NT, preferred_element_type=jnp.float32
    )
    spectrum[here] = back.reshape(each * frames_here, n_af, 8, twice)

    @pl.when(step == pl.num_programs(0) - 1)
    def _():
        loss[...] = loss_lanes[...]

        for h in range(n_row // 4):
            for af in range(n_af):
                source = []
                for tile in range(tiles):
                    four = []
                    for k in range(4):
                        pair = min(tile * 4 + k, pairs - 1)
                        both = [
                            spectrum[pair, af, :, c * rows + h * 128 : c * rows + h * 128 + 128]
                            for c in range(2)
                        ]
                        four.append(jnp.concatenate(both, axis=0).astype(jnp.bfloat16))
                    source.append(beside(four))
                moved = jnp.dot(
                    jnp.concatenate(source, axis=0),
                    chunks[...],
                    preferred_element_type=jnp.float32,
                ).astype(jnp.bfloat16)
                for m in range(4):
                    for tile in range(tiles):
                        out[af * n_row + h * 4 + m, :, tile * 128 : (tile + 1) * 128] = moved[
                            tile * size : (tile + 1) * size, m * 128 : (m + 1) * 128
                        ]


def kspace_step(received, measured, target, sampled, share, table, frames_here, factor):
    _, frames, lines, twice = measured.shape
    slices = measured.shape[0]
    n_af = frames // frames_here
    each = next(n for n in (5, 2, 1) if slices % n == 0)
    chunks = chunk_table()

    def some(shape):
        return pl.BlockSpec((each,) + tuple(shape[1:]), lambda s: (s, 0, 0, 0))

    return pl.pallas_call(
        functools.partial(kspace_kernel, frames_here, factor),
        grid=(slices // each,),
        in_specs=[
            pl.BlockSpec(memory_space=pltpu.VMEM),
            some(measured.shape),
            some(target.shape),
            whole(sampled.shape),
            pl.BlockSpec(memory_space=pltpu.SMEM),
            whole(table.shape),
            whole(chunks.shape),
        ],
        out_specs=[whole(received.shape), whole((lines, twice)), whole((8, 128))],
        out_shape=[
            jax.ShapeDtypeStruct(received.shape, jnp.bfloat16),
            jax.ShapeDtypeStruct((lines, twice), jnp.float32),
            jax.ShapeDtypeStruct((8, 128), jnp.float32),
        ],
        scratch_shapes=[
            pltpu.VMEM((slices * frames_here, n_af, lines, twice), jnp.float32),
            pltpu.VMEM((each * frames * lines, twice), jnp.float32),
            pltpu.VMEM((lines, twice), jnp.float32),
            pltpu.VMEM((lines, twice), jnp.float32),
        ],
        compiler_params=pltpu.CompilerParams(vmem_limit_bytes=VMEM),
        cost_estimate=expected(3 * slices),
        name="kspace",
    )(in_vmem(received), measured, target, sampled, share, table, chunks)


def middle_plain(main, added, measured, target, sampled, share, table_y, table_x):
    highest = lax.Precision.HIGHEST
    slices, frames_here, rows_here, twice = main.shape
    count = lax.psum(jnp.sum(1.0 - sampled) * (2.0 * slices * measured.shape[3] / 2), AXES)
    columns = twice // 2
    frames, lines = measured.shape[1:3]
    rows = measured.shape[3] // 2
    table_y = jnp.asarray(table_y, jnp.bfloat16)
    table_x = jnp.asarray(table_x, jnp.bfloat16)
    image = main.reshape(slices, frames_here, rows_here, 2, columns)
    below, above, upper, lower, *corners = (one.astype(jnp.float32) for one in added)
    image = image.at[:, 0].add(below.transpose(0, 2, 1, 3))
    image = image.at[:, frames_here - 1].add(above.transpose(0, 2, 1, 3))
    for at, line in ((0, upper), (rows_here - 1, lower)):
        line = line[:, :, columns:-columns].reshape(slices, 2, frames_here, columns)
        image = image.at[:, :, at].add(line.transpose(0, 2, 1, 3))
    for f, corner in ((0, corners[0]), (frames_here - 1, corners[1])):
        image = image.at[:, f, 0].add(corner[:, 0:2])
        image = image.at[:, f, rows_here - 1].add(corner[:, 2:4])
    flat = image.reshape(slices, frames_here, rows_here, twice).astype(jnp.bfloat16)
    hybrid = jnp.dot(flat, table_y, preferred_element_type=jnp.float32).astype(jnp.bfloat16)
    hybrid = hybrid.reshape(slices, frames_here, rows_here, 2, columns)
    part = lax.all_to_all(hybrid, "af", split_axis=4, concat_axis=1, tiled=True)
    spread = lax.all_to_all(part, "row", split_axis=4, concat_axis=2, tiled=True)
    spectrum = jnp.transpose(spread, (0, 1, 4, 3, 2)).reshape(slices, frames, lines, 2 * rows)
    kspace = jnp.dot(spectrum, table_x, preferred_element_type=jnp.float32)
    mask = sampled[None, :, :, None]
    filled = mask * measured + (1.0 - mask) * kspace
    shared = jnp.einsum("ts,bslk->btlk", share, filled, precision=highest)
    differ = mask * measured + (1.0 - mask) * shared - target
    root = jnp.sqrt(differ * differ + 1.0)
    loss = jnp.sum((1.0 - mask) * (root - 1.0))
    slope = (1.0 - mask) * differ / root / count
    grad = (1.0 - mask) * jnp.einsum("ts,btlk->bslk", share, slope, precision=highest)
    back = jnp.dot(grad, table_x.T.astype(jnp.float32), precision=highest).astype(jnp.bfloat16)
    back = jnp.transpose(back.reshape(slices, frames, lines, 2, rows), (0, 1, 4, 3, 2))
    part = lax.all_to_all(back, "row", split_axis=2, concat_axis=4, tiled=True)
    whole_rows = lax.all_to_all(part, "af", split_axis=1, concat_axis=4, tiled=True)
    grad = jnp.dot(
        whole_rows.reshape(slices, frames_here, rows_here, twice),
        table_y.T,
        preferred_element_type=jnp.float32,
    ).reshape(slices, frames_here, rows_here, 2, columns)
    grad = jnp.transpose(grad, (0, 3, 1, 2, 4)).astype(jnp.bfloat16)
    return loss, jnp.broadcast_to(count, (8, 128)), grad, jnp.sum(grad.astype(jnp.float32), axis=(0, 2, 3, 4))


def update_kernel(parts, *refs):
    count, *ins = refs[parts : parts + 13]
    outs = refs[parts + 13 :]
    total = refs[0][...]
    if parts == 4:
        total = (total + refs[1][...]) + (refs[2][...] + refs[3][...])
    *outs, loss, unsampled = outs
    taps, width = ins[0].shape
    turned = total[0:width, :].T

    def step(kind, at, grad):
        master, first, second, smooth = (one[at] for one in ins[kind::3])
        rate = (rate_in, rate_out, rate_bias)[kind]
        first, second, master = adam_step(master, grad, first, second, rate)
        average = average_keep * smooth + (1.0 - average_keep) * master
        for out, value in zip(outs[kind::3], (first, second, master, average, master)):
            out[at] = value.astype(out.dtype)

    step(0, ..., turned[0:taps, :])
    for tap in range(ins[1].shape[0]):
        start = PACKED // 2 + 2 * tap
        step(1, tap, turned[start : start + 2, :])
    step(2, (slice(0, 1), slice(0, width)), turned[54:55, :])
    step(2, (slice(0, 1), slice(width, width + 2)), total[width : width + 1, 1:3])
    loss[...] = total[width : width + 1, 0:1]
    unsampled[...] = count[0:1, 0:1]


def update(parts, count, weights, firsts, seconds, smooths):
    arrays = [*weights, *firsts, *seconds, *smooths]
    turn = {1: lambda one: one.reshape(1, -1), 2: jnp.transpose, 3: lambda one: one}
    arrays = [turn[one.ndim](one) for one in arrays]
    kinds = [jnp.float32] * 4 + [jnp.bfloat16]
    *outs, loss, unsampled = pl.pallas_call(
        functools.partial(update_kernel, len(parts)),
        out_shape=[jax.ShapeDtypeStruct(one.shape, kind) for kind in kinds for one in arrays[:3]]
        + [jax.ShapeDtypeStruct((1, 1), jnp.float32)] * 2,
        name="update",
    )(*map(in_vmem, parts), count, *arrays)
    back = (jnp.transpose, lambda one: one, lambda one: one.reshape(-1))
    return loss[0, 0], unsampled[0, 0], *[back[k % 3](one) for k, one in enumerate(outs)]


def middle_fast(
    main, added, note, measured, target, sampled, window_half, table_y, table_x, between, after
):
    devices = lax.axis_size("af") * lax.axis_size("row")
    slices, frames_here, rows, twice = main.shape
    lines, readout = measured.shape[2:]
    size = slices * frames_here * rows
    order = np.arange(twice).reshape(2, devices, lines).transpose(1, 0, 2).reshape(-1)
    permuted = jnp.asarray(np.ascontiguousarray(table_y[:, order].T), jnp.bfloat16)
    mask = jnp.broadcast_to(sampled[:, :, None], sampled.shape + (readout,))
    share = share_matrix(window_half, measured.shape[1])
    mask, share, *added = lax.optimization_barrier((mask, share, *added))
    lanes = (size // 128 + 1) * 128
    hybrid = image_to_hybrid(main, added, permuted, note, lanes)
    received = lax.all_to_all(
        hybrid.reshape(devices, 2 * lines, lanes), AXES, 0, 0, tiled=True
    )
    first = between(hybrid)
    received, first = lax.optimization_barrier((received, first))
    back, loss, count = kspace_step(
        received, measured, target, mask, share, jnp.asarray(table_x, jnp.bfloat16),
        frames_here, 1.0 * slices * readout,
    )
    returned = lax.all_to_all(back, AXES, 0, 0, tiled=True)
    second = after(back, first)
    returned, second = lax.optimization_barrier((returned, second))
    shape = (slices, 2, frames_here, rows, twice // 2)
    grad, *grad_edge, sums = hybrid_to_grad(returned.reshape(twice, lanes), permuted, shape)
    return loss, count, grad, grad_edge, sums, second


def train_step(
    image_in, measured, target, sampled, window_half, table_y, table_x, w_in, w_out, w_back, bias_out
):
    slices, _, frames_here, rows, columns = image_in.shape
    frames, lines = measured.shape[1:3]
    cut = (slices + 1) // 2
    groups = [(0, cut), (cut, slices - cut)]
    edges = image_edges(image_in, (0, slices))
    main, *part = conv_forward(image_in, edges, w_in, w_out, bias_out)
    note = jnp.sum(1.0 - sampled).reshape(1, 1)
    added = return_edges(*part, columns)

    def again(group, after, kept=()):
        held, _ = lax.optimization_barrier((w_in.T, after))
        return hidden_again(image_in, edges, group, held, kept)

    fits = rows == 32 and lines == 8 and lax.axis_size("row") % 4 == 0
    fits = fits and frames * lines <= 256
    if fits:
        loss, count, grad, grad_edge, sums, kept = middle_fast(
            main, added, note, measured, target, sampled, window_half, table_y, table_x,
            functools.partial(again, groups[0]), functools.partial(again, groups[1]),
        )
    else:
        loss, count, grad, sums = middle_plain(
            main, added, measured, target, sampled, share_matrix(window_half, frames),
            table_y, table_x,
        )
        flat = (slices, 2, frames_here * columns)
        grad_edge = (
            grad[:, :, 0], grad[:, :, frames_here - 1],
            grad[:, :, :, 0].reshape(flat), grad[:, :, :, rows - 1].reshape(flat),
        )
        kept = None
    around = share_edges(*grad_edge)
    if kept is not None:
        return count, conv_backward(image_in, edges, grad, around, *kept, w_back, loss, sums)
    total = 0.0
    loss, sums = loss.reshape(1, 1), sums.reshape(2, 1)
    for first, size in groups:
        own, *sides = (one[first : first + size] for one in (image_in, *edges, grad, *around))
        held, _ = lax.optimization_barrier((w_in.T, total))
        kept = hidden_again(own, sides[:EDGES], (0, size), held)
        total += conv_backward(
            own, sides[:EDGES], sides[EDGES], sides[EDGES + 1 :], *kept, w_back, loss, sums
        )
        loss, sums = 0.0 * loss, 0.0 * sums
    return count, total


def on_device(
    image_in, measured, target, line_mask, window_half, in_kernel, out_kernel, biases,
    in_moment, out_moment, bias_moment, in_square, out_square, bias_square,
    in_smooth, out_smooth, bias_smooth,
):
    slices, _, frames_here, rows_here, columns = image_in.shape
    frames = measured.shape[1]
    width = in_kernel.shape[0]
    rows = rows_here * lax.axis_size("row")
    table_y = dft_table(columns)
    table_x = dft_table(rows)
    sampled = line_mask.astype(jnp.float32)
    w_in = conv_in_weights(in_kernel, biases[:width])
    w_out = conv_out_weights(out_kernel)
    w_back = conv_back_weights(out_kernel)

    count, total = train_step(
        image_in, measured, target, sampled, window_half, table_y, table_x,
        w_in, w_out, w_back, biases,
    )
    return update(
        last_parts(sum_over(total, "row"), "af"),
        count,
        (in_kernel, out_kernel, biases),
        (in_moment, out_moment, bias_moment),
        (in_square, out_square, bias_square),
        (in_smooth, out_smooth, bias_smooth),
    )


def solution(mesh):
    in_specs = (
        P(None, None, "af", "row", None),
        P(None, None, ("af", "row"), None),
        P(None, None, ("af", "row"), None),
        P(None, ("af", "row")),
    ) + (P(),) * 13
    return jax.shard_map(
        on_device, mesh=mesh, in_specs=in_specs, out_specs=(P(),) * 17, check_vma=False
    )
```
